32 devices in a mesh: batch: 8 (over z, x), seq: 4 (over y, core).
Axes of the slice: x: 2, y: 2, z: 4, core: 2. Of those that a mesh axis runs over, the one named last changes fastest.
Arguments:
- stream_in: bfloat16 [8, 1024, 2048], P('batch', 'seq'), may hold values from -6 to 6
- segment_ids: int32 [8, 1024], P('batch', 'seq'), may hold values from 0 to 3, never falling along the last dimension, each value on 1 to 768 neighbouring positions
- out_grad: bfloat16 [8, 1024, 2048], P('batch', 'seq'), may hold values from -6 to 6
- branch_weight: bfloat16 [2048, 2730], P(('batch', 'seq')), may hold values from -0.125 to 0.125
- gating_weight: bfloat16 [2048, 2730], P(('batch', 'seq')), may hold values from -0.125 to 0.125
- output_weight: bfloat16 [2048, 2730], P(('batch', 'seq')), may hold values from -0.21875 to 0.21875
- hidden_gate: bfloat16 [2048, 6144], P(('batch', 'seq')), may hold values from -0.125 to 0.125
- hidden_linear: bfloat16 [2048, 6144], P(('batch', 'seq')), may hold values from -0.125 to 0.125
- hidden_output: bfloat16 [2048, 6144], P(('batch', 'seq')), may hold values from -0.15625 to 0.15625
- mixer_gain: bfloat16 [2048], P(('batch', 'seq')), may hold values from 0.5 to 1.5
- hidden_gain: bfloat16 [2048], P(('batch', 'seq')), may hold values from 0.5 to 1.5
- gate_blocks: bfloat16 [2, 16, 171, 171], replicated, may hold values from -0.4375 to 0.4375
- gate_biases: float32 [2, 2730], replicated, may hold values from -3 to 3
- conv_taps: float32 [4, 2730], replicated, may hold values from -3 to 3
- conv_bias: float32 [2730], replicated, may hold values from -3 to 3
- decay_param: float32 [2730], replicated, may hold values from 3 to 10, as said below
Outputs:
- stream_out: bfloat16 [8, 1024, 2048], P('batch', 'seq')
- stream_grad: bfloat16 [8, 1024, 2048], P('batch', 'seq')
- branch_grad: float32 [2048, 2730], P(('batch', 'seq'))
- gating_grad: float32 [2048, 2730], P(('batch', 'seq'))
- output_grad: float32 [2048, 2730], P(('batch', 'seq'))
- hidden_gate_grad: float32 [2048, 6144], P(('batch', 'seq'))
- hidden_linear_grad: float32 [2048, 6144], P(('batch', 'seq'))
- hidden_output_grad: float32 [2048, 6144], P(('batch', 'seq'))
- mixer_gain_grad: float32 [2048], P(('batch', 'seq'))
- hidden_gain_grad: float32 [2048], P(('batch', 'seq'))
- gate_blocks_grad: float32 [2, 16, 171, 171], replicated
- gate_biases_grad: float32 [2, 2730], replicated
- conv_taps_grad: float32 [4, 2730], replicated
- conv_bias_grad: float32 [2730], replicated
- decay_grad: float32 [2730], replicated
The draws below stay inside these ranges and needn't reach their ends.
Inputs may be any that keep to these rules, and one draw needn't show every extreme that they name: `segment_ids`: within a row the numbers never fall; each document has at most three quarters of 1024 tokens and one has exactly that many. softplus(-decay_param) lies between 1e-4 and 0.03.
All inputs are finite; a program needn't handle non-finite values.
Results may differ from the reference program's by a relative error of at most 0.01.
Values may be sent and summed in bfloat16 or wider, within the bound.
No kernel may reach another device: no remote copies, remote signals or barrier semaphores. Data moves between devices by JAX's collectives and lax.ppermute only.
A program may use at most 512 MiB of HBM per device.

```python
import math
import jax
import jax.numpy as jnp
import numpy as np
from jax import lax

D = 2048
F = 6144
NBLK = 16
BLK = 171
NBIG = 10
KW = 4
SEGS = 4
R = 2730
L = 1024
ROWS = 8


def draw_decay_param(key, part):
    log_rate = jax.random.uniform(key, (R,), jnp.float32, jnp.log(0.0002), jnp.log(0.03))
    rate = jnp.exp(log_rate)
    return -rate - jnp.log(-jnp.expm1(-rate))


def level_of(own_key, shape, cuts, low, largest):
    loudness = 1.0
    for axis_at, parts in cuts:
        heights = jax.random.uniform(jax.random.fold_in(jax.random.fold_in(own_key, 6), axis_at), (parts,), jnp.float32, low / len(cuts), largest / len(cuts))
        loudness = loudness * jnp.repeat(jnp.exp(heights), shape[axis_at] // parts).reshape((-1,) + (1,) * (len(shape) - 1 - axis_at))
    return loudness


def split_up(number_of, total, limit, slope):
    weights = [(1 << 20) // math.isqrt(grade ** slope) + 1 for grade in range(2, number_of + 1)]
    surplus, given = total - limit - (number_of - 1), [1] * (number_of - 1)
    while surplus > 0:
        candidates = [i for i in range(number_of - 1) if given[i] < limit]
        pool, remaining = sum([weights[i] for i in candidates]), surplus
        for i in candidates:
            addition = min(limit - given[i], max(1, remaining * weights[i] // pool), surplus)
            given[i] = given[i] + addition
            surplus = surplus - addition
    return np.array([limit] + given)


def uneven_parts(key, amount, total, limit, skew):
    if amount == 2:
        one = jax.random.randint(key, (), max(1, total - limit), min(limit, total - 1) + 1)
        return jnp.stack([one, total - one])
    sizes = jnp.asarray(split_up(amount, total, limit, skew), jnp.int32)
    twos = (amount - 1) // 2
    donor, taker = sizes[1:1 + 2 * twos:2], sizes[2:2 + 2 * twos:2]
    margin = jnp.minimum(donor - 1, limit - taker)
    passed = jax.random.randint(jax.random.fold_in(key, 1), (twos,), 0, 1 << 20) % (margin + 1)
    sizes = sizes.at[1:1 + 2 * twos:2].set(donor - passed).at[2:2 + 2 * twos:2].set(taker + passed)
    return sizes[jax.random.permutation(jax.random.fold_in(key, 2), amount)]


def normal_values(stream_key, dims, deviation, reach, pieces=(), held_as=jnp.bfloat16):
    factor_of = level_of(stream_key, dims, pieces, -0.22, 0.18) if pieces else 1.0
    drawn = jax.random.normal(stream_key, dims, jnp.float32) * deviation * factor_of
    return jnp.minimum(jnp.maximum(drawn, -reach), reach).astype(held_as)


def setup_inputs(seed: int = 0) -> dict:
    keys = jax.random.split(jax.random.key(seed), 17)
    return {
        "stream_in": normal_values(keys[0], (ROWS, L, D), 1.0, 6.0, ((0, 8), (1, 4))),
        "segment_ids": jax.vmap(lambda own: jnp.searchsorted(jnp.cumsum(uneven_parts(own, SEGS, L, 3 * L // 4, 2)), jnp.arange(L), side="right"))(jax.random.split(keys[1], ROWS)).reshape((ROWS, L)).astype(jnp.int32),
        "out_grad": normal_values(keys[2], (ROWS, L, D), 1.0, 6.0, ((0, 8), (1, 4))),
        "branch_weight": normal_values(keys[3], (D, R), D ** -0.5, 0.125, ((0, 32),)),
        "gating_weight": normal_values(keys[4], (D, R), D ** -0.5, 0.125, ((0, 32),)),
        "output_weight": normal_values(keys[5], (D, R), (R // 4) ** -0.5, 0.21875, ((0, 32),)),
        "hidden_gate": normal_values(keys[6], (D, F), D ** -0.5, 0.125, ((0, 32),)),
        "hidden_linear": normal_values(keys[7], (D, F), D ** -0.5, 0.125, ((0, 32),)),
        "hidden_output": normal_values(keys[8], (D, F), (F // 4) ** -0.5, 0.15625, ((0, 32),)),
        "mixer_gain": jnp.clip(1.0 + 0.1 * jax.random.normal(keys[9], (D,), jnp.float32), 0.5, 1.5).astype(jnp.bfloat16),
        "hidden_gain": jnp.clip(1.0 + 0.1 * jax.random.normal(keys[10], (D,), jnp.float32), 0.5, 1.5).astype(jnp.bfloat16),
        "gate_blocks": normal_values(keys[11], (2, NBLK, BLK, BLK), BLK ** -0.5, 0.4375),
        "gate_biases": normal_values(keys[12], (2, R), 0.5, 3.0, (), jnp.float32),
        "conv_taps": normal_values(keys[13], (KW, R), 0.5, 3.0, (), jnp.float32),
        "conv_bias": normal_values(keys[14], (R,), 0.5, 3.0, (), jnp.float32),
        "decay_param": draw_decay_param(jax.random.fold_in(keys[16], 71), 0),
    }


EPSILON = 1e-06
HIGHEST = lax.Precision.HIGHEST

@jax.custom_vjp
def low(v):
    return lax.optimization_barrier(v.astype(jnp.bfloat16)).astype(jnp.float32)

@jax.custom_vjp
def low_back(v):
    return v

def low_keep(v):
    return (low(v), None)

def low_pass(kept, grad):
    return (grad,)

def back_keep(v):
    return (v, None)

def back_low(kept, grad):
    return (low(grad),)
low.defvjp(low_keep, low_pass)
low_back.defvjp(back_keep, back_low)

def to_blocks(values):
    leading = values.shape[:-1]
    larger = values[..., :NBIG * BLK].reshape(leading + (NBIG, BLK))
    smaller = values[..., NBIG * BLK:].reshape(leading + (NBLK - NBIG, BLK - 1))
    smaller = jnp.pad(smaller, [(0, 0)] * len(leading) + [(0, 0), (0, 1)])
    return jnp.concatenate([larger, smaller], axis=-2)

def from_blocks(values):
    leading = values.shape[:-2]
    larger = values[..., :NBIG, :].reshape(leading + (NBIG * BLK,))
    smaller = values[..., NBIG:, :BLK - 1].reshape(leading + ((NBLK - NBIG) * (BLK - 1),))
    return jnp.concatenate([larger, smaller], axis=-1)

def rms_scale(values):
    return lax.rsqrt(lax.optimization_barrier(jnp.mean(values * values, axis=-1, keepdims=True)) + EPSILON)

def affine_join(earlier, later):
    return (earlier[0] * later[0], later[0] * earlier[1] + later[1])

def gate_math(recur_pre, input_pre, decay_param, conv_sum, starts):
    recur_gate = jax.nn.sigmoid(recur_pre)
    input_gate = jax.nn.sigmoid(input_pre)
    log_decay = -8.0 * recur_gate * jax.nn.softplus(-decay_param)
    decay = jnp.exp(log_decay)
    carry_mult = jnp.where(starts, 0.0, decay)
    scale_in = jnp.where(starts, 1.0, jnp.sqrt(-jnp.expm1(2.0 * log_decay)))
    return (carry_mult, scale_in * input_gate * conv_sum)

def forward_rows(params, inputs, segment):
    branch_weight, gating_weight, output_weight, hidden_gate, hidden_linear, hidden_output, mixer_gain, hidden_gain, gate_blocks, gate_biases, conv_taps, conv_bias, decay_param = params
    length = inputs.shape[1]
    normed = low(inputs * rms_scale(inputs) * mixer_gain)
    branch = low_back(jnp.einsum('gtd,dr->gtr', normed, branch_weight, precision=HIGHEST))
    gating = low_back(jnp.einsum('gtd,dr->gtr', normed, gating_weight, precision=HIGHEST))
    padded = jnp.pad(branch, ((0, 0), (KW - 1, 0), (0, 0)))
    seg_padded = jnp.pad(segment, ((0, 0), (KW - 1, 0)), constant_values=-1)
    conv_sum = conv_bias + jnp.zeros_like(branch)
    for offset in range(KW):
        begin = KW - 1 - offset
        same = (seg_padded[:, begin:begin + length] == segment).astype(jnp.float32)
        conv_sum = conv_sum + conv_taps[offset] * padded[:, begin:begin + length] * same[..., None]
    conv_low = low(conv_sum)
    conv_blocks = to_blocks(conv_low)
    recur_pre = low_back(from_blocks(jnp.einsum('gtki,kij->gtkj', conv_blocks, gate_blocks[0], precision=HIGHEST))) + gate_biases[0]
    input_pre = low_back(from_blocks(jnp.einsum('gtki,kij->gtkj', conv_blocks, gate_blocks[1], precision=HIGHEST))) + gate_biases[1]
    starts = jnp.concatenate([segment[:, :1] >= 0, segment[:, 1:] != segment[:, :-1]], axis=1)[..., None]
    carry_mult, drive = gate_math(recur_pre, input_pre, decay_param, conv_sum, starts)
    ignored, state = lax.associative_scan(affine_join, (carry_mult, drive), axis=1)
    mixed = low(state * jax.nn.gelu(gating))
    mixer_out = low_back(jnp.einsum('gtr,dr->gtd', mixed, output_weight, precision=HIGHEST))
    middle = inputs + mixer_out
    normed_mid = low(middle * rms_scale(middle) * hidden_gain)
    gate_pre = low_back(jnp.einsum('gtd,df->gtf', normed_mid, hidden_gate, precision=HIGHEST))
    linear_pre = low_back(jnp.einsum('gtd,df->gtf', normed_mid, hidden_linear, precision=HIGHEST))
    hidden = low(jax.nn.gelu(gate_pre) * linear_pre)
    hidden_out = low_back(jnp.einsum('gtf,df->gtd', hidden, hidden_output, precision=HIGHEST))
    return middle + hidden_out

def reference(stream_in, segment_ids, out_grad, branch_weight, gating_weight, output_weight, hidden_gate, hidden_linear, hidden_output, mixer_gain, hidden_gain, gate_blocks, gate_biases, conv_taps, conv_bias, decay_param):
    params = tuple((weight.astype(jnp.float32) for weight in (branch_weight, gating_weight, output_weight, hidden_gate, hidden_linear, hidden_output, mixer_gain, hidden_gain, gate_blocks, gate_biases, conv_taps, conv_bias, decay_param)))
    inputs = stream_in.astype(jnp.float32)
    groups = ROWS // 4
    seg_groups = segment_ids.reshape(groups, 4, L)
    stepper = jax.checkpoint(forward_rows)

    def whole(params, inputs):

        def one_group(packed):
            return stepper(params, packed[0], packed[1])
        stacked = lax.map(one_group, (inputs.reshape(groups, 4, L, D), seg_groups))
        return stacked.reshape(ROWS, L, D)
    result, pullback = jax.vjp(whole, params, inputs)
    param_grads, input_grad = pullback(out_grad.astype(jnp.float32))
    return (result.astype(jnp.bfloat16), input_grad.astype(jnp.bfloat16), param_grads[0], param_grads[1], param_grads[2], param_grads[3], param_grads[4], param_grads[5], param_grads[6], param_grads[7], param_grads[8], param_grads[9], param_grads[10], param_grads[11], param_grads[12])
```

```python
import functools

import jax
import jax.numpy as jnp
from jax import lax
from jax.experimental import pallas as pl
from jax.experimental.pallas import tpu as pltpu
from jax.sharding import PartitionSpec as P

NBLK = 16
BLK = 171
NBIG = 10
KW = 4
R = 2730

EPSILON = 1e-06

GROUP = 8
AXES = ("batch", "seq")
PAD = 192
WIDE = 2 * PAD
SIZES = [BLK] * NBIG + [BLK - 1] * (NBLK - NBIG)
BEGINS = [sum(SIZES[:i]) for i in range(NBLK)]
ORDER = (0, 2, 4, 6, 1, 3, 5, 7)

BF16 = jnp.bfloat16
F32 = jnp.float32


def device_count():
    return lax.axis_size("batch") * lax.axis_size("seq")


def flat_index():
    return lax.axis_index("batch") * lax.axis_size("seq") + lax.axis_index("seq")


def swap(values, bit):
    return lax.ppermute(values, AXES, [(i, i ^ bit) for i in range(device_count())])


def onward(values):
    count = device_count()
    return lax.ppermute(values, AXES, [(i, (i + GROUP) % count) for i in range(count)])


def low(values):
    return values.astype(BF16)


def wide(values):
    return values.astype(F32)


def pick(values, index):
    return lax.dynamic_index_in_dim(values, index, 0, False)


def put(values, part, index):
    return lax.dynamic_update_index_in_dim(values, part, index, 0)


def after(values, *others):
    return lax.optimization_barrier((values,) + others)[0]


def exchange(pieces, place):
    out = jnp.zeros_like(pieces)
    for bit in range(GROUP):
        part = pick(pieces, place ^ bit)
        out = put(out, swap(part, bit) if bit else part, place ^ bit)
    return out


def ring_gather(block, turn, groups):
    out = jnp.broadcast_to(block, (groups,) + block.shape)
    arrivals = []
    for step in range(1, groups):
        block = onward(block)
        arrivals.append(block)
        out = put(out, block, (turn + groups - step) % groups)
    return out.reshape((-1,) + block.shape[1:]), arrivals


def ring_reduce(values, turn, groups):
    values = values.reshape((groups, -1) + values.shape[1:])
    total = pick(values, (turn + groups - 1) % groups)
    for step in range(1, groups):
        total = wide(onward(low(total))) + pick(values, (turn + 2 * groups - 1 - step) % groups)
    return total


def tiny_gather(values, place):
    for bit in (1, 2, 4):
        other = swap(values, bit)
        values = jnp.where(
            (place & bit) != 0,
            jnp.concatenate([other, values], axis=0),
            jnp.concatenate([values, other], axis=0),
        )
    return values


def group_gather(own):
    half = own.shape[0] // 2
    across, along = swap(own, 4), swap(own, 2)
    first, second = swap(across[:half], 2), swap(along[half:], 4)
    mine = [own, along, across, first, second]
    return jnp.concatenate(mine + [swap(part, 1) for part in mine], axis=0)


def group_reduce(near, far):
    near = near.reshape(4, -1, near.shape[-1])
    total = near + wide(swap(low(far), 1)).reshape(near.shape)
    half = near.shape[1] // 2
    first, second = swap(low(total[3, :half]), 4), swap(low(total[3, half:]), 2)
    across = swap(low(total[2, :half]), 4)
    along = swap(low(total[1, half:]), 2)
    across_rest = swap(low(total[2, half:] + wide(second)), 4)
    along_rest = swap(low(total[1, :half] + wide(first)), 2)
    return (
        total[0]
        + wide(jnp.concatenate([across, across_rest], axis=0))
        + wide(jnp.concatenate([along_rest, along], axis=0))
    )


def to_windows(values):
    leading = [(0, 0)] * (values.ndim - 1)
    parts = [
        jnp.pad(values[..., begin : begin + size], leading + [(0, PAD - size)])
        for begin, size in zip(BEGINS, SIZES)
    ]
    return jnp.concatenate(parts, axis=-1).reshape(values.shape[:-1] + (GROUP, WIDE))


def from_windows(values):
    flat = values.reshape(values.shape[:-2] + (GROUP * WIDE,))
    parts = [flat[..., i * PAD : i * PAD + size] for i, size in enumerate(SIZES)]
    return jnp.concatenate(parts, axis=-1)


def rms_scale(values):
    return lax.rsqrt(jnp.mean(values * values, axis=-1, keepdims=True) + EPSILON)


def norm_back(values, scale, gain, grads):
    scaled = grads * gain
    return scale * (
        scaled - values * scale * scale * jnp.mean(scaled * values, axis=-1, keepdims=True)
    )


def product(left, right):
    return jnp.dot(left, right, preferred_element_type=F32)


def contract_rows(left, right):
    return lax.dot_general(left, right, (((0,), (0,)), ((), ())), preferred_element_type=F32)


def contract_cols(left, right):
    return lax.dot_general(left, right, (((1,), (1,)), ((), ())), preferred_element_type=F32)


def reduce_product(left, right):
    half = left.shape[0] // 2
    far = low(contract_cols(left[half:], right))
    return group_reduce(contract_cols(left[:half], right), far)


def sigmoid(values):
    return 1.0 / (1.0 + jnp.exp(-values))


GELU_A = 0.7978845608028654
GELU_B = 0.044715


def gelu_both(values):
    square = values * values
    bent = jnp.tanh(GELU_A * values * (1.0 + GELU_B * square))
    value = 0.5 * values * (1.0 + bent)
    slope = 0.5 * (1.0 + bent) + 0.5 * values * (1.0 - bent * bent) * GELU_A * (
        1.0 + 3.0 * GELU_B * square
    )
    return value, slope


def minus_expm1(values):
    series = 1.0 / 40320.0
    for divisor in (5040.0, 720.0, 120.0, 24.0, 6.0, 2.0, 1.0):
        series = series * values + 1.0 / divisor
    return -values * series


def gate_values(conv, masks, weight, bias, rate):
    pre = product(low(conv), weight) + bias
    width = conv.shape[1]
    recur, enter = sigmoid(pre[:, :width]), sigmoid(pre[:, width:])
    log_decay = rate * recur
    decay = jnp.exp(log_decay)
    raw_scale = jnp.sqrt(minus_expm1(2.0 * log_decay))
    fresh = masks[:, 3:4] > 0.5
    carry = jnp.where(fresh, 0.0, decay)
    scale = jnp.where(fresh, 1.0, raw_scale)
    return recur, enter, decay, raw_scale, fresh, carry, scale


def convolve(padded, masks, params, steps):
    conv = params[6:7] + params[2:3] * padded[8 : 8 + steps]
    for offset in range(1, KW):
        conv = conv + params[2 + offset : 3 + offset] * (
            padded[8 - offset : 8 - offset + steps] * masks[:, offset - 1 : offset]
        )
    return conv


def forward_kernel(
    place, pre, masks, weight, bias, params, state_out, mixed_out, padded, mult, partial, chain
):
    steps, width = padded.shape[0] - 8, padded.shape[1]
    chunk = steps // 8

    @pl.when(pl.program_id(1) == 0)
    def _():
        padded[0:8] = jnp.zeros((8, width), F32)
        chain[...] = jnp.zeros_like(chain)

    @pl.when(pl.program_id(1) > 0)
    def _():
        padded[0:8] = padded[steps : steps + 8]

    padded[8 : 8 + steps] = pre[0, :, :width]
    conv = convolve(padded, masks[0], params, steps)
    recur, enter, decay, raw_scale, fresh, carry, scale = gate_values(
        conv, masks[0], weight[...], bias[...], params[7:8]
    )
    for lane in range(width // 128):
        lanes = slice(lane * 128, lane * 128 + 128)
        mult[lane] = carry[:, lanes]
        partial[lane] = (scale * enter * conv)[:, lanes]
    for lane in range(width // 128):
        state = jnp.zeros((8, 128), F32)
        reach = jnp.ones((8, 128), F32)
        for step in range(chunk):
            rows = pl.ds(step, 8, stride=chunk)
            factor = mult[lane, rows, :]
            state = factor * state + partial[lane, rows, :]
            reach = factor * reach
            partial[lane, rows, :] = state
            mult[lane, rows, :] = reach
        lanes = slice(lane * 128, lane * 128 + 128)
        entering = chain[0:1, lanes]
        for part in range(8):
            rows = slice(part * chunk, part * chunk + chunk)
            state_out[0, rows, lanes] = partial[lane, rows, :] + mult[lane, rows, :] * entering
            entering = state[part : part + 1] + reach[part : part + 1] * entering
        chain[0:1, lanes] = entering
    value, _ = gelu_both(pre[0, :, width:])
    mixed_out[0] = low(state_out[0] * value)


def backward_kernel(
    place,
    pre,
    rim,
    masks,
    state,
    state_rim,
    d_mixed,
    weight,
    bias,
    params,
    d_both,
    grad_gate,
    grad_small,
    padded,
    mult,
    partial,
    adjoint_all,
    chain,
    later,
):
    steps, width = padded.shape[0] - 8, padded.shape[1]
    chunk = steps // 8
    last = pl.program_id(1) == 0

    @pl.when(last & (pl.program_id(0) == 0))
    def _():
        grad_gate[...] = jnp.zeros_like(grad_gate)
        grad_small[...] = jnp.zeros_like(grad_small)

    @pl.when(last)
    def _():
        chain[...] = jnp.zeros_like(chain)
        later[:, steps : steps + 8] = jnp.zeros((KW - 1, 8, width), F32)

    @pl.when(jnp.logical_not(last))
    def _():
        later[:, steps : steps + 8] = later[:, 0:8]

    mask = masks[0]
    padded[0:8] = rim[0]
    padded[8 : 8 + steps] = pre[0, :, :width]
    conv = convolve(padded, mask, params, steps)
    recur, enter, decay, raw_scale, fresh, carry, scale = gate_values(
        conv, mask, weight[...], bias[...], params[7:8]
    )
    value, slope = gelu_both(pre[0, :, width:])
    d_out = d_mixed[0]
    d_both[0, :, width:] = low(d_out * state[0] * slope)
    d_state = d_out * value
    for lane in range(width // 128):
        lanes = slice(lane * 128, lane * 128 + 128)
        mult[lane, 0:steps, :] = carry[:, lanes]
        mult[lane, steps : steps + 8, :] = jnp.ones((8, 128), F32)
        partial[lane] = d_state[:, lanes]
    for lane in range(width // 128):
        lanes = slice(lane * 128, lane * 128 + 128)
        first_mult = mult[lane, 0:1, :]
        total = jnp.zeros((8, 128), F32)
        reach = jnp.ones((8, 128), F32)
        for step in reversed(range(chunk)):
            rows = pl.ds(step, 8, stride=chunk)
            factor = mult[lane, pl.ds(step + 1, 8, stride=chunk), :]
            total = factor * total + partial[lane, rows, :]
            reach = factor * reach
            partial[lane, rows, :] = total
            mult[lane, pl.ds(step + 1, 8, stride=chunk), :] = reach
        entering = chain[0:1, lanes]
        for part in reversed(range(8)):
            begin = part * chunk
            adjoint_all[begin : begin + chunk, lanes] = (
                partial[lane, begin : begin + chunk, :]
                + mult[lane, begin + 1 : begin + 1 + chunk, :] * entering
            )
            entering = total[part : part + 1] + reach[part : part + 1] * entering
        chain[0:1, lanes] = first_mult * entering
    adjoint = adjoint_all[...]
    padded_state = jnp.concatenate([state_rim[0, 7:8], state[0, : steps - 1]], axis=0)
    d_scale = adjoint * enter * conv
    d_enter = adjoint * scale * conv
    d_log = jnp.where(
        fresh, 0.0, decay * (adjoint * padded_state - d_scale * decay / raw_scale)
    )
    d_recur_pre = d_log * params[7:8] * recur * (1.0 - recur)
    d_enter_pre = d_enter * enter * (1.0 - enter)
    d_pre = jnp.concatenate([d_recur_pre, d_enter_pre], axis=1)
    d_pre_low = low(d_pre)
    d_conv = adjoint * scale * enter + contract_cols(d_pre_low, weight[...])
    grad_gate[...] += contract_rows(low(conv), d_pre_low)
    sums = [
        jnp.sum(d_recur_pre, axis=0, keepdims=True),
        jnp.sum(d_enter_pre, axis=0, keepdims=True),
        jnp.sum(d_conv * padded[8 : 8 + steps], axis=0, keepdims=True),
    ]
    d_branch = d_conv * params[2:3]
    for offset in range(1, KW):
        masked = d_conv * mask[:, offset - 1 : offset]
        sums.append(
            jnp.sum(masked * padded[8 - offset : 8 - offset + steps], axis=0, keepdims=True)
        )
        later[offset - 1, 0:steps] = masked * params[2 + offset : 3 + offset]
        d_branch = d_branch + later[offset - 1, offset : offset + steps]
    sums.append(jnp.sum(d_conv, axis=0, keepdims=True))
    sums.append(jnp.sum(d_log * recur, axis=0, keepdims=True))
    for row, value_sum in enumerate(sums):
        grad_small[row : row + 1] += value_sum
    d_both[0, :, :width] = low(d_branch)


def mixer_calls(rows, shards, steps, channels):
    blocks = rows * shards

    def position(row, shard, place):
        offset = (row * shards + shard) ^ place
        return (offset // 2) + (offset % 2) * (GROUP // 2)

    def whole(*dims):
        return pl.BlockSpec(dims, lambda row, shard, place: (0,) * len(dims))

    params = pltpu.CompilerParams(
        dimension_semantics=("arbitrary", "arbitrary"), vmem_limit_bytes=48 * 1024 * 1024
    )
    lanes = channels // 128
    forward = pl.pallas_call(
        forward_kernel,
        grid_spec=pltpu.PrefetchScalarGridSpec(
            num_scalar_prefetch=1,
            grid=(rows, shards),
            in_specs=[
                pl.BlockSpec(
                    (1, steps, 2 * channels), lambda r, s, p: (position(r, s, p[0]), 0, 0)
                ),
                pl.BlockSpec((1, steps, 8), lambda r, s, p: (r * shards + s, 0, 0)),
                whole(channels, 2 * channels),
                whole(1, 2 * channels),
                whole(8, channels),
            ],
            out_specs=[
                pl.BlockSpec((1, steps, channels), lambda r, s, p: (r * shards + s, 0, 0)),
                pl.BlockSpec((1, steps, channels), lambda r, s, p: (position(r, s, p[0]), 0, 0)),
            ],
            scratch_shapes=[
                pltpu.VMEM((steps + 8, channels), F32),
                pltpu.VMEM((lanes, steps, 128), F32),
                pltpu.VMEM((lanes, steps, 128), F32),
                pltpu.VMEM((8, channels), F32),
            ],
        ),
        out_shape=[
            jax.ShapeDtypeStruct((blocks, steps, channels), F32),
            jax.ShapeDtypeStruct((blocks, steps, channels), BF16),
        ],
        compiler_params=params,
        cost_estimate=pl.CostEstimate(
            flops=blocks * steps * channels * channels * 4,
            bytes_accessed=blocks * steps * channels * 14,
            transcendentals=blocks * steps * channels * 6,
        ),
        name="mixer_forward",
    )

    def turned(shard):
        return shards - 1 - shard

    def before(shard):
        return jnp.maximum(shards - 2 - shard, 0)

    backward = pl.pallas_call(
        backward_kernel,
        grid_spec=pltpu.PrefetchScalarGridSpec(
            num_scalar_prefetch=1,
            grid=(rows, shards),
            in_specs=[
                pl.BlockSpec(
                    (1, steps, 2 * channels), lambda r, s, p: (position(r, turned(s), p[0]), 0, 0)
                ),
                pl.BlockSpec(
                    (1, 8, channels),
                    lambda r, s, p: (position(r, before(s), p[0]), steps // 8 - 1, 0),
                ),
                pl.BlockSpec((1, steps, 8), lambda r, s, p: (r * shards + turned(s), 0, 0)),
                pl.BlockSpec((1, steps, channels), lambda r, s, p: (r * shards + turned(s), 0, 0)),
                pl.BlockSpec(
                    (1, 8, channels),
                    lambda r, s, p: (r * shards + before(s), steps // 8 - 1, 0),
                ),
                pl.BlockSpec(
                    (1, steps, channels), lambda r, s, p: (position(r, turned(s), p[0]), 0, 0)
                ),
                whole(channels, 2 * channels),
                whole(1, 2 * channels),
                whole(8, channels),
            ],
            out_specs=[
                pl.BlockSpec(
                    (1, steps, 2 * channels), lambda r, s, p: (position(r, turned(s), p[0]), 0, 0)
                ),
                whole(channels, 2 * channels),
                whole(8, channels),
            ],
            scratch_shapes=[
                pltpu.VMEM((steps + 8, channels), F32),
                pltpu.VMEM((lanes, steps + 8, 128), F32),
                pltpu.VMEM((lanes, steps, 128), F32),
                pltpu.VMEM((steps, channels), F32),
                pltpu.VMEM((8, channels), F32),
                pltpu.VMEM((KW - 1, steps + 8, channels), F32),
            ],
        ),
        out_shape=[
            jax.ShapeDtypeStruct((blocks, steps, 2 * channels), BF16),
            jax.ShapeDtypeStruct((channels, 2 * channels), F32),
            jax.ShapeDtypeStruct((8, channels), F32),
        ],
        compiler_params=params,
        cost_estimate=pl.CostEstimate(
            flops=blocks * steps * channels * channels * 12,
            bytes_accessed=blocks * steps * channels * 24,
            transcendentals=blocks * steps * channels * 8,
        ),
        name="mixer_backward",
    )
    return forward, backward


def local(
    stream_in,
    segment_ids,
    out_grad,
    branch_weight,
    gating_weight,
    output_weight,
    hidden_gate,
    hidden_linear,
    hidden_output,
    mixer_gain,
    hidden_gain,
    gate_blocks,
    gate_biases,
    conv_taps,
    conv_bias,
    decay_param,
):
    rows_here, steps, model_width = stream_in.shape
    shards = lax.axis_size("seq")
    rows = GROUP // shards
    assert rows_here == 1 and rows * shards == GROUP
    groups = device_count() // GROUP
    place = flat_index() % GROUP
    turn = flat_index() // GROUP
    own_rows, hidden_width = hidden_gate.shape
    hidden_part = hidden_width // GROUP
    tokens = GROUP * steps

    tiny = jnp.concatenate(
        [wide(mixer_gain)[None], wide(hidden_gain)[None], wide(segment_ids)], axis=1
    )
    tiny = tiny_gather(tiny, place)
    gains, _ = ring_gather(tiny[:, : 2 * own_rows], turn, groups)
    mixer_scale = gains[:, :own_rows].reshape(1, model_width)
    hidden_scale = gains[:, own_rows:].reshape(1, model_width)
    segments = tiny[:, 2 * own_rows :].reshape(rows, shards * steps)
    flags = []
    for offset in range(1, KW):
        flags.append(
            jnp.pad(
                wide(segments[:, offset:] == segments[:, :-offset]), ((0, 0), (offset, 0))
            )
        )
    flags.append(1.0 - flags[0])
    flags = flags + [jnp.zeros_like(flags[0])] * 4
    masks = jnp.stack(flags, axis=-1).reshape(GROUP, steps, 8)

    mixer_pieces = jnp.concatenate(
        [to_windows(branch_weight), to_windows(gating_weight), to_windows(output_weight)], axis=-1
    )
    mixer_pieces = exchange(jnp.swapaxes(mixer_pieces, 0, 1), place).reshape(-1, 3 * WIDE)
    hidden_pieces = jnp.concatenate(
        [
            hidden_gate.reshape(own_rows, GROUP, hidden_part),
            hidden_linear.reshape(own_rows, GROUP, hidden_part),
            hidden_output.reshape(own_rows, GROUP, hidden_part),
        ],
        axis=-1,
    )
    hidden_pieces = exchange(
        after(jnp.swapaxes(hidden_pieces, 0, 1), mixer_pieces), place
    ).reshape(-1, 3 * hidden_part)
    both_weight, arrivals = ring_gather(mixer_pieces[:, : 2 * WIDE], turn, groups)
    out_weight, arrivals = ring_gather(
        after(mixer_pieces[:, 2 * WIDE :], arrivals[-2]), turn, groups
    )
    pair_weight, arrivals = ring_gather(
        after(hidden_pieces[:, : 2 * hidden_part], arrivals[-2]), turn, groups
    )
    last_weight, arrivals = ring_gather(
        after(hidden_pieces[:, 2 * hidden_part :], arrivals[-2]), turn, groups
    )

    inputs = wide(stream_in).reshape(steps, model_width)
    inputs_scale = rms_scale(inputs)
    normed = group_gather(low(inputs * inputs_scale * mixer_scale))
    upstream = wide(out_grad).reshape(steps, model_width)
    upstream_all = group_gather(after(out_grad.reshape(steps, model_width), normed))
    pre = product(normed, both_weight).reshape(GROUP, steps, 2 * WIDE)

    rate = -8.0 * jax.nn.softplus(-decay_param)
    params = jnp.concatenate(
        [gate_biases, conv_taps, conv_bias[None], rate[None]], axis=0
    )
    params = pick(jnp.swapaxes(to_windows(params), 0, 1), place)
    bias = params[:2].reshape(1, 2 * WIDE)
    params = params.at[7].set(jnp.where(params[7] == 0.0, -0.01, params[7]))
    blocks = lax.dynamic_slice_in_dim(gate_blocks, 2 * place, 2, 1)
    blocks = jnp.pad(blocks, ((0, 0), (0, 0), (0, PAD - BLK), (0, PAD - BLK)))
    empty = jnp.zeros((PAD, PAD), BF16)
    gate_weight = jnp.concatenate(
        [
            jnp.concatenate([blocks[0, 0], empty, blocks[1, 0], empty], axis=1),
            jnp.concatenate([empty, blocks[0, 1], empty, blocks[1, 1]], axis=1),
        ],
        axis=0,
    )
    mixer_forward, mixer_backward = mixer_calls(rows, shards, steps, WIDE)
    where = place.astype(jnp.int32).reshape(1)
    state, mixed = mixer_forward(where, pre, masks, gate_weight, bias, params)
    mixed = mixed.reshape(tokens, WIDE)
    middle = inputs + reduce_product(mixed, out_weight)

    middle_scale = rms_scale(middle)
    normed_mid = group_gather(low(middle * middle_scale * hidden_scale))
    pair = product(normed_mid, pair_weight)
    gate_pre, linear_pre = pair[:, :hidden_part], pair[:, hidden_part:]
    value, slope = gelu_both(gate_pre)
    hidden = low(value * linear_pre)
    d_hidden = product(upstream_all, last_weight)
    d_pair = jnp.concatenate(
        [low(d_hidden * linear_pre * slope), low(d_hidden * value)], axis=1
    )
    d_middle = upstream + norm_back(
        middle, middle_scale, hidden_scale, reduce_product(d_pair, pair_weight)
    )
    result = low(middle + reduce_product(hidden, last_weight))
    grad_pair = ring_reduce(contract_rows(normed_mid, d_pair), turn, groups)
    grad_last = ring_reduce(contract_rows(upstream_all, hidden), turn, groups)

    middle_low = group_gather(low(d_middle))
    d_mixed = product(middle_low, out_weight).reshape(GROUP, steps, WIDE)
    d_both, grad_gate, grad_small = mixer_backward(
        where, pre, pre, masks, state, state, d_mixed, gate_weight, bias, params
    )
    d_both = d_both.reshape(tokens, 2 * WIDE)
    stream_grad = low(
        d_middle
        + norm_back(inputs, inputs_scale, mixer_scale, reduce_product(d_both, both_weight))
    )
    grad_out = ring_reduce(contract_rows(middle_low, mixed), turn, groups)
    grad_both = ring_reduce(contract_rows(normed, d_both), turn, groups)

    def to_owner(grads):
        return wide(exchange(low(grads).reshape(GROUP, own_rows, -1), place))

    def hidden_rows(grads):
        return jnp.swapaxes(grads, 0, 1).reshape(own_rows, hidden_width)

    def mixer_rows(grads):
        return from_windows(jnp.swapaxes(grads, 0, 1))

    grad_pair, grad_last = to_owner(grad_pair), to_owner(grad_last)
    grad_both, grad_out = to_owner(grad_both), to_owner(grad_out)
    grad_hgate = hidden_rows(grad_pair[..., :hidden_part])
    grad_hlinear = hidden_rows(grad_pair[..., hidden_part:])
    grad_houtput = hidden_rows(grad_last)
    grad_branch = mixer_rows(grad_both[..., :WIDE])
    grad_gating = mixer_rows(grad_both[..., WIDE:])
    grad_output = mixer_rows(grad_out)
    grad_hgain = jnp.sum(
        wide(hidden_gate) * grad_hgate + wide(hidden_linear) * grad_hlinear, axis=1
    ) / wide(hidden_gain)
    grad_mgain = jnp.sum(
        wide(branch_weight) * grad_branch + wide(gating_weight) * grad_gating, axis=1
    ) / wide(mixer_gain)

    upper = lax.broadcasted_iota(jnp.int32, (PAD, 2 * WIDE), 1) % WIDE < PAD
    packed = low(jnp.where(upper, grad_gate[:PAD], grad_gate[PAD:]))
    packed, _ = ring_gather(packed, turn, groups)
    packed = low(jnp.sum(wide(packed.reshape(groups, PAD, 2 * WIDE)), axis=0))
    packed = wide(tiny_gather(packed[None], place))
    packed = packed.reshape(GROUP, PAD, 2, 2, PAD).transpose(2, 0, 3, 1, 4)
    grad_gblocks = packed.reshape(2, NBLK, PAD, PAD)[:, :, :BLK, :BLK]
    small, _ = ring_gather(grad_small, turn, groups)
    small = jnp.sum(small.reshape(groups, 8, WIDE), axis=0)
    small = from_windows(jnp.swapaxes(tiny_gather(small[None], place), 0, 1))
    grad_decay = 8.0 * jax.nn.sigmoid(-decay_param) * small[7]

    shape = (rows_here, steps, model_width)
    return (
        result.reshape(shape),
        stream_grad.reshape(shape),
        grad_branch,
        grad_gating,
        grad_output,
        grad_hgate,
        grad_hlinear,
        grad_houtput,
        grad_mgain,
        grad_hgain,
        grad_gblocks,
        small[:2],
        small[2:6],
        small[6],
        grad_decay,
    )


def solution(mesh):
    return jax.shard_map(
        local,
        mesh=mesh,
        in_specs=(
            P("batch", "seq", None),
            P("batch", "seq"),
            P("batch", "seq", None),
            P(("batch", "seq"), None),
            P(("batch", "seq"), None),
            P(("batch", "seq"), None),
            P(("batch", "seq"), None),
            P(("batch", "seq"), None),
            P(("batch", "seq"), None),
            P(("batch", "seq")),
            P(("batch", "seq")),
            P(),
            P(),
            P(),
            P(),
            P(),
        ),
        out_specs=(
            P("batch", "seq", None),
            P("batch", "seq", None),
            P(("batch", "seq"), None),
            P(("batch", "seq"), None),
            P(("batch", "seq"), None),
            P(("batch", "seq"), None),
            P(("batch", "seq"), None),
            P(("batch", "seq"), None),
            P(("batch", "seq")),
            P(("batch", "seq")),
            P(),
            P(),
            P(),
            P(),
            P(),
        ),
        check_vma=False,
    )
```

```python
import functools

import jax
import jax.numpy as jnp
from jax import lax
from jax.experimental import pallas as pl
from jax.experimental.pallas import tpu as pltpu
from jax.sharding import PartitionSpec as P

NBLK = 16
BLK = 171
NBIG = 10
KW = 4
R = 2730

EPSILON = 1e-06

GROUP = 8
AXES = ("batch", "seq")
PAD = 192
SMALL = 176
WIDE = 2 * PAD
SIZES = [BLK] * NBIG + [BLK - 1] * (NBLK - NBIG)
BEGINS = [sum(SIZES[:i]) for i in range(NBLK)]
ORDER = (0, 2, 4, 6, 1, 3, 5, 7)

BF16 = jnp.bfloat16
F32 = jnp.float32


def device_count():
    return lax.axis_size("batch") * lax.axis_size("seq")


def flat_index():
    return lax.axis_index("batch") * lax.axis_size("seq") + lax.axis_index("seq")


def swap(values, bit):
    return lax.ppermute(values, AXES, [(i, i ^ bit) for i in range(device_count())])


def onward(values, turns):
    count = device_count()
    pairs = [(i, (i + turns * GROUP) % count) for i in range(count)]
    return lax.ppermute(values, AXES, pairs)


def low(values):
    return values.astype(BF16)


def wide(values):
    return values.astype(F32)


def pick(values, index):
    return lax.dynamic_index_in_dim(values, index, 0, False)


def put(values, part, index):
    return lax.dynamic_update_index_in_dim(values, part, index, 0)


def after(values, *others):
    return lax.optimization_barrier((values,) + others)[0]


def ring_groups():
    count = device_count()
    return [list(range(i, count, GROUP)) for i in range(GROUP)]


def ring_gather(block):
    return lax.all_gather(block, AXES, axis=0, tiled=True, axis_index_groups=ring_groups())


def ring_reduce(values):
    return lax.psum_scatter(
        values, AXES, scatter_dimension=0, tiled=True, axis_index_groups=ring_groups()
    )


def ring_stack(block, turn, groups, wait_for=()):
    arrived = [onward(block, step) for step in range(1, groups)]
    arrived, _ = lax.optimization_barrier((arrived, wait_for))
    out = jnp.broadcast_to(block, (groups,) + block.shape)
    for step in range(1, groups):
        out = put(out, arrived[step - 1], (turn + groups - step) % groups)
    return out


def ring_sum(values, turn, groups):
    chunks = values.reshape((groups, -1) + values.shape[1:])
    total = wide(pick(chunks, turn))
    for step in range(1, groups):
        total = total + wide(onward(pick(chunks, (turn + step) % groups), step))
    return low(total)


def all_swapped(parts):
    return [parts[0]] + [swap(parts[bit], bit) for bit in range(1, GROUP)]


def first_swaps(own):
    return swap(own, 4), swap(own, 2)


def group_parts(own, swapped=None):
    half = own.shape[0] // 2
    across, along = swapped or first_swaps(own)
    first, second = swap(across[:half], 2), swap(along[half:], 4)
    mine = [own, along, across, first, second]
    return mine + [swap(part, 1) for part in mine]


def group_gather(own):
    return jnp.concatenate(group_parts(own), axis=0)


def pair_total(near, far):
    near = near.reshape(4, -1, near.shape[-1])
    return near + wide(swap(low(far), 1)).reshape(near.shape)


def send_totals(total):
    half = total.shape[1] // 2
    return (
        swap(low(total[3, :half]), 4),
        swap(low(total[3, half:]), 2),
        swap(low(total[2, :half]), 4),
        swap(low(total[1, half:]), 2),
    )


def join_totals(total, arrived):
    first, second, across, along = arrived
    half = total.shape[1] // 2
    across_rest = swap(low(total[2, half:] + wide(second)), 4)
    along_rest = swap(low(total[1, :half] + wide(first)), 2)
    return (
        total[0]
        + wide(jnp.concatenate([across, across_rest], axis=0))
        + wide(jnp.concatenate([along_rest, along], axis=0))
    )


def group_total(total):
    return join_totals(total, send_totals(total))


def to_windows(values):
    leading = [(0, 0)] * (values.ndim - 1)
    parts = [
        jnp.pad(values[..., begin : begin + size], leading + [(0, PAD - size)])
        for begin, size in zip(BEGINS, SIZES)
    ]
    return jnp.concatenate(parts, axis=-1).reshape(values.shape[:-1] + (GROUP, WIDE))


def norm_kernel(values, gain, out):
    rows = wide(values[...])
    out[...] = low(rows * rms_scale(rows) * gain[...])


def norm_rows(values, gain, steps):
    rows, width = values.shape
    return pl.pallas_call(
        norm_kernel,
        grid=(rows // steps,),
        in_specs=[
            pl.BlockSpec((steps, width), lambda i: (i, 0)),
            pl.BlockSpec((1, width), lambda i: (0, 0)),
        ],
        out_specs=pl.BlockSpec((steps, width), lambda i: (i, 0)),
        out_shape=jax.ShapeDtypeStruct((rows, width), BF16),
        compiler_params=pltpu.CompilerParams(vmem_limit_bytes=48 * 1024 * 1024),
        cost_estimate=pl.CostEstimate(flops=1, bytes_accessed=1, transcendentals=0),
        name="norm_rows",
    )(values, gain)


SCALAR = pl.BlockSpec(memory_space=pltpu.SMEM)
BUFFER = pl.BlockSpec(memory_space=pltpu.VMEM)


def simple_call(kernel, name, place, arrays, outs, scratch=()):
    moved = sum(a.size * a.dtype.itemsize for a in arrays)
    return pl.pallas_call(
        kernel,
        in_specs=[SCALAR] + [BUFFER] * len(arrays),
        out_specs=[BUFFER] * len(outs),
        out_shape=[jax.ShapeDtypeStruct(shape, dtype) for shape, dtype in outs],
        scratch_shapes=list(scratch),
        compiler_params=pltpu.CompilerParams(vmem_limit_bytes=48 * 1024 * 1024),
        cost_estimate=pl.CostEstimate(flops=moved, bytes_accessed=2 * moved, transcendentals=0),
        name=name,
    )(place, *arrays)


def split_mixer_kernel(place, branch, gating, output, tiny, *rest):
    outs, held = rest[:GROUP], rest[GROUP]
    rows = branch.shape[0]
    held[...] = jnp.zeros_like(held)
    for slot, ref in enumerate((branch, gating, output)):
        values = wide(ref[...])
        for i in range(NBLK):
            begin = slot * WIDE + (i % 2) * PAD
            held[i // 2, :, begin : begin + SIZES[i]] = values[
                :, BEGINS[i] : BEGINS[i] + SIZES[i]
            ]
    for bit in range(GROUP):
        outs[bit][:rows] = low(held[place[0] ^ bit])
        outs[bit][rows:] = tiny[...]


def split_hidden_kernel(place, gate, linear, output, *outs):
    part = gate.shape[1] // GROUP
    for bit in range(GROUP):
        columns = pl.ds(pl.multiple_of((place[0] ^ bit) * part, 128), part)
        for slot, ref in enumerate((gate, linear, output)):
            outs[bit][:, slot * part : (slot + 1) * part] = ref[:, columns]


def collect_kernel(place, *refs):
    parts, (first, second) = refs[:GROUP], refs[GROUP:]
    cut = first.shape[2]
    for bit in range(GROUP):
        first[place[0] ^ bit] = parts[bit][:, :cut]
        second[place[0] ^ bit] = parts[bit][:, cut:]


def collect_mixer_kernel(place, *refs):
    parts, (columns, tiny) = refs[:GROUP], refs[GROUP:]
    rows = columns.shape[1]
    for bit in range(GROUP):
        columns[place[0] ^ bit] = parts[bit][:rows]
        tiny[place[0] ^ bit] = wide(parts[bit][rows:])[:1, : tiny.shape[2]]


def deal_kernel(place, *refs):
    values, outs = refs[:-GROUP], refs[-GROUP:]
    for bit in range(GROUP):
        begin = 0
        for ref in values:
            outs[bit][:, begin : begin + ref.shape[2]] = ref[place[0] ^ bit]
            begin += ref.shape[2]


def hidden_owner_kernel(place, gate, linear, gain, *refs):
    parts, outs = refs[:GROUP], refs[GROUP:]
    part = gate.shape[1] // GROUP
    total = jnp.zeros((gate.shape[0], 1), F32)
    for bit in range(GROUP):
        columns = pl.ds(pl.multiple_of((place[0] ^ bit) * part, 128), part)
        d_gate, d_linear = wide(parts[bit][:, :part]), wide(parts[bit][:, part : 2 * part])
        outs[0][:, columns] = d_gate
        outs[1][:, columns] = d_linear
        outs[2][:, columns] = wide(parts[bit][:, 2 * part : 3 * part])
        terms = d_gate * wide(gate[:, columns]) + d_linear * wide(linear[:, columns])
        total = total + jnp.sum(terms, axis=1, keepdims=True)
    outs[3][...] = total / gain[...]


def mixer_owner_kernel(place, branch, gating, gain, *refs):
    boths, lasts = refs[:GROUP], refs[GROUP : 2 * GROUP]
    outs, held = refs[2 * GROUP : -1], refs[-1]
    for bit in range(GROUP):
        held[place[0] ^ bit, :, : 2 * WIDE] = wide(boths[bit][...])
        held[place[0] ^ bit, :, 2 * WIDE :] = wide(lasts[bit][:, -WIDE:])
    for slot in range(3):
        for i in range(NBLK):
            begin = slot * WIDE + (i % 2) * PAD
            outs[slot][:, BEGINS[i] : BEGINS[i] + SIZES[i]] = held[
                i // 2, :, begin : begin + SIZES[i]
            ]
    terms = outs[0][...] * wide(branch[...]) + outs[1][...] * wide(gating[...])
    outs[3][...] = jnp.sum(terms, axis=1, keepdims=True) / gain[...]


def gates_owner_kernel(place, *refs):
    parts, (blocks, small), held = refs[:GROUP], refs[GROUP : GROUP + 2], refs[-1]
    for part, bit in zip(parts, ORDER):
        device = place[0] ^ bit
        for gate in range(2):
            for block in range(2):
                begin = gate * WIDE + block * PAD
                blocks[gate, 2 * device + block] = wide(part[:BLK, begin : begin + BLK])
        ending = wide(part[SMALL:PAD])[:8]
        held[device] = ending[:, :WIDE] + ending[:, WIDE:]
    for i in range(NBLK):
        begin = (i % 2) * PAD
        small[:, BEGINS[i] : BEGINS[i] + SIZES[i]] = held[i // 2, :, begin : begin + SIZES[i]]


def rms_scale(values):
    return lax.rsqrt(jnp.mean(values * values, axis=-1, keepdims=True) + EPSILON)


def norm_back(values, scale, gain, grads):
    scaled = grads * gain
    return scale * (
        scaled - values * scale * scale * jnp.mean(scaled * values, axis=-1, keepdims=True)
    )


def product(left, right):
    return jnp.dot(left, right, preferred_element_type=F32)


def contract_rows(left, right):
    return lax.dot_general(left, right, (((0,), (0,)), ((), ())), preferred_element_type=F32)


def contract_cols(left, right):
    return lax.dot_general(left, right, (((1,), (1,)), ((), ())), preferred_element_type=F32)


def pair_product(left, right, first=None):
    half = left.shape[0] // 2
    far = low(contract_cols(left[half:], right))
    near = left[:half] if first is None else after(left[:half], first)
    return pair_total(contract_cols(near, right), far)


def sigmoid(values):
    return 1.0 / (1.0 + jnp.exp(-values))


GELU_A = 0.7978845608028654
GELU_B = 0.044715


def gelu_both(values):
    square = values * values
    bent = jnp.tanh(GELU_A * values * (1.0 + GELU_B * square))
    value = 0.5 * values * (1.0 + bent)
    slope = 0.5 * (1.0 + bent) + 0.5 * values * (1.0 - bent * bent) * GELU_A * (
        1.0 + 3.0 * GELU_B * square
    )
    return value, slope


def minus_expm1(values):
    series = 1.0 / 40320.0
    for divisor in (5040.0, 720.0, 120.0, 24.0, 6.0, 2.0, 1.0):
        series = series * values + 1.0 / divisor
    return -values * series


def repeated(values, width):
    return jnp.concatenate([values] * (width // 128), axis=1)


def gate_values(conv, fresh, weight, bias, rate):
    pre = product(low(conv), weight) + bias
    width = conv.shape[1]
    recur, enter = sigmoid(pre[:, :width]), sigmoid(pre[:, width:])
    log_decay = rate * recur
    decay = jnp.exp(log_decay)
    raw_scale = jnp.sqrt(minus_expm1(2.0 * log_decay))
    carry = jnp.where(fresh, 0.0, decay)
    scale = jnp.where(fresh, 1.0, raw_scale)
    return recur, enter, decay, raw_scale, carry, scale


def same_masks(numbers, steps, width):
    own = numbers[8 : 8 + steps]
    masks = [
        repeated(jnp.where(numbers[8 - k : 8 - k + steps] == own, 1.0, 0.0), width)
        for k in range(1, KW)
    ]
    return masks, masks[0] < 0.5


def convolve(padded, masks, params, steps):
    conv = params[6:7] + params[2:3] * padded[8 : 8 + steps]
    for offset in range(1, KW):
        conv = conv + params[2 + offset : 3 + offset] * (
            padded[8 - offset : 8 - offset + steps] * masks[offset - 1]
        )
    return conv


def forward_kernel(
    place,
    pre,
    segment,
    weight,
    bias,
    params,
    state_out,
    mixed_out,
    padded,
    mult,
    partial,
    chain,
    numbers,
):
    steps, width = padded.shape[0] - 8, padded.shape[1]
    chunk = steps // 8

    @pl.when(pl.program_id(1) == 0)
    def _():
        padded[0:8] = jnp.zeros((8, width), F32)
        numbers[0:8] = jnp.full((8, 128), -1.0, F32)
        chain[...] = jnp.zeros_like(chain)

    @pl.when(pl.program_id(1) > 0)
    def _():
        padded[0:8] = padded[steps : steps + 8]
        numbers[0:8] = numbers[steps : steps + 8]

    padded[8 : 8 + steps] = pre[0, :, :width]
    numbers[8 : 8 + steps] = segment[0]
    masks, fresh = same_masks(numbers, steps, width)
    conv = convolve(padded, masks, params, steps)
    recur, enter, decay, raw_scale, carry, scale = gate_values(
        conv, fresh, weight[...], bias[...], params[7:8]
    )
    for lane in range(width // 128):
        lanes = slice(lane * 128, lane * 128 + 128)
        mult[lane] = carry[:, lanes]
        partial[lane] = (scale * enter * conv)[:, lanes]
    for lane in range(width // 128):
        state = jnp.zeros((8, 128), F32)
        reach = jnp.ones((8, 128), F32)
        for step in range(chunk):
            rows = pl.ds(step, 8, stride=chunk)
            factor = mult[lane, rows, :]
            state = factor * state + partial[lane, rows, :]
            reach = factor * reach
            partial[lane, rows, :] = state
            mult[lane, rows, :] = reach
        lanes = slice(lane * 128, lane * 128 + 128)
        entering = chain[0:1, lanes]
        for part in range(8):
            rows = slice(part * chunk, part * chunk + chunk)
            state_out[0, rows, lanes] = partial[lane, rows, :] + mult[lane, rows, :] * entering
            entering = state[part : part + 1] + reach[part : part + 1] * entering
        chain[0:1, lanes] = entering
    value, _ = gelu_both(pre[0, :, width:])
    mixed_out[0] = low(state_out[0] * value)


def backward_kernel(
    place,
    pre,
    rim,
    segment,
    segment_rim,
    state,
    state_rim,
    d_mixed,
    weight,
    bias,
    params,
    d_both,
    packed,
    padded,
    mult,
    partial,
    adjoint_all,
    chain,
    later,
    numbers,
    grad_gate,
    grad_small,
):
    steps, width = padded.shape[0] - 8, padded.shape[1]
    chunk = steps // 8
    last = pl.program_id(1) == 0
    first = pl.program_id(1) == pl.num_programs(1) - 1

    @pl.when(last & (pl.program_id(0) == 0))
    def _():
        grad_gate[...] = jnp.zeros_like(grad_gate)
        grad_small[...] = jnp.zeros_like(grad_small)

    @pl.when(last)
    def _():
        chain[...] = jnp.zeros_like(chain)
        later[:, steps : steps + 8] = jnp.zeros((KW - 1, 8, width), F32)

    @pl.when(jnp.logical_not(last))
    def _():
        later[:, steps : steps + 8] = later[:, 0:8]

    padded[0:8] = rim[0]
    padded[8 : 8 + steps] = pre[0, :, :width]
    numbers[0:8] = jnp.where(first, -1.0, segment_rim[0])
    numbers[8 : 8 + steps] = segment[0]
    masks, fresh = same_masks(numbers, steps, width)
    conv = convolve(padded, masks, params, steps)
    recur, enter, decay, raw_scale, carry, scale = gate_values(
        conv, fresh, weight[...], bias[...], params[7:8]
    )
    value, slope = gelu_both(pre[0, :, width:])
    d_out = d_mixed[0]
    d_both[0, :, width:] = low(d_out * state[0] * slope)
    d_state = d_out * value
    for lane in range(width // 128):
        lanes = slice(lane * 128, lane * 128 + 128)
        mult[lane, 0:steps, :] = carry[:, lanes]
        mult[lane, steps : steps + 8, :] = jnp.ones((8, 128), F32)
        partial[lane] = d_state[:, lanes]
    for lane in range(width // 128):
        lanes = slice(lane * 128, lane * 128 + 128)
        first_mult = mult[lane, 0:1, :]
        total = jnp.zeros((8, 128), F32)
        reach = jnp.ones((8, 128), F32)
        for step in reversed(range(chunk)):
            rows = pl.ds(step, 8, stride=chunk)
            factor = mult[lane, pl.ds(step + 1, 8, stride=chunk), :]
            total = factor * total + partial[lane, rows, :]
            reach = factor * reach
            partial[lane, rows, :] = total
            mult[lane, pl.ds(step + 1, 8, stride=chunk), :] = reach
        entering = chain[0:1, lanes]
        for part in reversed(range(8)):
            begin = part * chunk
            adjoint_all[begin : begin + chunk, lanes] = (
                partial[lane, begin : begin + chunk, :]
                + mult[lane, begin + 1 : begin + 1 + chunk, :] * entering
            )
            entering = total[part : part + 1] + reach[part : part + 1] * entering
        chain[0:1, lanes] = first_mult * entering
    adjoint = adjoint_all[...]
    padded_state = jnp.concatenate([state_rim[0, 7:8], state[0, : steps - 1]], axis=0)
    d_scale = adjoint * enter * conv
    d_enter = adjoint * scale * conv
    d_log = jnp.where(
        fresh, 0.0, decay * (adjoint * padded_state - d_scale * decay / raw_scale)
    )
    d_recur_pre = d_log * params[7:8] * recur * (1.0 - recur)
    d_enter_pre = d_enter * enter * (1.0 - enter)
    d_pre = jnp.concatenate([d_recur_pre, d_enter_pre], axis=1)
    d_pre_low = low(d_pre)
    d_conv = adjoint * scale * enter + contract_cols(d_pre_low, weight[...])
    grad_gate[...] += contract_rows(low(conv), d_pre_low)
    sums = [
        jnp.sum(d_recur_pre, axis=0, keepdims=True),
        jnp.sum(d_enter_pre, axis=0, keepdims=True),
        jnp.sum(d_conv * padded[8 : 8 + steps], axis=0, keepdims=True),
    ]
    d_branch = d_conv * params[2:3]
    for offset in range(1, KW):
        masked = d_conv * masks[offset - 1]
        sums.append(
            jnp.sum(masked * padded[8 - offset : 8 - offset + steps], axis=0, keepdims=True)
        )
        later[offset - 1, 0:steps] = masked * params[2 + offset : 3 + offset]
        d_branch = d_branch + later[offset - 1, offset : offset + steps]
    sums.append(jnp.sum(d_conv, axis=0, keepdims=True))
    sums.append(jnp.sum(d_log * recur, axis=0, keepdims=True))
    for row, value_sum in enumerate(sums):
        grad_small[row : row + 1] += value_sum
    d_both[0, :, :width] = low(d_branch)

    @pl.when(first & (pl.program_id(0) == pl.num_programs(0) - 1))
    def _():
        side = lax.broadcasted_iota(jnp.int32, (PAD, 2 * width), 1) % width
        blocks = jnp.where(side < PAD, grad_gate[0:PAD], grad_gate[PAD : 2 * PAD])
        rest = grad_small[...] - wide(low(grad_small[...]))
        packed[...] = low(blocks)
        packed[SMALL:PAD] = low(
            jnp.concatenate([jnp.concatenate([grad_small[...], rest], axis=1), blocks[-8:]], axis=0)
        )


def mixer_calls(rows, shards, steps, channels):
    blocks = rows * shards

    def position(row, shard, place):
        offset = (row * shards + shard) ^ place
        return (offset // 2) + (offset % 2) * (GROUP // 2)

    def whole(*dims):
        return pl.BlockSpec(dims, lambda row, shard, place: (0,) * len(dims))

    params = pltpu.CompilerParams(
        dimension_semantics=("arbitrary", "arbitrary"), vmem_limit_bytes=48 * 1024 * 1024
    )
    lanes = channels // 128
    forward = pl.pallas_call(
        forward_kernel,
        grid_spec=pltpu.PrefetchScalarGridSpec(
            num_scalar_prefetch=1,
            grid=(rows, shards),
            in_specs=[
                pl.BlockSpec(
                    (1, steps, 2 * channels), lambda r, s, p: (position(r, s, p[0]), 0, 0)
                ),
                pl.BlockSpec((1, steps, 128), lambda r, s, p: (r * shards + s, 0, 0)),
                whole(channels, 2 * channels),
                whole(1, 2 * channels),
                whole(8, channels),
            ],
            out_specs=[
                pl.BlockSpec((1, steps, channels), lambda r, s, p: (r * shards + s, 0, 0)),
                pl.BlockSpec((1, steps, channels), lambda r, s, p: (position(r, s, p[0]), 0, 0)),
            ],
            scratch_shapes=[
                pltpu.VMEM((steps + 8, channels), F32),
                pltpu.VMEM((lanes, steps, 128), F32),
                pltpu.VMEM((lanes, steps, 128), F32),
                pltpu.VMEM((8, channels), F32),
                pltpu.VMEM((steps + 8, 128), F32),
            ],
        ),
        out_shape=[
            jax.ShapeDtypeStruct((blocks, steps, channels), F32),
            jax.ShapeDtypeStruct((blocks, steps, channels), BF16),
        ],
        compiler_params=params,
        cost_estimate=pl.CostEstimate(flops=1, bytes_accessed=1, transcendentals=0),
        name="mixer_forward",
    )

    def turned(shard):
        return shards - 1 - shard

    def before(shard):
        return jnp.maximum(shards - 2 - shard, 0)

    backward = pl.pallas_call(
        backward_kernel,
        grid_spec=pltpu.PrefetchScalarGridSpec(
            num_scalar_prefetch=1,
            grid=(rows, shards),
            in_specs=[
                pl.BlockSpec(
                    (1, steps, 2 * channels), lambda r, s, p: (position(r, turned(s), p[0]), 0, 0)
                ),
                pl.BlockSpec(
                    (1, 8, channels),
                    lambda r, s, p: (position(r, before(s), p[0]), steps // 8 - 1, 0),
                ),
                pl.BlockSpec((1, steps, 128), lambda r, s, p: (r * shards + turned(s), 0, 0)),
                pl.BlockSpec(
                    (1, 8, 128), lambda r, s, p: (r * shards + before(s), steps // 8 - 1, 0)
                ),
                pl.BlockSpec((1, steps, channels), lambda r, s, p: (r * shards + turned(s), 0, 0)),
                pl.BlockSpec(
                    (1, 8, channels),
                    lambda r, s, p: (r * shards + before(s), steps // 8 - 1, 0),
                ),
                pl.BlockSpec(
                    (1, steps, channels), lambda r, s, p: (position(r, turned(s), p[0]), 0, 0)
                ),
                whole(channels, 2 * channels),
                whole(1, 2 * channels),
                whole(8, channels),
            ],
            out_specs=[
                pl.BlockSpec(
                    (1, steps, 2 * channels), lambda r, s, p: (position(r, turned(s), p[0]), 0, 0)
                ),
                whole(PAD, 2 * channels),
            ],
            scratch_shapes=[
                pltpu.VMEM((steps + 8, channels), F32),
                pltpu.VMEM((lanes, steps + 8, 128), F32),
                pltpu.VMEM((lanes, steps, 128), F32),
                pltpu.VMEM((steps, channels), F32),
                pltpu.VMEM((8, channels), F32),
                pltpu.VMEM((KW - 1, steps + 8, channels), F32),
                pltpu.VMEM((steps + 8, 128), F32),
                pltpu.VMEM((channels, 2 * channels), F32),
                pltpu.VMEM((8, channels), F32),
            ],
        ),
        out_shape=[
            jax.ShapeDtypeStruct((blocks, steps, 2 * channels), BF16),
            jax.ShapeDtypeStruct((PAD, 2 * channels), BF16),
        ],
        compiler_params=params,
        cost_estimate=pl.CostEstimate(
            flops=blocks * steps * channels * channels * 12,
            bytes_accessed=blocks * steps * channels * 24,
            transcendentals=blocks * steps * channels * 8,
        ),
        name="mixer_backward",
    )
    return forward, backward


def local(
    stream_in,
    segment_ids,
    out_grad,
    branch_weight,
    gating_weight,
    output_weight,
    hidden_gate,
    hidden_linear,
    hidden_output,
    mixer_gain,
    hidden_gain,
    gate_blocks,
    gate_biases,
    conv_taps,
    conv_bias,
    decay_param,
):
    rows_here, steps, model_width = stream_in.shape
    shards = lax.axis_size("seq")
    rows = GROUP // shards
    assert rows_here == 1 and rows * shards == GROUP
    groups = device_count() // GROUP
    place = flat_index() % GROUP
    turn = flat_index() // GROUP
    own_rows, hidden_width = hidden_gate.shape
    hidden_part = hidden_width // GROUP
    tokens = GROUP * steps

    where = place.astype(jnp.int32).reshape(1)
    tiny = jnp.concatenate(
        [mixer_gain[None], hidden_gain[None], low(segment_ids)], axis=1
    )
    tiny_width = tiny.shape[1]
    mixer_parts = simple_call(
        split_mixer_kernel,
        "split_mixer",
        where,
        (
            branch_weight,
            gating_weight,
            output_weight,
            jnp.pad(tiny, ((0, 15), (0, 3 * WIDE - tiny_width))),
        ),
        [((own_rows + 16, 3 * WIDE), BF16)] * GROUP,
        [pltpu.VMEM((GROUP, own_rows, 3 * WIDE), F32)],
    )
    mixer_rows, tiny = simple_call(
        collect_mixer_kernel,
        "collect_mixer",
        where,
        all_swapped(mixer_parts),
        [
            ((GROUP, own_rows, 3 * WIDE), BF16),
            ((GROUP, 1, tiny_width), F32),
        ],
    )
    tiny = tiny.reshape(GROUP, tiny_width)
    mixer_weight = ring_gather(mixer_rows.reshape(-1, 3 * WIDE))
    both_weight, out_weight = mixer_weight[:, : 2 * WIDE], mixer_weight[:, 2 * WIDE :]
    gains = ring_stack(tiny[:, : 2 * own_rows], turn, groups)
    mixer_scale = gains[..., :own_rows].reshape(1, model_width)
    hidden_scale = gains[..., own_rows:].reshape(1, model_width)
    segments = jnp.broadcast_to(tiny[:, 2 * own_rows :, None], (GROUP, steps, 128))

    inputs = wide(stream_in).reshape(steps, model_width)
    inputs_scale = rms_scale(inputs)
    parts = group_parts(stream_in.reshape(steps, model_width))
    normed = norm_rows(jnp.concatenate(parts, axis=0), mixer_scale, steps)
    upstream = wide(out_grad).reshape(steps, model_width)
    hidden_parts = simple_call(
        split_hidden_kernel,
        "split_hidden",
        where,
        (hidden_gate, hidden_linear, hidden_output),
        [((own_rows, 3 * hidden_part), BF16)] * GROUP,
    )
    pair_rows, last_rows = simple_call(
        collect_kernel,
        "collect_hidden",
        where,
        all_swapped(lax.optimization_barrier((hidden_parts, parts[3:5]))[0]),
        [((GROUP, own_rows, 2 * hidden_part), BF16), ((GROUP, own_rows, hidden_part), BF16)],
    )
    pair_weight = ring_gather(pair_rows.reshape(-1, 2 * hidden_part))
    pre = product(after(normed, pair_rows), both_weight).reshape(GROUP, steps, 2 * WIDE)

    rate = -8.0 * jax.nn.softplus(-decay_param)
    params = jnp.concatenate(
        [gate_biases, conv_taps, conv_bias[None], rate[None]], axis=0
    )
    params = pick(jnp.swapaxes(to_windows(params), 0, 1), place)
    bias = params[:2].reshape(1, 2 * WIDE)
    params = params.at[7].set(jnp.where(params[7] == 0.0, -0.01, params[7]))
    blocks = lax.dynamic_slice_in_dim(gate_blocks, 2 * place, 2, 1)
    blocks = jnp.pad(blocks, ((0, 0), (0, 0), (0, PAD - BLK), (0, PAD - BLK)))
    empty = jnp.zeros((PAD, PAD), BF16)
    gate_weight = jnp.concatenate(
        [
            jnp.concatenate([blocks[0, 0], empty, blocks[1, 0], empty], axis=1),
            jnp.concatenate([empty, blocks[0, 1], empty, blocks[1, 1]], axis=1),
        ],
        axis=0,
    )
    mixer_forward, mixer_backward = mixer_calls(rows, shards, steps, WIDE)
    state, mixed = mixer_forward(where, pre, segments, gate_weight, bias, params)
    mixed = mixed.reshape(tokens, WIDE)
    last_weight = ring_gather(after(last_rows, mixed).reshape(-1, hidden_part))
    middle = inputs + group_total(pair_product(mixed, out_weight))

    middle_scale = rms_scale(middle)
    own = low(middle * middle_scale * hidden_scale)
    parts = group_parts(own, lax.optimization_barrier((first_swaps(own), pair_weight))[0])
    own = out_grad.reshape(steps, model_width)
    swapped = first_swaps(lax.optimization_barrier((own, parts[3:5]))[0])
    normed_mid = jnp.concatenate(parts, axis=0)
    upstream_all = jnp.concatenate(group_parts(own, swapped), axis=0)
    pair = product(normed_mid, pair_weight)
    gate_pre, linear_pre = pair[:, :hidden_part], pair[:, hidden_part:]
    value, slope = gelu_both(gate_pre)
    hidden = low(value * linear_pre)
    grad_last_low = low(contract_rows(upstream_all, hidden))
    grad_last = ring_reduce(grad_last_low)
    d_hidden = product(after(upstream_all, grad_last_low), last_weight)
    d_pair = jnp.concatenate(
        [low(d_hidden * linear_pre * slope), low(d_hidden * value)], axis=1
    )
    grad_pair_low = low(contract_rows(normed_mid, d_pair))
    grad_pair = ring_reduce(grad_pair_low)
    d_normed_mid = pair_product(after(d_pair, grad_pair_low), pair_weight)
    hidden_out = pair_product(after(hidden, d_normed_mid), last_weight)
    result = low(middle + group_total(hidden_out))
    d_middle = upstream + norm_back(
        middle, middle_scale, hidden_scale, group_total(d_normed_mid)
    )

    def to_owner(name, *grads):
        grads = [values.reshape(GROUP, own_rows, -1) for values in grads]
        width = sum(values.shape[2] for values in grads)
        parts = simple_call(
            deal_kernel, name, where, grads, [((own_rows, width), BF16)] * GROUP
        )
        return all_swapped(parts)

    middle_low = group_gather(after(low(d_middle), grad_last, hidden_out))
    d_mixed = product(middle_low, out_weight).reshape(GROUP, steps, WIDE)
    grad_out_low = low(contract_rows(middle_low, mixed))
    grad_out = ring_reduce(grad_out_low)
    d_mixed = after(d_mixed, grad_out_low, grad_pair)
    d_both, packed = mixer_backward(
        where, pre, pre, segments, segments, state, state, d_mixed, gate_weight, bias, params
    )
    d_both = d_both.reshape(tokens, 2 * WIDE)
    grad_both_low = low(contract_rows(normed, after(d_both, grad_out)))
    grad_both = ring_reduce(grad_both_low)
    early_parts = to_owner("deal_early", grad_pair, grad_last, grad_out)
    d_normed = pair_product(after(d_both, grad_both_low), both_weight)
    d_normed = group_total(d_normed)
    stream_grad = low(d_middle + norm_back(inputs, inputs_scale, mixer_scale, d_normed))

    grad_hgate, grad_hlinear, grad_houtput, grad_hgain = simple_call(
        hidden_owner_kernel,
        "hidden_owner",
        where,
        (hidden_gate, hidden_linear, wide(hidden_gain)[:, None])
        + tuple(early_parts),
        [((own_rows, hidden_width), F32)] * 3 + [((own_rows, 1), F32)],
    )
    grad_branch, grad_gating, grad_output, grad_mgain = simple_call(
        mixer_owner_kernel,
        "mixer_owner",
        where,
        (branch_weight, gating_weight, wide(mixer_gain)[:, None])
        + tuple(to_owner("deal_both", grad_both) + early_parts),
        [((own_rows, R), F32)] * 3 + [((own_rows, 1), F32)],
        [pltpu.VMEM((GROUP, own_rows, 3 * WIDE), F32)],
    )

    packed = ring_stack(ring_sum(packed, turn, groups), turn, groups).reshape(PAD, 2 * WIDE)
    across, along = swap(packed, 4), swap(packed, 2)
    near = [packed, along, across, swap(across, 2)]
    grad_gblocks, small = simple_call(
        gates_owner_kernel,
        "gates_owner",
        where,
        near + [swap(part, 1) for part in near],
        [((2, NBLK, BLK, BLK), F32), ((8, R), F32)],
        [pltpu.VMEM((GROUP, 8, WIDE), F32)],
    )
    grad_decay = 8.0 * jax.nn.sigmoid(-decay_param) * small[7]

    shape = (rows_here, steps, model_width)
    return (
        result.reshape(shape),
        stream_grad.reshape(shape),
        grad_branch,
        grad_gating,
        grad_output,
        grad_hgate,
        grad_hlinear,
        grad_houtput,
        grad_mgain.reshape(own_rows),
        grad_hgain.reshape(own_rows),
        grad_gblocks,
        small[:2],
        small[2:6],
        small[6],
        grad_decay,
    )


def solution(mesh):
    return jax.shard_map(
        local,
        mesh=mesh,
        in_specs=(
            P("batch", "seq", None),
            P("batch", "seq"),
            P("batch", "seq", None),
            P(("batch", "seq"), None),
            P(("batch", "seq"), None),
            P(("batch", "seq"), None),
            P(("batch", "seq"), None),
            P(("batch", "seq"), None),
            P(("batch", "seq"), None),
            P(("batch", "seq")),
            P(("batch", "seq")),
            P(),
            P(),
            P(),
            P(),
            P(),
        ),
        out_specs=(
            P("batch", "seq", None),
            P("batch", "seq", None),
            P(("batch", "seq"), None),
            P(("batch", "seq"), None),
            P(("batch", "seq"), None),
            P(("batch", "seq"), None),
            P(("batch", "seq"), None),
            P(("batch", "seq"), None),
            P(("batch", "seq")),
            P(("batch", "seq")),
            P(),
            P(),
            P(),
            P(),
            P(),
        ),
        check_vma=False,
    )
```

```python
import functools

import jax
import jax.numpy as jnp
from jax import lax
from jax.experimental import pallas as pl
from jax.experimental.pallas import tpu as pltpu
from jax.sharding import PartitionSpec as P

NBLK = 16
BLK = 171
NBIG = 10
KW = 4
R = 2730

EPSILON = 1e-06

GROUP = 8
AXES = ("batch", "seq")
PAD = 192
SMALL = 176
WIDE = 2 * PAD
SIZES = [BLK] * NBIG + [BLK - 1] * (NBLK - NBIG)
BEGINS = [sum(SIZES[:i]) for i in range(NBLK)]
ORDER = (0, 2, 4, 6, 1, 3, 5, 7)

BF16 = jnp.bfloat16
F32 = jnp.float32


def device_count():
    return lax.axis_size("batch") * lax.axis_size("seq")


def flat_index():
    return lax.axis_index("batch") * lax.axis_size("seq") + lax.axis_index("seq")


def swap(values, bit):
    return lax.ppermute(values, AXES, [(i, i ^ bit) for i in range(device_count())])


def onward(values, turns):
    count = device_count()
    pairs = [(i, (i + turns * GROUP) % count) for i in range(count)]
    return lax.ppermute(values, AXES, pairs)


def low(values):
    return values.astype(BF16)


def wide(values):
    return values.astype(F32)


def pick(values, index):
    return lax.dynamic_index_in_dim(values, index, 0, False)


def put(values, part, index):
    return lax.dynamic_update_index_in_dim(values, part, index, 0)


def after(values, *others):
    return lax.optimization_barrier((values,) + others)[0]


def ring_groups():
    count = device_count()
    return [list(range(i, count, GROUP)) for i in range(GROUP)]


def ring_gather(block):
    return lax.all_gather(block, AXES, axis=0, tiled=True, axis_index_groups=ring_groups())


def ring_reduce(values):
    return lax.psum_scatter(
        values, AXES, scatter_dimension=0, tiled=True, axis_index_groups=ring_groups()
    )


def ring_stack(block, turn, groups):
    out = jnp.broadcast_to(block, (groups,) + block.shape)
    for step in range(1, groups):
        out = put(out, onward(block, step), (turn + groups - step) % groups)
    return out


def ring_sum(values, turn, groups):
    chunks = values.reshape((groups, -1) + values.shape[1:])
    total = wide(pick(chunks, turn))
    for step in range(1, groups):
        total = total + wide(onward(pick(chunks, (turn + step) % groups), step))
    return low(total)


def exchange(pieces):
    count = device_count()
    sets = [list(range(i, i + GROUP)) for i in range(0, count, GROUP)]
    return lax.all_to_all(pieces, AXES, 0, 0, axis_index_groups=sets)


def all_swapped(parts):
    return [parts[0]] + [swap(parts[bit], bit) for bit in range(1, GROUP)]


def first_swaps(own):
    return swap(own, 4), swap(own, 2)


def group_parts(own, swapped=None):
    half = own.shape[0] // 2
    across, along = swapped or first_swaps(own)
    first, second = swap(across[:half], 2), swap(along[half:], 4)
    mine = [own, along, across, first, second]
    return mine + [swap(part, 1) for part in mine]


def group_gather(own):
    return jnp.concatenate(group_parts(own), axis=0)


def pair_total(near, far):
    near = near.reshape(4, -1, near.shape[-1])
    return near + wide(swap(low(far), 1)).reshape(near.shape)


def send_totals(total):
    half = total.shape[1] // 2
    return (
        swap(low(total[3, :half]), 4),
        swap(low(total[3, half:]), 2),
        swap(low(total[2, :half]), 4),
        swap(low(total[1, half:]), 2),
    )


def join_totals(total, arrived):
    first, second, across, along = arrived
    half = total.shape[1] // 2
    across_rest = swap(low(total[2, half:] + wide(second)), 4)
    along_rest = swap(low(total[1, :half] + wide(first)), 2)
    return (
        total[0]
        + wide(jnp.concatenate([across, across_rest], axis=0))
        + wide(jnp.concatenate([along_rest, along], axis=0))
    )


def group_total(total):
    return join_totals(total, send_totals(total))


def to_windows(values):
    leading = [(0, 0)] * (values.ndim - 1)
    parts = [
        jnp.pad(values[..., begin : begin + size], leading + [(0, PAD - size)])
        for begin, size in zip(BEGINS, SIZES)
    ]
    return jnp.concatenate(parts, axis=-1).reshape(values.shape[:-1] + (GROUP, WIDE))


def norm_kernel(values, gain, out):
    rows = wide(values[...])
    out[...] = low(rows * rms_scale(rows) * gain[...])


def norm_rows(values, gain, steps):
    rows, width = values.shape
    return pl.pallas_call(
        norm_kernel,
        grid=(rows // steps,),
        in_specs=[
            pl.BlockSpec((steps, width), lambda i: (i, 0)),
            pl.BlockSpec((1, width), lambda i: (0, 0)),
        ],
        out_specs=pl.BlockSpec((steps, width), lambda i: (i, 0)),
        out_shape=jax.ShapeDtypeStruct((rows, width), BF16),
        compiler_params=pltpu.CompilerParams(vmem_limit_bytes=48 * 1024 * 1024),
        cost_estimate=pl.CostEstimate(flops=1, bytes_accessed=1, transcendentals=0),
        name="norm_rows",
    )(values, gain)


SCALAR = pl.BlockSpec(memory_space=pltpu.SMEM)
BUFFER = pl.BlockSpec(memory_space=pltpu.VMEM)


def simple_call(kernel, name, place, arrays, outs, scratch=()):
    moved = sum(a.size * a.dtype.itemsize for a in arrays)
    return pl.pallas_call(
        kernel,
        in_specs=[SCALAR] + [BUFFER] * len(arrays),
        out_specs=[BUFFER] * len(outs),
        out_shape=[jax.ShapeDtypeStruct(shape, dtype) for shape, dtype in outs],
        scratch_shapes=list(scratch),
        compiler_params=pltpu.CompilerParams(vmem_limit_bytes=48 * 1024 * 1024),
        cost_estimate=pl.CostEstimate(flops=moved, bytes_accessed=2 * moved, transcendentals=0),
        name=name,
    )(place, *arrays)


def split_mixer_kernel(place, branch, gating, output, tiny, *rest):
    outs, held = rest[:GROUP], rest[GROUP]
    rows = branch.shape[0]
    held[...] = jnp.zeros_like(held)
    for slot, ref in enumerate((branch, gating, output)):
        values = wide(ref[...])
        for i in range(NBLK):
            begin = slot * WIDE + (i % 2) * PAD
            held[i // 2, :, begin : begin + SIZES[i]] = values[
                :, BEGINS[i] : BEGINS[i] + SIZES[i]
            ]
    for bit in range(GROUP):
        outs[bit][:rows] = low(held[place[0] ^ bit])
        outs[bit][rows:] = tiny[...]


def split_hidden_kernel(place, gate, linear, output, *outs):
    part = gate.shape[1] // GROUP
    for bit in range(GROUP):
        columns = pl.ds(pl.multiple_of((place[0] ^ bit) * part, 128), part)
        for slot, ref in enumerate((gate, linear, output)):
            outs[bit][:, slot * part : (slot + 1) * part] = ref[:, columns]


def collect_kernel(place, *refs):
    parts, (first, second) = refs[:GROUP], refs[GROUP:]
    cut = first.shape[2]
    for bit in range(GROUP):
        first[place[0] ^ bit] = parts[bit][:, :cut]
        second[place[0] ^ bit] = parts[bit][:, cut:]


def collect_mixer_kernel(place, *refs):
    parts, (columns, tiny) = refs[:GROUP], refs[GROUP:]
    rows = columns.shape[1]
    for bit in range(GROUP):
        columns[place[0] ^ bit] = parts[bit][:rows]
        tiny[place[0] ^ bit] = wide(parts[bit][rows:])[:1, : tiny.shape[2]]


def hidden_owner_kernel(place, gate, linear, gain, grads, *outs):
    part = gate.shape[1] // GROUP
    total = jnp.zeros((gate.shape[0], 1), F32)
    for device in range(GROUP):
        columns = slice(device * part, device * part + part)
        d_gate = wide(grads[device, :, :part])
        d_linear = wide(grads[device, :, part : 2 * part])
        outs[0][:, columns] = d_gate
        outs[1][:, columns] = d_linear
        outs[2][:, columns] = wide(grads[device, :, 2 * part :])
        terms = d_gate * wide(gate[:, columns]) + d_linear * wide(linear[:, columns])
        total = total + jnp.sum(terms, axis=1, keepdims=True)
    outs[3][...] = total / gain[...]


def mixer_owner_kernel(place, branch, gating, gain, both, last, *outs):
    for i in range(NBLK):
        columns = slice(BEGINS[i], BEGINS[i] + SIZES[i])
        begin = (i % 2) * PAD
        values = wide(both[i // 2])
        outs[0][:, columns] = values[:, begin : begin + SIZES[i]]
        outs[1][:, columns] = values[:, WIDE + begin : WIDE + begin + SIZES[i]]
        outs[2][:, columns] = wide(last[i // 2])[:, begin : begin + SIZES[i]]
    terms = outs[0][...] * wide(branch[...]) + outs[1][...] * wide(gating[...])
    outs[3][...] = jnp.sum(terms, axis=1, keepdims=True) / gain[...]


def gates_owner_kernel(place, *refs):
    parts, (blocks, small), held = refs[:GROUP], refs[GROUP : GROUP + 2], refs[-1]
    for part, bit in zip(parts, ORDER):
        device = place[0] ^ bit
        for gate in range(2):
            for block in range(2):
                begin = gate * WIDE + block * PAD
                blocks[gate, 2 * device + block] = wide(part[:BLK, begin : begin + BLK])
        ending = wide(part[SMALL:PAD])[:8]
        held[device] = ending[:, :WIDE] + ending[:, WIDE:]
    for i in range(NBLK):
        begin = (i % 2) * PAD
        small[:, BEGINS[i] : BEGINS[i] + SIZES[i]] = held[i // 2, :, begin : begin + SIZES[i]]


def rms_scale(values):
    return lax.rsqrt(jnp.mean(values * values, axis=-1, keepdims=True) + EPSILON)


def norm_back(values, scale, gain, grads):
    scaled = grads * gain
    return scale * (
        scaled - values * scale * scale * jnp.mean(scaled * values, axis=-1, keepdims=True)
    )


def product(left, right):
    return jnp.dot(left, right, preferred_element_type=F32)


def contract_rows(left, right):
    return lax.dot_general(left, right, (((0,), (0,)), ((), ())), preferred_element_type=F32)


def contract_cols(left, right):
    return lax.dot_general(left, right, (((1,), (1,)), ((), ())), preferred_element_type=F32)


def pair_product(left, right, first=None):
    half = left.shape[0] // 2
    far = low(contract_cols(left[half:], right))
    if first is None:
        return pair_total(contract_cols(left[:half], right), far)
    near, first = lax.optimization_barrier((left[:half], first))
    return pair_total(contract_cols(near, right), far), first


def sigmoid(values):
    return 1.0 / (1.0 + jnp.exp(-values))


GELU_A = 0.7978845608028654
GELU_B = 0.044715


def gelu_both(values):
    square = values * values
    bent = jnp.tanh(GELU_A * values * (1.0 + GELU_B * square))
    value = 0.5 * values * (1.0 + bent)
    slope = 0.5 * (1.0 + bent) + 0.5 * values * (1.0 - bent * bent) * GELU_A * (
        1.0 + 3.0 * GELU_B * square
    )
    return value, slope


def minus_expm1(values):
    series = 1.0 / 40320.0
    for divisor in (5040.0, 720.0, 120.0, 24.0, 6.0, 2.0, 1.0):
        series = series * values + 1.0 / divisor
    return -values * series


def repeated(values, width):
    return jnp.concatenate([values] * (width // 128), axis=1)


def gate_values(conv, fresh, weight, bias, rate):
    pre = product(low(conv), weight) + bias
    width = conv.shape[1]
    recur, enter = sigmoid(pre[:, :width]), sigmoid(pre[:, width:])
    log_decay = rate * recur
    decay = jnp.exp(log_decay)
    raw_scale = jnp.sqrt(minus_expm1(2.0 * log_decay))
    carry = jnp.where(fresh, 0.0, decay)
    scale = jnp.where(fresh, 1.0, raw_scale)
    return recur, enter, decay, raw_scale, carry, scale


def same_masks(numbers, steps, width):
    own = numbers[8 : 8 + steps]
    masks = [
        repeated(jnp.where(numbers[8 - k : 8 - k + steps] == own, 1.0, 0.0), width)
        for k in range(1, KW)
    ]
    return masks, masks[0] < 0.5


def convolve(padded, masks, params, steps):
    conv = params[6:7] + params[2:3] * padded[8 : 8 + steps]
    for offset in range(1, KW):
        conv = conv + params[2 + offset : 3 + offset] * (
            padded[8 - offset : 8 - offset + steps] * masks[offset - 1]
        )
    return conv


def forward_kernel(
    place,
    normed,
    segment,
    both_weight,
    weight,
    bias,
    params,
    pre,
    state_out,
    mixed_out,
    padded,
    mult,
    partial,
    chain,
    numbers,
):
    steps, width = padded.shape[0] - 8, padded.shape[1]
    chunk = steps // 8

    @pl.when(pl.program_id(1) == 0)
    def _():
        padded[0:8] = jnp.zeros((8, width), F32)
        numbers[0:8] = jnp.full((8, 128), -1.0, F32)
        chain[...] = jnp.zeros_like(chain)

    @pl.when(pl.program_id(1) > 0)
    def _():
        padded[0:8] = padded[steps : steps + 8]
        numbers[0:8] = numbers[steps : steps + 8]

    pre[0] = product(normed[0], both_weight[...])
    padded[8 : 8 + steps] = pre[0, :, :width]
    numbers[8 : 8 + steps] = segment[0]
    masks, fresh = same_masks(numbers, steps, width)
    conv = convolve(padded, masks, params, steps)
    recur, enter, decay, raw_scale, carry, scale = gate_values(
        conv, fresh, weight[...], bias[...], params[7:8]
    )
    for lane in range(width // 128):
        lanes = slice(lane * 128, lane * 128 + 128)
        mult[lane] = carry[:, lanes]
        partial[lane] = (scale * enter * conv)[:, lanes]
    for lane in range(width // 128):
        state = jnp.zeros((8, 128), F32)
        reach = jnp.ones((8, 128), F32)
        for step in range(chunk):
            rows = pl.ds(step, 8, stride=chunk)
            factor = mult[lane, rows, :]
            state = factor * state + partial[lane, rows, :]
            reach = factor * reach
            partial[lane, rows, :] = state
            mult[lane, rows, :] = reach
        lanes = slice(lane * 128, lane * 128 + 128)
        entering = chain[0:1, lanes]
        for part in range(8):
            rows = slice(part * chunk, part * chunk + chunk)
            state_out[0, rows, lanes] = partial[lane, rows, :] + mult[lane, rows, :] * entering
            entering = state[part : part + 1] + reach[part : part + 1] * entering
        chain[0:1, lanes] = entering
    value, _ = gelu_both(pre[0, :, width:])
    mixed_out[0] = low(state_out[0] * value)


def backward_kernel(
    place,
    pre,
    rim,
    segment,
    segment_rim,
    state,
    state_rim,
    middle,
    out_weight,
    weight,
    bias,
    params,
    d_both,
    packed,
    padded,
    mult,
    partial,
    adjoint_all,
    chain,
    later,
    numbers,
    grad_gate,
    grad_small,
):
    steps, width = padded.shape[0] - 8, padded.shape[1]
    chunk = steps // 8
    last = pl.program_id(1) == 0
    first = pl.program_id(1) == pl.num_programs(1) - 1

    @pl.when(last & (pl.program_id(0) == 0))
    def _():
        grad_gate[...] = jnp.zeros_like(grad_gate)
        grad_small[...] = jnp.zeros_like(grad_small)

    @pl.when(last)
    def _():
        chain[...] = jnp.zeros_like(chain)
        later[:, steps : steps + 8] = jnp.zeros((KW - 1, 8, width), F32)

    @pl.when(jnp.logical_not(last))
    def _():
        later[:, steps : steps + 8] = later[:, 0:8]

    padded[0:8] = rim[0]
    padded[8 : 8 + steps] = pre[0, :, :width]
    numbers[0:8] = jnp.where(first, -1.0, segment_rim[0])
    numbers[8 : 8 + steps] = segment[0]
    masks, fresh = same_masks(numbers, steps, width)
    conv = convolve(padded, masks, params, steps)
    recur, enter, decay, raw_scale, carry, scale = gate_values(
        conv, fresh, weight[...], bias[...], params[7:8]
    )
    value, slope = gelu_both(pre[0, :, width:])
    d_out = product(middle[0], out_weight[...])
    d_both[0, :, width:] = low(d_out * state[0] * slope)
    d_state = d_out * value
    for lane in range(width // 128):
        lanes = slice(lane * 128, lane * 128 + 128)
        mult[lane, 0:steps, :] = carry[:, lanes]
        mult[lane, steps : steps + 8, :] = jnp.ones((8, 128), F32)
        partial[lane] = d_state[:, lanes]
    for lane in range(width // 128):
        lanes = slice(lane * 128, lane * 128 + 128)
        first_mult = mult[lane, 0:1, :]
        total = jnp.zeros((8, 128), F32)
        reach = jnp.ones((8, 128), F32)
        for step in reversed(range(chunk)):
            rows = pl.ds(step, 8, stride=chunk)
            factor = mult[lane, pl.ds(step + 1, 8, stride=chunk), :]
            total = factor * total + partial[lane, rows, :]
            reach = factor * reach
            partial[lane, rows, :] = total
            mult[lane, pl.ds(step + 1, 8, stride=chunk), :] = reach
        entering = chain[0:1, lanes]
        for part in reversed(range(8)):
            begin = part * chunk
            adjoint_all[begin : begin + chunk, lanes] = (
                partial[lane, begin : begin + chunk, :]
                + mult[lane, begin + 1 : begin + 1 + chunk, :] * entering
            )
            entering = total[part : part + 1] + reach[part : part + 1] * entering
        chain[0:1, lanes] = first_mult * entering
    adjoint = adjoint_all[...]
    padded_state = jnp.concatenate([state_rim[0, 7:8], state[0, : steps - 1]], axis=0)
    d_scale = adjoint * enter * conv
    d_enter = adjoint * scale * conv
    d_log = jnp.where(
        fresh, 0.0, decay * (adjoint * padded_state - d_scale * decay / raw_scale)
    )
    d_recur_pre = d_log * params[7:8] * recur * (1.0 - recur)
    d_enter_pre = d_enter * enter * (1.0 - enter)
    d_pre = jnp.concatenate([d_recur_pre, d_enter_pre], axis=1)
    d_pre_low = low(d_pre)
    d_conv = adjoint * scale * enter + contract_cols(d_pre_low, weight[...])
    grad_gate[...] += contract_rows(low(conv), d_pre_low)
    sums = [
        jnp.sum(d_recur_pre, axis=0, keepdims=True),
        jnp.sum(d_enter_pre, axis=0, keepdims=True),
        jnp.sum(d_conv * padded[8 : 8 + steps], axis=0, keepdims=True),
    ]
    d_branch = d_conv * params[2:3]
    for offset in range(1, KW):
        masked = d_conv * masks[offset - 1]
        sums.append(
            jnp.sum(masked * padded[8 - offset : 8 - offset + steps], axis=0, keepdims=True)
        )
        later[offset - 1, 0:steps] = masked * params[2 + offset : 3 + offset]
        d_branch = d_branch + later[offset - 1, offset : offset + steps]
    sums.append(jnp.sum(d_conv, axis=0, keepdims=True))
    sums.append(jnp.sum(d_log * recur, axis=0, keepdims=True))
    for row, value_sum in enumerate(sums):
        grad_small[row : row + 1] += value_sum
    d_both[0, :, :width] = low(d_branch)

    @pl.when(first & (pl.program_id(0) == pl.num_programs(0) - 1))
    def _():
        side = lax.broadcasted_iota(jnp.int32, (PAD, 2 * width), 1) % width
        blocks = jnp.where(side < PAD, grad_gate[0:PAD], grad_gate[PAD : 2 * PAD])
        rest = grad_small[...] - wide(low(grad_small[...]))
        packed[...] = low(blocks)
        packed[SMALL:PAD] = low(
            jnp.concatenate([jnp.concatenate([grad_small[...], rest], axis=1), blocks[-8:]], axis=0)
        )


def mixer_calls(rows, shards, steps, channels, model):
    blocks = rows * shards

    def position(row, shard, place):
        offset = (row * shards + shard) ^ place
        return (offset // 2) + (offset % 2) * (GROUP // 2)

    def whole(*dims):
        return pl.BlockSpec(dims, lambda row, shard, place: (0,) * len(dims))

    params = pltpu.CompilerParams(
        dimension_semantics=("arbitrary", "arbitrary"), vmem_limit_bytes=48 * 1024 * 1024
    )
    lanes = channels // 128
    forward = pl.pallas_call(
        forward_kernel,
        grid_spec=pltpu.PrefetchScalarGridSpec(
            num_scalar_prefetch=1,
            grid=(rows, shards),
            in_specs=[
                pl.BlockSpec((1, steps, model), lambda r, s, p: (position(r, s, p[0]), 0, 0)),
                pl.BlockSpec((1, steps, 128), lambda r, s, p: (r * shards + s, 0, 0)),
                whole(model, 2 * channels),
                whole(channels, 2 * channels),
                whole(1, 2 * channels),
                whole(8, channels),
            ],
            out_specs=[
                pl.BlockSpec(
                    (1, steps, 2 * channels), lambda r, s, p: (position(r, s, p[0]), 0, 0)
                ),
                pl.BlockSpec((1, steps, channels), lambda r, s, p: (r * shards + s, 0, 0)),
                pl.BlockSpec((1, steps, channels), lambda r, s, p: (position(r, s, p[0]), 0, 0)),
            ],
            scratch_shapes=[
                pltpu.VMEM((steps + 8, channels), F32),
                pltpu.VMEM((lanes, steps, 128), F32),
                pltpu.VMEM((lanes, steps, 128), F32),
                pltpu.VMEM((8, channels), F32),
                pltpu.VMEM((steps + 8, 128), F32),
            ],
        ),
        out_shape=[
            jax.ShapeDtypeStruct((blocks, steps, 2 * channels), F32),
            jax.ShapeDtypeStruct((blocks, steps, channels), F32),
            jax.ShapeDtypeStruct((blocks, steps, channels), BF16),
        ],
        compiler_params=params,
        cost_estimate=pl.CostEstimate(flops=1, bytes_accessed=1, transcendentals=0),
        name="mixer_forward",
    )

    def turned(shard):
        return shards - 1 - shard

    def before(shard):
        return jnp.maximum(shards - 2 - shard, 0)

    backward = pl.pallas_call(
        backward_kernel,
        grid_spec=pltpu.PrefetchScalarGridSpec(
            num_scalar_prefetch=1,
            grid=(rows, shards),
            in_specs=[
                pl.BlockSpec(
                    (1, steps, 2 * channels), lambda r, s, p: (position(r, turned(s), p[0]), 0, 0)
                ),
                pl.BlockSpec(
                    (1, 8, channels),
                    lambda r, s, p: (position(r, before(s), p[0]), steps // 8 - 1, 0),
                ),
                pl.BlockSpec((1, steps, 128), lambda r, s, p: (r * shards + turned(s), 0, 0)),
                pl.BlockSpec(
                    (1, 8, 128), lambda r, s, p: (r * shards + before(s), steps // 8 - 1, 0)
                ),
                pl.BlockSpec((1, steps, channels), lambda r, s, p: (r * shards + turned(s), 0, 0)),
                pl.BlockSpec(
                    (1, 8, channels),
                    lambda r, s, p: (r * shards + before(s), steps // 8 - 1, 0),
                ),
                pl.BlockSpec(
                    (1, steps, model), lambda r, s, p: (position(r, turned(s), p[0]), 0, 0)
                ),
                pl.BlockSpec((model, channels), lambda r, s, p: (0, 2)),
                whole(channels, 2 * channels),
                whole(1, 2 * channels),
                whole(8, channels),
            ],
            out_specs=[
                pl.BlockSpec(
                    (1, steps, 2 * channels), lambda r, s, p: (position(r, turned(s), p[0]), 0, 0)
                ),
                whole(PAD, 2 * channels),
            ],
            scratch_shapes=[
                pltpu.VMEM((steps + 8, channels), F32),
                pltpu.VMEM((lanes, steps + 8, 128), F32),
                pltpu.VMEM((lanes, steps, 128), F32),
                pltpu.VMEM((steps, channels), F32),
                pltpu.VMEM((8, channels), F32),
                pltpu.VMEM((KW - 1, steps + 8, channels), F32),
                pltpu.VMEM((steps + 8, 128), F32),
                pltpu.VMEM((channels, 2 * channels), F32),
                pltpu.VMEM((8, channels), F32),
            ],
        ),
        out_shape=[
            jax.ShapeDtypeStruct((blocks, steps, 2 * channels), BF16),
            jax.ShapeDtypeStruct((PAD, 2 * channels), BF16),
        ],
        compiler_params=params,
        cost_estimate=pl.CostEstimate(
            flops=blocks * steps * channels * (channels * 12 + model * 2),
            bytes_accessed=blocks * steps * channels * 24,
            transcendentals=blocks * steps * channels * 8,
        ),
        name="mixer_backward",
    )
    return forward, backward


def local(
    stream_in,
    segment_ids,
    out_grad,
    branch_weight,
    gating_weight,
    output_weight,
    hidden_gate,
    hidden_linear,
    hidden_output,
    mixer_gain,
    hidden_gain,
    gate_blocks,
    gate_biases,
    conv_taps,
    conv_bias,
    decay_param,
):
    rows_here, steps, model_width = stream_in.shape
    shards = lax.axis_size("seq")
    rows = GROUP // shards
    assert rows_here == 1 and rows * shards == GROUP
    groups = device_count() // GROUP
    place = flat_index() % GROUP
    turn = flat_index() // GROUP
    own_rows, hidden_width = hidden_gate.shape
    hidden_part = hidden_width // GROUP
    tokens = GROUP * steps

    where = place.astype(jnp.int32).reshape(1)
    tiny = jnp.concatenate(
        [mixer_gain[None], hidden_gain[None], low(segment_ids)], axis=1
    )
    tiny_width = tiny.shape[1]
    mixer_parts = simple_call(
        split_mixer_kernel,
        "split_mixer",
        where,
        (
            branch_weight,
            gating_weight,
            output_weight,
            jnp.pad(tiny, ((0, 15), (0, 3 * WIDE - tiny_width))),
        ),
        [((own_rows + 16, 3 * WIDE), BF16)] * GROUP,
        [pltpu.VMEM((GROUP, own_rows, 3 * WIDE), F32)],
    )
    mixer_rows, tiny = simple_call(
        collect_mixer_kernel,
        "collect_mixer",
        where,
        all_swapped(mixer_parts),
        [
            ((GROUP, own_rows, 3 * WIDE), BF16),
            ((GROUP, 1, tiny_width), F32),
        ],
    )
    tiny = tiny.reshape(GROUP, tiny_width)
    mixer_weight = ring_gather(mixer_rows.reshape(-1, 3 * WIDE))
    both_weight, out_weight = mixer_weight[:, : 2 * WIDE], mixer_weight[:, 2 * WIDE :]
    gains = ring_stack(tiny[:, : 2 * own_rows], turn, groups)
    mixer_scale = gains[..., :own_rows].reshape(1, model_width)
    hidden_scale = gains[..., own_rows:].reshape(1, model_width)
    segments = jnp.broadcast_to(tiny[:, 2 * own_rows :, None], (GROUP, steps, 128))

    inputs = wide(stream_in).reshape(steps, model_width)
    inputs_scale = rms_scale(inputs)
    parts = group_parts(stream_in.reshape(steps, model_width))
    normed = norm_rows(jnp.concatenate(parts, axis=0), mixer_scale, steps)
    upstream = wide(out_grad).reshape(steps, model_width)
    hidden_parts = simple_call(
        split_hidden_kernel,
        "split_hidden",
        where,
        (hidden_gate, hidden_linear, hidden_output),
        [((own_rows, 3 * hidden_part), BF16)] * GROUP,
    )
    pair_rows, last_rows = simple_call(
        collect_kernel,
        "collect_hidden",
        where,
        all_swapped(lax.optimization_barrier((hidden_parts, parts[3:5]))[0]),
        [((GROUP, own_rows, 2 * hidden_part), BF16), ((GROUP, own_rows, hidden_part), BF16)],
    )
    pair_weight = ring_gather(pair_rows.reshape(-1, 2 * hidden_part))
    normed_blocks = after(normed, pair_rows).reshape(GROUP, steps, model_width)

    rate = -8.0 * jax.nn.softplus(-decay_param)
    params = jnp.concatenate(
        [gate_biases, conv_taps, conv_bias[None], rate[None]], axis=0
    )
    params = pick(jnp.swapaxes(to_windows(params), 0, 1), place)
    bias = params[:2].reshape(1, 2 * WIDE)
    params = params.at[7].set(jnp.where(params[7] == 0.0, -0.01, params[7]))
    blocks = lax.dynamic_slice_in_dim(gate_blocks, 2 * place, 2, 1)
    blocks = jnp.pad(blocks, ((0, 0), (0, 0), (0, PAD - BLK), (0, PAD - BLK)))
    empty = jnp.zeros((PAD, PAD), BF16)
    gate_weight = jnp.concatenate(
        [
            jnp.concatenate([blocks[0, 0], empty, blocks[1, 0], empty], axis=1),
            jnp.concatenate([empty, blocks[0, 1], empty, blocks[1, 1]], axis=1),
        ],
        axis=0,
    )
    mixer_forward, mixer_backward = mixer_calls(rows, shards, steps, WIDE, model_width)
    pre, state, mixed = mixer_forward(
        where, normed_blocks, segments, mixer_weight, gate_weight, bias, params
    )
    mixed = mixed.reshape(tokens, WIDE)
    last_weight = ring_gather(after(last_rows, mixed).reshape(-1, hidden_part))
    middle = inputs + group_total(pair_product(mixed, out_weight))

    middle_scale = rms_scale(middle)
    own = low(middle * middle_scale * hidden_scale)
    parts = group_parts(own, lax.optimization_barrier((first_swaps(own), pair_weight))[0])
    own = out_grad.reshape(steps, model_width)
    swapped = first_swaps(lax.optimization_barrier((own, parts[3:5]))[0])
    normed_mid = jnp.concatenate(parts, axis=0)
    upstream_all = jnp.concatenate(group_parts(own, swapped), axis=0)
    pair = product(normed_mid, pair_weight)
    gate_pre, linear_pre = pair[:, :hidden_part], pair[:, hidden_part:]
    value, slope = gelu_both(gate_pre)
    hidden, value, slope = lax.optimization_barrier(
        (low(value * linear_pre), value, linear_pre * slope)
    )
    grad_last_low = low(contract_rows(upstream_all, hidden))
    grad_last = ring_reduce(grad_last_low)
    half = tokens // 2
    hidden_far = low(contract_cols(after(hidden[half:], grad_last_low), last_weight))
    d_hidden = product(after(upstream_all, grad_last_low, hidden_far), last_weight)
    d_pair = jnp.concatenate(
        [low(d_hidden * slope), low(d_hidden * value)], axis=1
    )
    hidden_near = contract_cols(after(hidden[:half], d_pair), last_weight)
    hidden_out = pair_total(hidden_near, hidden_far)
    hidden_sent = send_totals(hidden_out)
    grad_pair_low = low(contract_rows(normed_mid, after(d_pair, hidden_out)))
    grad_pair = ring_reduce(grad_pair_low)
    d_pair, hidden_sent = lax.optimization_barrier((after(d_pair, grad_pair_low), hidden_sent))
    d_normed_mid, hidden_out = pair_product(
        d_pair, pair_weight, join_totals(hidden_out, hidden_sent)
    )
    result = low(middle + hidden_out)
    d_middle = upstream + norm_back(
        middle, middle_scale, hidden_scale, group_total(d_normed_mid)
    )

    def to_owner(grads):
        return exchange(grads.reshape(GROUP, own_rows, -1))

    own = after(low(d_middle), grad_last)
    middle_low = group_gather(own)
    grad_out_low = low(contract_rows(middle_low, mixed))
    grad_out = ring_reduce(grad_out_low)
    middle_blocks = after(middle_low, grad_out_low, grad_pair).reshape(GROUP, steps, model_width)
    hidden_grads = to_owner(jnp.concatenate([grad_pair, grad_last], axis=1))
    d_both, packed = mixer_backward(
        where,
        pre,
        pre,
        segments,
        segments,
        state,
        state,
        middle_blocks,
        mixer_weight,
        gate_weight,
        bias,
        params,
    )
    d_both = d_both.reshape(tokens, 2 * WIDE)
    grad_both_low = low(contract_rows(normed, after(d_both, grad_out, hidden_grads)))
    grad_both = ring_reduce(grad_both_low)
    packed = ring_sum(packed, turn, groups)
    d_normed, packed = pair_product(after(d_both, grad_both_low), both_weight, packed)
    d_normed = group_total(d_normed)
    stream_grad = low(d_middle + norm_back(inputs, inputs_scale, mixer_scale, d_normed))

    grad_hgate, grad_hlinear, grad_houtput, grad_hgain = simple_call(
        hidden_owner_kernel,
        "hidden_owner",
        where,
        (hidden_gate, hidden_linear, wide(hidden_gain)[:, None])
        + (hidden_grads,),
        [((own_rows, hidden_width), F32)] * 3 + [((own_rows, 1), F32)],
    )
    both_grads, out_grads = to_owner(grad_both), to_owner(grad_out)

    packed = ring_stack(packed, turn, groups).reshape(PAD, 2 * WIDE)
    packed, out_grads = lax.optimization_barrier((packed, out_grads))
    across, along = swap(packed, 4), swap(packed, 2)
    near = [packed, along, across, swap(across, 2)]
    near, both_grads = lax.optimization_barrier((near, both_grads))
    grad_gblocks, small = simple_call(
        gates_owner_kernel,
        "gates_owner",
        where,
        near + [swap(part, 1) for part in near],
        [((2, NBLK, BLK, BLK), F32), ((8, R), F32)],
        [pltpu.VMEM((GROUP, 8, WIDE), F32)],
    )
    grad_decay = 8.0 * jax.nn.sigmoid(-decay_param) * small[7]

    grad_branch, grad_gating, grad_output, grad_mgain = simple_call(
        mixer_owner_kernel,
        "mixer_owner",
        where,
        (branch_weight, gating_weight, wide(mixer_gain)[:, None])
        + (both_grads, out_grads),
        [((own_rows, R), F32)] * 3 + [((own_rows, 1), F32)],
    )

    shape = (rows_here, steps, model_width)
    return (
        result.reshape(shape),
        stream_grad.reshape(shape),
        grad_branch,
        grad_gating,
        grad_output,
        grad_hgate,
        grad_hlinear,
        grad_houtput,
        grad_mgain.reshape(own_rows),
        grad_hgain.reshape(own_rows),
        grad_gblocks,
        small[:2],
        small[2:6],
        small[6],
        grad_decay,
    )


def solution(mesh):
    return jax.shard_map(
        local,
        mesh=mesh,
        in_specs=(
            P("batch", "seq", None),
            P("batch", "seq"),
            P("batch", "seq", None),
            P(("batch", "seq"), None),
            P(("batch", "seq"), None),
            P(("batch", "seq"), None),
            P(("batch", "seq"), None),
            P(("batch", "seq"), None),
            P(("batch", "seq"), None),
            P(("batch", "seq")),
            P(("batch", "seq")),
            P(),
            P(),
            P(),
            P(),
            P(),
        ),
        out_specs=(
            P("batch", "seq", None),
            P("batch", "seq", None),
            P(("batch", "seq"), None),
            P(("batch", "seq"), None),
            P(("batch", "seq"), None),
            P(("batch", "seq"), None),
            P(("batch", "seq"), None),
            P(("batch", "seq"), None),
            P(("batch", "seq")),
            P(("batch", "seq")),
            P(),
            P(),
            P(),
            P(),
            P(),
        ),
        check_vma=False,
    )
```

```python
import functools

import jax
import jax.numpy as jnp
from jax import lax
from jax.experimental import pallas as pl
from jax.experimental.pallas import tpu as pltpu
from jax.sharding import PartitionSpec as P

NBLK = 16
BLK = 171
NBIG = 10
KW = 4
R = 2730

EPSILON = 1e-06

GROUP = 8
AXES = ("batch", "seq")
PAD = 192
SMALL = 176
WIDE = 2 * PAD
SIZES = [BLK] * NBIG + [BLK - 1] * (NBLK - NBIG)
BEGINS = [sum(SIZES[:i]) for i in range(NBLK)]
ORDER = (0, 2, 4, 6, 1, 3, 5, 7)

BF16 = jnp.bfloat16
F32 = jnp.float32


def device_count():
    return lax.axis_size("batch") * lax.axis_size("seq")


def flat_index():
    return lax.axis_index("batch") * lax.axis_size("seq") + lax.axis_index("seq")


def swap(values, bit):
    return lax.ppermute(values, AXES, [(i, i ^ bit) for i in range(device_count())])


def onward(values, turns):
    count = device_count()
    pairs = [(i, (i + turns * GROUP) % count) for i in range(count)]
    return lax.ppermute(values, AXES, pairs)


def low(values):
    return values.astype(BF16)


def wide(values):
    return values.astype(F32)


def pick(values, index):
    return lax.dynamic_index_in_dim(values, index, 0, False)


def put(values, part, index):
    return lax.dynamic_update_index_in_dim(values, part, index, 0)


def after(values, *others):
    return lax.optimization_barrier((values,) + others)[0]


def ring_groups():
    count = device_count()
    return [list(range(i, count, GROUP)) for i in range(GROUP)]


def ring_gather(block):
    return lax.all_gather(block, AXES, axis=0, tiled=True, axis_index_groups=ring_groups())


def ring_reduce(values):
    return lax.psum_scatter(
        values, AXES, scatter_dimension=0, tiled=True, axis_index_groups=ring_groups()
    )


def ring_stack(block, turn, groups):
    out = jnp.broadcast_to(block, (groups,) + block.shape)
    for step in range(1, groups):
        out = put(out, onward(block, step), (turn + groups - step) % groups)
    return out


def ring_sum(values, turn, groups):
    chunks = values.reshape((groups, -1) + values.shape[1:])
    total = wide(pick(chunks, turn))
    for step in range(1, groups):
        total = total + wide(onward(pick(chunks, (turn + step) % groups), step))
    return low(total)


def exchange(pieces):
    count = device_count()
    sets = [list(range(i, i + GROUP)) for i in range(0, count, GROUP)]
    return lax.all_to_all(pieces, AXES, 0, 0, axis_index_groups=sets)


def all_swapped(parts):
    return [parts[0]] + [swap(parts[bit], bit) for bit in range(1, GROUP)]


def first_swaps(own):
    return swap(own, 4), swap(own, 2)


def group_parts(own, swapped=None):
    half = own.shape[0] // 2
    across, along = swapped or first_swaps(own)
    first, second = swap(across[:half], 2), swap(along[half:], 4)
    mine = [own, along, across, first, second]
    return mine + [swap(part, 1) for part in mine]


def group_gather(own):
    return jnp.concatenate(group_parts(own), axis=0)


def pair_total(near, far):
    near = near.reshape(4, -1, near.shape[-1])
    return near + wide(swap(low(far), 1)).reshape(near.shape)


def send_totals(total):
    half = total.shape[1] // 2
    return (
        swap(low(total[3, :half]), 4),
        swap(low(total[3, half:]), 2),
        swap(low(total[2, :half]), 4),
        swap(low(total[1, half:]), 2),
    )


def rest_totals(total, arrived):
    first, second, across, along = arrived
    half = total.shape[1] // 2
    return low(total[2, half:] + wide(second)), low(total[1, :half] + wide(first))


def join_totals(total, arrived, rest=None):
    first, second, across, along = arrived
    across_rest, along_rest = rest or rest_totals(total, arrived)
    across_rest, along_rest = swap(across_rest, 4), swap(along_rest, 2)
    return (
        total[0]
        + wide(jnp.concatenate([across, across_rest], axis=0))
        + wide(jnp.concatenate([along_rest, along], axis=0))
    )


def group_total(total):
    return join_totals(total, send_totals(total))


def to_windows(values):
    leading = [(0, 0)] * (values.ndim - 1)
    parts = [
        jnp.pad(values[..., begin : begin + size], leading + [(0, PAD - size)])
        for begin, size in zip(BEGINS, SIZES)
    ]
    return jnp.concatenate(parts, axis=-1).reshape(values.shape[:-1] + (GROUP, WIDE))


def norm_kernel(values, gain, out):
    rows = wide(values[...])
    out[...] = low(rows * rms_scale(rows) * gain[...])


def norm_rows(values, gain, steps):
    rows, width = values.shape
    return pl.pallas_call(
        norm_kernel,
        grid=(rows // steps,),
        in_specs=[
            pl.BlockSpec((steps, width), lambda i: (i, 0)),
            pl.BlockSpec((1, width), lambda i: (0, 0)),
        ],
        out_specs=pl.BlockSpec((steps, width), lambda i: (i, 0)),
        out_shape=jax.ShapeDtypeStruct((rows, width), BF16),
        compiler_params=pltpu.CompilerParams(vmem_limit_bytes=48 * 1024 * 1024),
        cost_estimate=pl.CostEstimate(flops=1, bytes_accessed=1, transcendentals=0),
        name="norm_rows",
    )(values, gain)


SCALAR = pl.BlockSpec(memory_space=pltpu.SMEM)
BUFFER = pl.BlockSpec(memory_space=pltpu.VMEM)


def simple_call(kernel, name, place, arrays, outs, scratch=()):
    moved = sum(a.size * a.dtype.itemsize for a in arrays)
    return pl.pallas_call(
        kernel,
        in_specs=[SCALAR] + [BUFFER] * len(arrays),
        out_specs=[BUFFER] * len(outs),
        out_shape=[jax.ShapeDtypeStruct(shape, dtype) for shape, dtype in outs],
        scratch_shapes=list(scratch),
        compiler_params=pltpu.CompilerParams(vmem_limit_bytes=48 * 1024 * 1024),
        cost_estimate=pl.CostEstimate(flops=moved, bytes_accessed=2 * moved, transcendentals=0),
        name=name,
    )(place, *arrays)


def split_mixer_kernel(place, branch, gating, output, tiny, *rest):
    outs, held = rest[:GROUP], rest[GROUP]
    rows = branch.shape[0]
    held[...] = jnp.zeros_like(held)
    for slot, ref in enumerate((branch, gating, output)):
        values = wide(ref[...])
        for i in range(NBLK):
            begin = slot * WIDE + (i % 2) * PAD
            held[i // 2, :, begin : begin + SIZES[i]] = values[
                :, BEGINS[i] : BEGINS[i] + SIZES[i]
            ]
    for bit in range(GROUP):
        outs[bit][:rows] = low(held[place[0] ^ bit])
        outs[bit][rows:] = tiny[...]


def split_hidden_kernel(place, gate, linear, output, *outs):
    part = gate.shape[1] // GROUP
    for bit in range(GROUP):
        columns = pl.ds(pl.multiple_of((place[0] ^ bit) * part, 128), part)
        for slot, ref in enumerate((gate, linear, output)):
            outs[bit][:, slot * part : (slot + 1) * part] = ref[:, columns]


def collect_kernel(place, *refs):
    parts, (first, second) = refs[:GROUP], refs[GROUP:]
    cut = first.shape[2]
    for bit in range(GROUP):
        first[place[0] ^ bit] = parts[bit][:, :cut]
        second[place[0] ^ bit] = parts[bit][:, cut:]


def collect_mixer_kernel(place, *refs):
    parts, (columns, tiny) = refs[:GROUP], refs[GROUP:]
    rows = columns.shape[1]
    for bit in range(GROUP):
        columns[place[0] ^ bit] = parts[bit][:rows]
        tiny[place[0] ^ bit] = wide(parts[bit][rows:])[:1, : tiny.shape[2]]


def hidden_owner_kernel(place, gate, linear, gain, grads, *outs):
    part = gate.shape[1] // GROUP
    total = jnp.zeros((gate.shape[0], 1), F32)
    for device in range(GROUP):
        columns = slice(device * part, device * part + part)
        d_gate = wide(grads[device, :, :part])
        d_linear = wide(grads[device, :, part : 2 * part])
        outs[0][:, columns] = d_gate
        outs[1][:, columns] = d_linear
        outs[2][:, columns] = wide(grads[device, :, 2 * part :])
        terms = d_gate * wide(gate[:, columns]) + d_linear * wide(linear[:, columns])
        total = total + jnp.sum(terms, axis=1, keepdims=True)
    outs[3][...] = total / gain[...]


def mixer_owner_kernel(place, branch, gating, gain, both, last, *outs):
    for i in range(NBLK):
        columns = slice(BEGINS[i], BEGINS[i] + SIZES[i])
        begin = (i % 2) * PAD
        values = wide(both[i // 2])
        outs[0][:, columns] = values[:, begin : begin + SIZES[i]]
        outs[1][:, columns] = values[:, WIDE + begin : WIDE + begin + SIZES[i]]
        outs[2][:, columns] = wide(last[i // 2])[:, begin : begin + SIZES[i]]
    terms = outs[0][...] * wide(branch[...]) + outs[1][...] * wide(gating[...])
    outs[3][...] = jnp.sum(terms, axis=1, keepdims=True) / gain[...]


def gates_owner_kernel(place, *refs):
    parts, (blocks, small), held = refs[:GROUP], refs[GROUP : GROUP + 2], refs[-1]
    for part, bit in zip(parts, ORDER):
        device = place[0] ^ bit
        for gate in range(2):
            for block in range(2):
                begin = gate * WIDE + block * PAD
                blocks[gate, 2 * device + block] = wide(part[:BLK, begin : begin + BLK])
        ending = wide(part[SMALL:PAD])[:8]
        held[device] = ending[:, :WIDE] + ending[:, WIDE:]
    for i in range(NBLK):
        begin = (i % 2) * PAD
        small[:, BEGINS[i] : BEGINS[i] + SIZES[i]] = held[i // 2, :, begin : begin + SIZES[i]]


def rms_scale(values):
    return lax.rsqrt(jnp.mean(values * values, axis=-1, keepdims=True) + EPSILON)


def norm_back(values, scale, gain, grads):
    scaled = grads * gain
    return scale * (
        scaled - values * scale * scale * jnp.mean(scaled * values, axis=-1, keepdims=True)
    )


def product(left, right):
    return jnp.dot(left, right, preferred_element_type=F32)


def contract_rows(left, right):
    return lax.dot_general(left, right, (((0,), (0,)), ((), ())), preferred_element_type=F32)


def contract_cols(left, right):
    return lax.dot_general(left, right, (((1,), (1,)), ((), ())), preferred_element_type=F32)


def pair_product(left, right, first=None):
    half = left.shape[0] // 2
    far = low(contract_cols(left[half:], right))
    if first is None:
        return pair_total(contract_cols(left[:half], right), far)
    near, first = lax.optimization_barrier((left[:half], first))
    return pair_total(contract_cols(near, right), far), first


def sigmoid(values):
    return 1.0 / (1.0 + jnp.exp(-values))


GELU_A = 0.7978845608028654
GELU_B = 0.044715


def gelu_both(values):
    square = values * values
    bent = jnp.tanh(GELU_A * values * (1.0 + GELU_B * square))
    value = 0.5 * values * (1.0 + bent)
    slope = 0.5 * (1.0 + bent) + 0.5 * values * (1.0 - bent * bent) * GELU_A * (
        1.0 + 3.0 * GELU_B * square
    )
    return value, slope


def minus_expm1(values):
    series = 1.0 / 40320.0
    for divisor in (5040.0, 720.0, 120.0, 24.0, 6.0, 2.0, 1.0):
        series = series * values + 1.0 / divisor
    return -values * series


def repeated(values, width):
    return jnp.concatenate([values] * (width // 128), axis=1)


def gate_values(conv, fresh, weight, bias, rate):
    pre = product(low(conv), weight) + bias
    width = conv.shape[1]
    recur, enter = sigmoid(pre[:, :width]), sigmoid(pre[:, width:])
    log_decay = rate * recur
    decay = jnp.exp(log_decay)
    raw_scale = jnp.sqrt(minus_expm1(2.0 * log_decay))
    carry = jnp.where(fresh, 0.0, decay)
    scale = jnp.where(fresh, 1.0, raw_scale)
    return recur, enter, decay, raw_scale, carry, scale


def same_masks(numbers, steps, width):
    own = numbers[8 : 8 + steps]
    masks = [
        repeated(jnp.where(numbers[8 - k : 8 - k + steps] == own, 1.0, 0.0), width)
        for k in range(1, KW)
    ]
    return masks, masks[0] < 0.5


def convolve(padded, masks, params, steps):
    conv = params[6:7] + params[2:3] * padded[8 : 8 + steps]
    for offset in range(1, KW):
        conv = conv + params[2 + offset : 3 + offset] * (
            padded[8 - offset : 8 - offset + steps] * masks[offset - 1]
        )
    return conv


def forward_kernel(
    place,
    normed,
    segment,
    both_weight,
    weight,
    bias,
    params,
    pre,
    state_out,
    mixed_out,
    padded,
    mult,
    partial,
    chain,
    numbers,
):
    steps, width = padded.shape[0] - 8, padded.shape[1]
    chunk = steps // 8

    @pl.when(pl.program_id(1) == 0)
    def _():
        padded[0:8] = jnp.zeros((8, width), F32)
        numbers[0:8] = jnp.full((8, 128), -1.0, F32)
        chain[...] = jnp.zeros_like(chain)

    @pl.when(pl.program_id(1) > 0)
    def _():
        padded[0:8] = padded[steps : steps + 8]
        numbers[0:8] = numbers[steps : steps + 8]

    pre[0] = product(normed[0], both_weight[...])
    padded[8 : 8 + steps] = pre[0, :, :width]
    numbers[8 : 8 + steps] = segment[0]
    masks, fresh = same_masks(numbers, steps, width)
    conv = convolve(padded, masks, params, steps)
    recur, enter, decay, raw_scale, carry, scale = gate_values(
        conv, fresh, weight[...], bias[...], params[7:8]
    )
    for lane in range(width // 128):
        lanes = slice(lane * 128, lane * 128 + 128)
        mult[lane] = carry[:, lanes]
        partial[lane] = (scale * enter * conv)[:, lanes]
    for lane in range(width // 128):
        state = jnp.zeros((8, 128), F32)
        reach = jnp.ones((8, 128), F32)
        for step in range(chunk):
            rows = pl.ds(step, 8, stride=chunk)
            factor = mult[lane, rows, :]
            state = factor * state + partial[lane, rows, :]
            reach = factor * reach
            partial[lane, rows, :] = state
            mult[lane, rows, :] = reach
        lanes = slice(lane * 128, lane * 128 + 128)
        entering = chain[0:1, lanes]
        for part in range(8):
            rows = slice(part * chunk, part * chunk + chunk)
            state_out[0, rows, lanes] = partial[lane, rows, :] + mult[lane, rows, :] * entering
            entering = state[part : part + 1] + reach[part : part + 1] * entering
        chain[0:1, lanes] = entering
    value, _ = gelu_both(pre[0, :, width:])
    mixed_out[0] = low(state_out[0] * value)


def backward_kernel(
    place,
    pre,
    rim,
    segment,
    segment_rim,
    state,
    state_rim,
    middle,
    out_weight,
    weight,
    bias,
    params,
    d_both,
    packed,
    padded,
    mult,
    partial,
    adjoint_all,
    chain,
    later,
    numbers,
    grad_gate,
    grad_small,
):
    steps, width = padded.shape[0] - 8, padded.shape[1]
    chunk = steps // 8
    last = pl.program_id(1) == 0
    first = pl.program_id(1) == pl.num_programs(1) - 1

    @pl.when(last & (pl.program_id(0) == 0))
    def _():
        grad_gate[...] = jnp.zeros_like(grad_gate)
        grad_small[...] = jnp.zeros_like(grad_small)

    @pl.when(last)
    def _():
        chain[...] = jnp.zeros_like(chain)
        later[:, steps : steps + 8] = jnp.zeros((KW - 1, 8, width), F32)

    @pl.when(jnp.logical_not(last))
    def _():
        later[:, steps : steps + 8] = later[:, 0:8]

    padded[0:8] = rim[0]
    padded[8 : 8 + steps] = pre[0, :, :width]
    numbers[0:8] = jnp.where(first, -1.0, segment_rim[0])
    numbers[8 : 8 + steps] = segment[0]
    masks, fresh = same_masks(numbers, steps, width)
    conv = convolve(padded, masks, params, steps)
    recur, enter, decay, raw_scale, carry, scale = gate_values(
        conv, fresh, weight[...], bias[...], params[7:8]
    )
    value, slope = gelu_both(pre[0, :, width:])
    d_out = product(middle[0], out_weight[...])
    d_both[0, :, width:] = low(d_out * state[0] * slope)
    d_state = d_out * value
    for lane in range(width // 128):
        lanes = slice(lane * 128, lane * 128 + 128)
        mult[lane, 0:steps, :] = carry[:, lanes]
        mult[lane, steps : steps + 8, :] = jnp.ones((8, 128), F32)
        partial[lane] = d_state[:, lanes]
    for lane in range(width // 128):
        lanes = slice(lane * 128, lane * 128 + 128)
        first_mult = mult[lane, 0:1, :]
        total = jnp.zeros((8, 128), F32)
        reach = jnp.ones((8, 128), F32)
        for step in reversed(range(chunk)):
            rows = pl.ds(step, 8, stride=chunk)
            factor = mult[lane, pl.ds(step + 1, 8, stride=chunk), :]
            total = factor * total + partial[lane, rows, :]
            reach = factor * reach
            partial[lane, rows, :] = total
            mult[lane, pl.ds(step + 1, 8, stride=chunk), :] = reach
        entering = chain[0:1, lanes]
        for part in reversed(range(8)):
            begin = part * chunk
            adjoint_all[begin : begin + chunk, lanes] = (
                partial[lane, begin : begin + chunk, :]
                + mult[lane, begin + 1 : begin + 1 + chunk, :] * entering
            )
            entering = total[part : part + 1] + reach[part : part + 1] * entering
        chain[0:1, lanes] = first_mult * entering
    adjoint = adjoint_all[...]
    padded_state = jnp.concatenate([state_rim[0, 7:8], state[0, : steps - 1]], axis=0)
    d_scale = adjoint * enter * conv
    d_enter = adjoint * scale * conv
    d_log = jnp.where(
        fresh, 0.0, decay * (adjoint * padded_state - d_scale * decay / raw_scale)
    )
    d_recur_pre = d_log * params[7:8] * recur * (1.0 - recur)
    d_enter_pre = d_enter * enter * (1.0 - enter)
    d_pre = jnp.concatenate([d_recur_pre, d_enter_pre], axis=1)
    d_pre_low = low(d_pre)
    d_conv = adjoint * scale * enter + contract_cols(d_pre_low, weight[...])
    grad_gate[...] += contract_rows(low(conv), d_pre_low)
    sums = [
        jnp.sum(d_recur_pre, axis=0, keepdims=True),
        jnp.sum(d_enter_pre, axis=0, keepdims=True),
        jnp.sum(d_conv * padded[8 : 8 + steps], axis=0, keepdims=True),
    ]
    d_branch = d_conv * params[2:3]
    for offset in range(1, KW):
        masked = d_conv * masks[offset - 1]
        sums.append(
            jnp.sum(masked * padded[8 - offset : 8 - offset + steps], axis=0, keepdims=True)
        )
        later[offset - 1, 0:steps] = masked * params[2 + offset : 3 + offset]
        d_branch = d_branch + later[offset - 1, offset : offset + steps]
    sums.append(jnp.sum(d_conv, axis=0, keepdims=True))
    sums.append(jnp.sum(d_log * recur, axis=0, keepdims=True))
    for row, value_sum in enumerate(sums):
        grad_small[row : row + 1] += value_sum
    d_both[0, :, :width] = low(d_branch)

    @pl.when(first & (pl.program_id(0) == pl.num_programs(0) - 1))
    def _():
        side = lax.broadcasted_iota(jnp.int32, (PAD, 2 * width), 1) % width
        blocks = jnp.where(side < PAD, grad_gate[0:PAD], grad_gate[PAD : 2 * PAD])
        rest = grad_small[...] - wide(low(grad_small[...]))
        packed[...] = low(blocks)
        packed[SMALL:PAD] = low(
            jnp.concatenate([jnp.concatenate([grad_small[...], rest], axis=1), blocks[-8:]], axis=0)
        )


def mixer_calls(rows, shards, steps, channels, model):
    blocks = rows * shards

    def position(row, shard, place):
        offset = (row * shards + shard) ^ place
        return (offset // 2) + (offset % 2) * (GROUP // 2)

    def whole(*dims):
        return pl.BlockSpec(dims, lambda row, shard, place: (0,) * len(dims))

    params = pltpu.CompilerParams(
        dimension_semantics=("arbitrary", "arbitrary"), vmem_limit_bytes=48 * 1024 * 1024
    )
    lanes = channels // 128
    forward = pl.pallas_call(
        forward_kernel,
        grid_spec=pltpu.PrefetchScalarGridSpec(
            num_scalar_prefetch=1,
            grid=(rows, shards),
            in_specs=[
                pl.BlockSpec((1, steps, model), lambda r, s, p: (position(r, s, p[0]), 0, 0)),
                pl.BlockSpec((1, steps, 128), lambda r, s, p: (r * shards + s, 0, 0)),
                whole(model, 2 * channels),
                whole(channels, 2 * channels),
                whole(1, 2 * channels),
                whole(8, channels),
            ],
            out_specs=[
                pl.BlockSpec(
                    (1, steps, 2 * channels), lambda r, s, p: (position(r, s, p[0]), 0, 0)
                ),
                pl.BlockSpec((1, steps, channels), lambda r, s, p: (r * shards + s, 0, 0)),
                pl.BlockSpec((1, steps, channels), lambda r, s, p: (position(r, s, p[0]), 0, 0)),
            ],
            scratch_shapes=[
                pltpu.VMEM((steps + 8, channels), F32),
                pltpu.VMEM((lanes, steps, 128), F32),
                pltpu.VMEM((lanes, steps, 128), F32),
                pltpu.VMEM((8, channels), F32),
                pltpu.VMEM((steps + 8, 128), F32),
            ],
        ),
        out_shape=[
            jax.ShapeDtypeStruct((blocks, steps, 2 * channels), F32),
            jax.ShapeDtypeStruct((blocks, steps, channels), F32),
            jax.ShapeDtypeStruct((blocks, steps, channels), BF16),
        ],
        compiler_params=params,
        cost_estimate=pl.CostEstimate(
            flops=blocks * steps * channels * (channels * 4 + model * 4),
            bytes_accessed=blocks * steps * channels * 14,
            transcendentals=blocks * steps * channels * 6,
        ),
        name="mixer_forward",
    )

    def turned(shard):
        return shards - 1 - shard

    def before(shard):
        return jnp.maximum(shards - 2 - shard, 0)

    backward = pl.pallas_call(
        backward_kernel,
        grid_spec=pltpu.PrefetchScalarGridSpec(
            num_scalar_prefetch=1,
            grid=(rows, shards),
            in_specs=[
                pl.BlockSpec(
                    (1, steps, 2 * channels), lambda r, s, p: (position(r, turned(s), p[0]), 0, 0)
                ),
                pl.BlockSpec(
                    (1, 8, channels),
                    lambda r, s, p: (position(r, before(s), p[0]), steps // 8 - 1, 0),
                ),
                pl.BlockSpec((1, steps, 128), lambda r, s, p: (r * shards + turned(s), 0, 0)),
                pl.BlockSpec(
                    (1, 8, 128), lambda r, s, p: (r * shards + before(s), steps // 8 - 1, 0)
                ),
                pl.BlockSpec((1, steps, channels), lambda r, s, p: (r * shards + turned(s), 0, 0)),
                pl.BlockSpec(
                    (1, 8, channels),
                    lambda r, s, p: (r * shards + before(s), steps // 8 - 1, 0),
                ),
                pl.BlockSpec(
                    (1, steps, model), lambda r, s, p: (position(r, turned(s), p[0]), 0, 0)
                ),
                pl.BlockSpec((model, channels), lambda r, s, p: (0, 2)),
                whole(channels, 2 * channels),
                whole(1, 2 * channels),
                whole(8, channels),
            ],
            out_specs=[
                pl.BlockSpec(
                    (1, steps, 2 * channels), lambda r, s, p: (position(r, turned(s), p[0]), 0, 0)
                ),
                whole(PAD, 2 * channels),
            ],
            scratch_shapes=[
                pltpu.VMEM((steps + 8, channels), F32),
                pltpu.VMEM((lanes, steps + 8, 128), F32),
                pltpu.VMEM((lanes, steps, 128), F32),
                pltpu.VMEM((steps, channels), F32),
                pltpu.VMEM((8, channels), F32),
                pltpu.VMEM((KW - 1, steps + 8, channels), F32),
                pltpu.VMEM((steps + 8, 128), F32),
                pltpu.VMEM((channels, 2 * channels), F32),
                pltpu.VMEM((8, channels), F32),
            ],
        ),
        out_shape=[
            jax.ShapeDtypeStruct((blocks, steps, 2 * channels), BF16),
            jax.ShapeDtypeStruct((PAD, 2 * channels), BF16),
        ],
        compiler_params=params,
        cost_estimate=pl.CostEstimate(
            flops=blocks * steps * channels * (channels * 12 + model * 2),
            bytes_accessed=blocks * steps * channels * 24,
            transcendentals=blocks * steps * channels * 8,
        ),
        name="mixer_backward",
    )
    return forward, backward


def local(
    stream_in,
    segment_ids,
    out_grad,
    branch_weight,
    gating_weight,
    output_weight,
    hidden_gate,
    hidden_linear,
    hidden_output,
    mixer_gain,
    hidden_gain,
    gate_blocks,
    gate_biases,
    conv_taps,
    conv_bias,
    decay_param,
):
    rows_here, steps, model_width = stream_in.shape
    shards = lax.axis_size("seq")
    rows = GROUP // shards
    assert rows_here == 1 and rows * shards == GROUP
    groups = device_count() // GROUP
    place = flat_index() % GROUP
    turn = flat_index() // GROUP
    own_rows, hidden_width = hidden_gate.shape
    hidden_part = hidden_width // GROUP
    tokens = GROUP * steps

    where = place.astype(jnp.int32).reshape(1)
    tiny = jnp.concatenate(
        [mixer_gain[None], hidden_gain[None], low(segment_ids)], axis=1
    )
    tiny_width = tiny.shape[1]
    mixer_parts = simple_call(
        split_mixer_kernel,
        "split_mixer",
        where,
        (
            branch_weight,
            gating_weight,
            output_weight,
            jnp.pad(tiny, ((0, 15), (0, 3 * WIDE - tiny_width))),
        ),
        [((own_rows + 16, 3 * WIDE), BF16)] * GROUP,
        [pltpu.VMEM((GROUP, own_rows, 3 * WIDE), F32)],
    )
    mixer_rows, tiny = simple_call(
        collect_mixer_kernel,
        "collect_mixer",
        where,
        all_swapped(mixer_parts),
        [
            ((GROUP, own_rows, 3 * WIDE), BF16),
            ((GROUP, 1, tiny_width), F32),
        ],
    )
    tiny = tiny.reshape(GROUP, tiny_width)
    mixer_weight = ring_gather(mixer_rows.reshape(-1, 3 * WIDE))
    both_weight, out_weight = mixer_weight[:, : 2 * WIDE], mixer_weight[:, 2 * WIDE :]
    gains = ring_stack(tiny[:, : 2 * own_rows], turn, groups)
    mixer_scale = gains[..., :own_rows].reshape(1, model_width)
    hidden_scale = gains[..., own_rows:].reshape(1, model_width)
    segments = jnp.broadcast_to(tiny[:, 2 * own_rows :, None], (GROUP, steps, 128))

    inputs = wide(stream_in).reshape(steps, model_width)
    inputs_scale = rms_scale(inputs)
    parts = group_parts(stream_in.reshape(steps, model_width))
    raw = jnp.concatenate(parts, axis=0)
    normed = norm_rows(raw, mixer_scale, steps)
    upstream = wide(out_grad).reshape(steps, model_width)
    hidden_parts = simple_call(
        split_hidden_kernel,
        "split_hidden",
        where,
        (hidden_gate, hidden_linear, hidden_output),
        [((own_rows, 3 * hidden_part), BF16)] * GROUP,
    )
    pair_rows, last_rows = simple_call(
        collect_kernel,
        "collect_hidden",
        where,
        lax.optimization_barrier(
            (
                all_swapped(lax.optimization_barrier((hidden_parts, parts[3:5]))[0]),
                (raw, mixer_scale),
            )
        )[0],
        [((GROUP, own_rows, 2 * hidden_part), BF16), ((GROUP, own_rows, hidden_part), BF16)],
    )
    pair_weight = ring_gather(pair_rows.reshape(-1, 2 * hidden_part))
    normed_blocks = after(normed, pair_rows).reshape(GROUP, steps, model_width)

    rate = -8.0 * jax.nn.softplus(-decay_param)
    params = jnp.concatenate(
        [gate_biases, conv_taps, conv_bias[None], rate[None]], axis=0
    )
    params = pick(jnp.swapaxes(to_windows(params), 0, 1), place)
    bias = params[:2].reshape(1, 2 * WIDE)
    params = params.at[7].set(jnp.where(params[7] == 0.0, -0.01, params[7]))
    blocks = lax.dynamic_slice_in_dim(gate_blocks, 2 * place, 2, 1)
    blocks = jnp.pad(blocks, ((0, 0), (0, 0), (0, PAD - BLK), (0, PAD - BLK)))
    empty = jnp.zeros((PAD, PAD), BF16)
    gate_weight = jnp.concatenate(
        [
            jnp.concatenate([blocks[0, 0], empty, blocks[1, 0], empty], axis=1),
            jnp.concatenate([empty, blocks[0, 1], empty, blocks[1, 1]], axis=1),
        ],
        axis=0,
    )
    mixer_forward, mixer_backward = mixer_calls(rows, shards, steps, WIDE, model_width)
    own = after(out_grad.reshape(steps, model_width), normed)
    swapped = first_swaps(own)
    pre, state, mixed = mixer_forward(
        where, normed_blocks, segments, mixer_weight, gate_weight, bias, params
    )
    mixed, swapped = lax.optimization_barrier((mixed.reshape(tokens, WIDE), swapped))
    upstream_parts = group_parts(own, swapped)
    last_weight = ring_gather(after(last_rows, mixed).reshape(-1, hidden_part))
    middle = inputs + group_total(pair_product(mixed, out_weight))

    middle_scale = rms_scale(middle)
    own = low(middle * middle_scale * hidden_scale)
    parts = group_parts(own, lax.optimization_barrier((first_swaps(own), pair_weight))[0])
    normed_mid = jnp.concatenate(parts, axis=0)
    upstream_all = jnp.concatenate(upstream_parts, axis=0)
    pair = product(normed_mid, pair_weight)
    gate_pre, linear_pre = pair[:, :hidden_part], pair[:, hidden_part:]
    value, slope = gelu_both(gate_pre)
    hidden, value, slope = lax.optimization_barrier(
        (low(value * linear_pre), value, linear_pre * slope)
    )
    grad_last_low = low(contract_rows(upstream_all, hidden))
    grad_last = ring_reduce(grad_last_low)
    half = tokens // 2
    hidden_far = low(contract_cols(after(hidden[half:], grad_last_low), last_weight))
    d_hidden = product(after(upstream_all, grad_last_low, hidden_far), last_weight)
    d_pair = jnp.concatenate(
        [low(d_hidden * slope), low(d_hidden * value)], axis=1
    )
    hidden_near = contract_cols(after(hidden[:half], d_pair), last_weight)
    hidden_out = pair_total(hidden_near, hidden_far)
    hidden_sent = send_totals(hidden_out)
    grad_pair_low = low(contract_rows(normed_mid, after(d_pair, hidden_out)))
    grad_pair = ring_reduce(grad_pair_low)
    hidden_rest = rest_totals(hidden_out, hidden_sent)
    d_pair, hidden_rest, hidden_sent = lax.optimization_barrier(
        (after(d_pair, grad_pair_low), hidden_rest, hidden_sent)
    )
    d_normed_mid, hidden_out = pair_product(
        d_pair, pair_weight, join_totals(hidden_out, hidden_sent, hidden_rest)
    )
    result = low(middle + hidden_out)
    d_middle = upstream + norm_back(
        middle, middle_scale, hidden_scale, group_total(d_normed_mid)
    )

    def to_owner(grads):
        return exchange(grads.reshape(GROUP, own_rows, -1))

    own = after(low(d_middle), grad_last)
    middle_low = group_gather(own)
    grad_out_low = low(contract_rows(middle_low, mixed))
    grad_out = ring_reduce(grad_out_low)
    middle_blocks = after(middle_low, grad_out_low, grad_pair).reshape(GROUP, steps, model_width)
    hidden_grads = to_owner(jnp.concatenate([grad_pair, grad_last], axis=1))
    d_both, packed = mixer_backward(
        where,
        pre,
        pre,
        segments,
        segments,
        state,
        state,
        middle_blocks,
        mixer_weight,
        gate_weight,
        bias,
        params,
    )
    d_both = d_both.reshape(tokens, 2 * WIDE)
    grad_both_low = low(contract_rows(normed, after(d_both, grad_out, hidden_grads)))
    grad_both = ring_reduce(grad_both_low)
    packed = ring_sum(packed, turn, groups)
    d_normed, packed = pair_product(after(d_both, grad_both_low), both_weight, packed)
    d_normed = group_total(d_normed)
    stream_grad = low(d_middle + norm_back(inputs, inputs_scale, mixer_scale, d_normed))

    grad_hgate, grad_hlinear, grad_houtput, grad_hgain = simple_call(
        hidden_owner_kernel,
        "hidden_owner",
        where,
        (hidden_gate, hidden_linear, wide(hidden_gain)[:, None])
        + (hidden_grads,),
        [((own_rows, hidden_width), F32)] * 3 + [((own_rows, 1), F32)],
    )
    both_grads, out_grads = to_owner(grad_both), to_owner(grad_out)

    packed = ring_stack(packed, turn, groups).reshape(PAD, 2 * WIDE)
    packed, out_grads = lax.optimization_barrier((packed, out_grads))
    across, along = swap(packed, 4), swap(packed, 2)
    near = [packed, along, across, swap(across, 2)]
    near, both_grads = lax.optimization_barrier((near, both_grads))
    grad_gblocks, small = simple_call(
        gates_owner_kernel,
        "gates_owner",
        where,
        near + [swap(part, 1) for part in near],
        [((2, NBLK, BLK, BLK), F32), ((8, R), F32)],
        [pltpu.VMEM((GROUP, 8, WIDE), F32)],
    )
    grad_decay = 8.0 * jax.nn.sigmoid(-decay_param) * small[7]

    grad_branch, grad_gating, grad_output, grad_mgain = simple_call(
        mixer_owner_kernel,
        "mixer_owner",
        where,
        (branch_weight, gating_weight, wide(mixer_gain)[:, None])
        + (both_grads, out_grads),
        [((own_rows, R), F32)] * 3 + [((own_rows, 1), F32)],
    )

    shape = (rows_here, steps, model_width)
    return (
        result.reshape(shape),
        stream_grad.reshape(shape),
        grad_branch,
        grad_gating,
        grad_output,
        grad_hgate,
        grad_hlinear,
        grad_houtput,
        grad_mgain.reshape(own_rows),
        grad_hgain.reshape(own_rows),
        grad_gblocks,
        small[:2],
        small[2:6],
        small[6],
        grad_decay,
    )


def solution(mesh):
    return jax.shard_map(
        local,
        mesh=mesh,
        in_specs=(
            P("batch", "seq", None),
            P("batch", "seq"),
            P("batch", "seq", None),
            P(("batch", "seq"), None),
            P(("batch", "seq"), None),
            P(("batch", "seq"), None),
            P(("batch", "seq"), None),
            P(("batch", "seq"), None),
            P(("batch", "seq"), None),
            P(("batch", "seq")),
            P(("batch", "seq")),
            P(),
            P(),
            P(),
            P(),
            P(),
        ),
        out_specs=(
            P("batch", "seq", None),
            P("batch", "seq", None),
            P(("batch", "seq"), None),
            P(("batch", "seq"), None),
            P(("batch", "seq"), None),
            P(("batch", "seq"), None),
            P(("batch", "seq"), None),
            P(("batch", "seq"), None),
            P(("batch", "seq")),
            P(("batch", "seq")),
            P(),
            P(),
            P(),
            P(),
            P(),
        ),
        check_vma=False,
    )
```

```python
import functools

import jax
import jax.numpy as jnp
from jax import lax
from jax.experimental import pallas as pl
from jax.experimental.pallas import tpu as pltpu
from jax.sharding import PartitionSpec as P

NBLK = 16
BLK = 171
NBIG = 10
KW = 4
R = 2730

EPSILON = 1e-06

GROUP = 8
AXES = ("batch", "seq")
PAD = 192
SMALL = 176
WIDE = 2 * PAD
SIZES = [BLK] * NBIG + [BLK - 1] * (NBLK - NBIG)
BEGINS = [sum(SIZES[:i]) for i in range(NBLK)]
ORDER = (0, 2, 4, 6, 1, 3, 5, 7)

BF16 = jnp.bfloat16
F32 = jnp.float32


def device_count():
    return lax.axis_size("batch") * lax.axis_size("seq")


def flat_index():
    return lax.axis_index("batch") * lax.axis_size("seq") + lax.axis_index("seq")


def swap(values, bit):
    return lax.ppermute(values, AXES, [(i, i ^ bit) for i in range(device_count())])


def onward(values, turns):
    count = device_count()
    pairs = [(i, (i + turns * GROUP) % count) for i in range(count)]
    return lax.ppermute(values, AXES, pairs)


def low(values):
    return values.astype(BF16)


def wide(values):
    return values.astype(F32)


def pick(values, index):
    return lax.dynamic_index_in_dim(values, index, 0, False)


def put(values, part, index):
    return lax.dynamic_update_index_in_dim(values, part, index, 0)


def after(values, *others):
    return lax.optimization_barrier((values,) + others)[0]


def ring_groups():
    count = device_count()
    return [list(range(i, count, GROUP)) for i in range(GROUP)]


def ring_gather(block):
    return lax.all_gather(block, AXES, axis=0, tiled=True, axis_index_groups=ring_groups())


def ring_reduce(values):
    return lax.psum_scatter(
        values, AXES, scatter_dimension=0, tiled=True, axis_index_groups=ring_groups()
    )


def ring_stack(block, turn, groups):
    out = jnp.broadcast_to(block, (groups,) + block.shape)
    for step in range(1, groups):
        out = put(out, onward(block, step), (turn + groups - step) % groups)
    return out


def ring_sum(values, turn, groups):
    chunks = values.reshape((groups, -1) + values.shape[1:])
    total = wide(pick(chunks, turn))
    for step in range(1, groups):
        total = total + wide(onward(pick(chunks, (turn + step) % groups), step))
    return low(total)


def exchange(pieces):
    count = device_count()
    sets = [list(range(i, i + GROUP)) for i in range(0, count, GROUP)]
    return lax.all_to_all(pieces, AXES, 0, 0, axis_index_groups=sets)


def all_swapped(parts):
    return [parts[0]] + [swap(parts[bit], bit) for bit in range(1, GROUP)]


def first_swaps(own):
    return swap(own, 4), swap(own, 2)


def group_parts(own, swapped=None):
    half = own.shape[0] // 2
    across, along = swapped or first_swaps(own)
    first, second = swap(across[:half], 2), swap(along[half:], 4)
    mine = [own, along, across, first, second]
    return mine + [swap(part, 1) for part in mine]


def group_gather(own):
    return jnp.concatenate(group_parts(own), axis=0)


def pair_total(near, far):
    near = near.reshape(4, -1, near.shape[-1])
    return near + wide(swap(low(far), 1)).reshape(near.shape)


def send_totals(total):
    half = total.shape[1] // 2
    return (
        swap(low(total[3, :half]), 4),
        swap(low(total[3, half:]), 2),
        swap(low(total[2, :half]), 4),
        swap(low(total[1, half:]), 2),
    )


def rest_totals(total, arrived):
    first, second, across, along = arrived
    half = total.shape[1] // 2
    return low(total[2, half:] + wide(second)), low(total[1, :half] + wide(first))


def join_totals(total, arrived, rest=None):
    first, second, across, along = arrived
    across_rest, along_rest = rest or rest_totals(total, arrived)
    across_rest, along_rest = swap(across_rest, 4), swap(along_rest, 2)
    return (
        total[0]
        + wide(jnp.concatenate([across, across_rest], axis=0))
        + wide(jnp.concatenate([along_rest, along], axis=0))
    )


def group_total(total):
    return join_totals(total, send_totals(total))


def to_windows(values):
    leading = [(0, 0)] * (values.ndim - 1)
    parts = [
        jnp.pad(values[..., begin : begin + size], leading + [(0, PAD - size)])
        for begin, size in zip(BEGINS, SIZES)
    ]
    return jnp.concatenate(parts, axis=-1).reshape(values.shape[:-1] + (GROUP, WIDE))


def norm_kernel(values, gain, out):
    rows = wide(values[...])
    out[...] = low(rows * rms_scale(rows) * gain[...])


def norm_rows(values, gain, steps):
    rows, width = values.shape
    return pl.pallas_call(
        norm_kernel,
        grid=(rows // steps,),
        in_specs=[
            pl.BlockSpec((steps, width), lambda i: (i, 0)),
            pl.BlockSpec((1, width), lambda i: (0, 0)),
        ],
        out_specs=pl.BlockSpec((steps, width), lambda i: (i, 0)),
        out_shape=jax.ShapeDtypeStruct((rows, width), BF16),
        compiler_params=pltpu.CompilerParams(vmem_limit_bytes=48 * 1024 * 1024),
        cost_estimate=pl.CostEstimate(flops=1, bytes_accessed=1, transcendentals=0),
        name="norm_rows",
    )(values, gain)


SCALAR = pl.BlockSpec(memory_space=pltpu.SMEM)
BUFFER = pl.BlockSpec(memory_space=pltpu.VMEM)


def simple_call(kernel, name, place, arrays, outs, scratch=()):
    moved = sum(a.size * a.dtype.itemsize for a in arrays)
    return pl.pallas_call(
        kernel,
        in_specs=[SCALAR] + [BUFFER] * len(arrays),
        out_specs=[BUFFER] * len(outs),
        out_shape=[jax.ShapeDtypeStruct(shape, dtype) for shape, dtype in outs],
        scratch_shapes=list(scratch),
        compiler_params=pltpu.CompilerParams(vmem_limit_bytes=48 * 1024 * 1024),
        cost_estimate=pl.CostEstimate(flops=moved, bytes_accessed=2 * moved, transcendentals=0),
        name=name,
    )(place, *arrays)


def split_mixer_kernel(place, branch, gating, output, tiny, *rest):
    outs, held = rest[:GROUP], rest[GROUP]
    rows = branch.shape[0]
    held[...] = jnp.zeros_like(held)
    for slot, ref in enumerate((branch, gating, output)):
        values = wide(ref[...])
        for i in range(NBLK):
            begin = slot * WIDE + (i % 2) * PAD
            held[i // 2, :, begin : begin + SIZES[i]] = values[
                :, BEGINS[i] : BEGINS[i] + SIZES[i]
            ]
    for bit in range(GROUP):
        outs[bit][:rows] = low(held[place[0] ^ bit])
        outs[bit][rows:] = tiny[...]


def split_hidden_kernel(place, gate, linear, output, *outs):
    part = gate.shape[1] // GROUP
    for bit in range(GROUP):
        columns = pl.ds(pl.multiple_of((place[0] ^ bit) * part, 128), part)
        for slot, ref in enumerate((gate, linear, output)):
            outs[bit][:, slot * part : (slot + 1) * part] = ref[:, columns]


def collect_kernel(place, *refs):
    parts, (first, second) = refs[:GROUP], refs[GROUP:]
    cut = first.shape[2]
    for bit in range(GROUP):
        first[place[0] ^ bit] = parts[bit][:, :cut]
        second[place[0] ^ bit] = parts[bit][:, cut:]


def collect_mixer_kernel(place, *refs):
    parts, (columns, tiny) = refs[:GROUP], refs[GROUP:]
    rows = columns.shape[1]
    for bit in range(GROUP):
        columns[place[0] ^ bit] = parts[bit][:rows]
        tiny[place[0] ^ bit] = wide(parts[bit][rows:])[:1, : tiny.shape[2]]


def hidden_owner_kernel(place, gate, linear, gain, grads, *outs):
    part = gate.shape[1] // GROUP
    total = jnp.zeros((gate.shape[0], 1), F32)
    for device in range(GROUP):
        columns = slice(device * part, device * part + part)
        d_gate = wide(grads[device, :, :part])
        d_linear = wide(grads[device, :, part : 2 * part])
        outs[0][:, columns] = d_gate
        outs[1][:, columns] = d_linear
        outs[2][:, columns] = wide(grads[device, :, 2 * part :])
        terms = d_gate * wide(gate[:, columns]) + d_linear * wide(linear[:, columns])
        total = total + jnp.sum(terms, axis=1, keepdims=True)
    outs[3][...] = total / gain[...]


def mixer_owner_kernel(place, branch, gating, gain, both, last, *outs):
    for i in range(NBLK):
        columns = slice(BEGINS[i], BEGINS[i] + SIZES[i])
        begin = (i % 2) * PAD
        values = wide(both[i // 2])
        outs[0][:, columns] = values[:, begin : begin + SIZES[i]]
        outs[1][:, columns] = values[:, WIDE + begin : WIDE + begin + SIZES[i]]
        outs[2][:, columns] = wide(last[i // 2])[:, begin : begin + SIZES[i]]
    terms = outs[0][...] * wide(branch[...]) + outs[1][...] * wide(gating[...])
    outs[3][...] = jnp.sum(terms, axis=1, keepdims=True) / gain[...]


def gates_owner_kernel(place, *refs):
    parts, (blocks, small), held = refs[:GROUP], refs[GROUP : GROUP + 2], refs[-1]
    for part, bit in zip(parts, ORDER):
        device = place[0] ^ bit
        for gate in range(2):
            for block in range(2):
                begin = gate * WIDE + block * PAD
                blocks[gate, 2 * device + block] = wide(part[:BLK, begin : begin + BLK])
        ending = wide(part[SMALL:PAD])[:8]
        held[device] = ending[:, :WIDE] + ending[:, WIDE:]
    for i in range(NBLK):
        begin = (i % 2) * PAD
        small[:, BEGINS[i] : BEGINS[i] + SIZES[i]] = held[i // 2, :, begin : begin + SIZES[i]]


def rms_scale(values):
    return lax.rsqrt(jnp.mean(values * values, axis=-1, keepdims=True) + EPSILON)


def norm_back(values, scale, gain, grads):
    scaled = grads * gain
    return scale * (
        scaled - values * scale * scale * jnp.mean(scaled * values, axis=-1, keepdims=True)
    )


def product(left, right):
    return jnp.dot(left, right, preferred_element_type=F32)


def contract_rows(left, right):
    return lax.dot_general(left, right, (((0,), (0,)), ((), ())), preferred_element_type=F32)


def contract_cols(left, right):
    return lax.dot_general(left, right, (((1,), (1,)), ((), ())), preferred_element_type=F32)


def pair_product(left, right, first=None):
    half = left.shape[0] // 2
    far = low(contract_cols(left[half:], right))
    if first is None:
        return pair_total(contract_cols(left[:half], right), far)
    near, first = lax.optimization_barrier((left[:half], first))
    return pair_total(contract_cols(near, right), far), first


def sigmoid(values):
    return 1.0 / (1.0 + jnp.exp(-values))


GELU_A = 0.7978845608028654
GELU_B = 0.044715


def gelu_both(values):
    square = values * values
    bent = jnp.tanh(GELU_A * values * (1.0 + GELU_B * square))
    value = 0.5 * values * (1.0 + bent)
    slope = 0.5 * (1.0 + bent) + 0.5 * values * (1.0 - bent * bent) * GELU_A * (
        1.0 + 3.0 * GELU_B * square
    )
    return value, slope


def minus_expm1(values):
    series = 1.0 / 40320.0
    for divisor in (5040.0, 720.0, 120.0, 24.0, 6.0, 2.0, 1.0):
        series = series * values + 1.0 / divisor
    return -values * series


def repeated(values, width):
    return jnp.concatenate([values] * (width // 128), axis=1)


def gate_values(conv, fresh, weight, bias, rate):
    pre = product(low(conv), weight) + bias
    width = conv.shape[1]
    recur, enter = sigmoid(pre[:, :width]), sigmoid(pre[:, width:])
    log_decay = rate * recur
    decay = jnp.exp(log_decay)
    raw_scale = jnp.sqrt(minus_expm1(2.0 * log_decay))
    carry = jnp.where(fresh, 0.0, decay)
    scale = jnp.where(fresh, 1.0, raw_scale)
    return recur, enter, decay, raw_scale, carry, scale


def same_masks(numbers, steps, width):
    own = numbers[8 : 8 + steps]
    masks = [
        repeated(jnp.where(numbers[8 - k : 8 - k + steps] == own, 1.0, 0.0), width)
        for k in range(1, KW)
    ]
    return masks, masks[0] < 0.5


def convolve(padded, masks, params, steps):
    conv = params[6:7] + params[2:3] * padded[8 : 8 + steps]
    for offset in range(1, KW):
        conv = conv + params[2 + offset : 3 + offset] * (
            padded[8 - offset : 8 - offset + steps] * masks[offset - 1]
        )
    return conv


def forward_kernel(
    place,
    normed,
    segment,
    both_weight,
    weight,
    bias,
    params,
    pre,
    state_out,
    mixed_out,
    padded,
    mult,
    partial,
    chain,
    numbers,
):
    steps, width = padded.shape[0] - 8, padded.shape[1]
    chunk = steps // 8

    @pl.when(pl.program_id(1) == 0)
    def _():
        padded[0:8] = jnp.zeros((8, width), F32)
        numbers[0:8] = jnp.full((8, 128), -1.0, F32)
        chain[...] = jnp.zeros_like(chain)

    @pl.when(pl.program_id(1) > 0)
    def _():
        padded[0:8] = padded[steps : steps + 8]
        numbers[0:8] = numbers[steps : steps + 8]

    pre[0] = product(normed[0], both_weight[...])
    padded[8 : 8 + steps] = pre[0, :, :width]
    numbers[8 : 8 + steps] = segment[0]
    masks, fresh = same_masks(numbers, steps, width)
    conv = convolve(padded, masks, params, steps)
    recur, enter, decay, raw_scale, carry, scale = gate_values(
        conv, fresh, weight[...], bias[...], params[7:8]
    )
    for lane in range(width // 128):
        lanes = slice(lane * 128, lane * 128 + 128)
        mult[lane] = carry[:, lanes]
        partial[lane] = (scale * enter * conv)[:, lanes]
    for lane in range(width // 128):
        state = jnp.zeros((8, 128), F32)
        reach = jnp.ones((8, 128), F32)
        for step in range(chunk):
            rows = pl.ds(step, 8, stride=chunk)
            factor = mult[lane, rows, :]
            state = factor * state + partial[lane, rows, :]
            reach = factor * reach
            partial[lane, rows, :] = state
            mult[lane, rows, :] = reach
        lanes = slice(lane * 128, lane * 128 + 128)
        entering = chain[0:1, lanes]
        for part in range(8):
            rows = slice(part * chunk, part * chunk + chunk)
            state_out[0, rows, lanes] = partial[lane, rows, :] + mult[lane, rows, :] * entering
            entering = state[part : part + 1] + reach[part : part + 1] * entering
        chain[0:1, lanes] = entering
    value, _ = gelu_both(pre[0, :, width:])
    mixed_out[0] = low(state_out[0] * value)


def backward_kernel(
    place,
    pre,
    rim,
    segment,
    segment_rim,
    state,
    state_rim,
    middle,
    out_weight,
    weight,
    bias,
    params,
    d_both,
    packed,
    padded,
    mult,
    partial,
    adjoint_all,
    chain,
    later,
    numbers,
    grad_gate,
    grad_small,
):
    steps, width = padded.shape[0] - 8, padded.shape[1]
    chunk = steps // 8
    last = pl.program_id(1) == 0
    first = pl.program_id(1) == pl.num_programs(1) - 1

    @pl.when(last & (pl.program_id(0) == 0))
    def _():
        grad_gate[...] = jnp.zeros_like(grad_gate)
        grad_small[...] = jnp.zeros_like(grad_small)

    @pl.when(last)
    def _():
        chain[...] = jnp.zeros_like(chain)
        later[:, steps : steps + 8] = jnp.zeros((KW - 1, 8, width), F32)

    @pl.when(jnp.logical_not(last))
    def _():
        later[:, steps : steps + 8] = later[:, 0:8]

    padded[0:8] = rim[0]
    padded[8 : 8 + steps] = pre[0, :, :width]
    numbers[0:8] = jnp.where(first, -1.0, segment_rim[0])
    numbers[8 : 8 + steps] = segment[0]
    masks, fresh = same_masks(numbers, steps, width)
    conv = convolve(padded, masks, params, steps)
    recur, enter, decay, raw_scale, carry, scale = gate_values(
        conv, fresh, weight[...], bias[...], params[7:8]
    )
    value, slope = gelu_both(pre[0, :, width:])
    d_out = product(middle[0], out_weight[...])
    d_both[0, :, width:] = low(d_out * state[0] * slope)
    d_state = d_out * value
    for lane in range(width // 128):
        lanes = slice(lane * 128, lane * 128 + 128)
        mult[lane, 0:steps, :] = carry[:, lanes]
        mult[lane, steps : steps + 8, :] = jnp.ones((8, 128), F32)
        partial[lane] = d_state[:, lanes]
    for lane in range(width // 128):
        lanes = slice(lane * 128, lane * 128 + 128)
        first_mult = mult[lane, 0:1, :]
        total = jnp.zeros((8, 128), F32)
        reach = jnp.ones((8, 128), F32)
        for step in reversed(range(chunk)):
            rows = pl.ds(step, 8, stride=chunk)
            factor = mult[lane, pl.ds(step + 1, 8, stride=chunk), :]
            total = factor * total + partial[lane, rows, :]
            reach = factor * reach
            partial[lane, rows, :] = total
            mult[lane, pl.ds(step + 1, 8, stride=chunk), :] = reach
        entering = chain[0:1, lanes]
        for part in reversed(range(8)):
            begin = part * chunk
            adjoint_all[begin : begin + chunk, lanes] = (
                partial[lane, begin : begin + chunk, :]
                + mult[lane, begin + 1 : begin + 1 + chunk, :] * entering
            )
            entering = total[part : part + 1] + reach[part : part + 1] * entering
        chain[0:1, lanes] = first_mult * entering
    adjoint = adjoint_all[...]
    padded_state = jnp.concatenate([state_rim[0, 7:8], state[0, : steps - 1]], axis=0)
    d_scale = adjoint * enter * conv
    d_enter = adjoint * scale * conv
    d_log = jnp.where(
        fresh, 0.0, decay * (adjoint * padded_state - d_scale * decay / raw_scale)
    )
    d_recur_pre = d_log * params[7:8] * recur * (1.0 - recur)
    d_enter_pre = d_enter * enter * (1.0 - enter)
    d_pre = jnp.concatenate([d_recur_pre, d_enter_pre], axis=1)
    d_pre_low = low(d_pre)
    d_conv = adjoint * scale * enter + contract_cols(d_pre_low, weight[...])
    grad_gate[...] += contract_rows(low(conv), d_pre_low)
    sums = [
        jnp.sum(d_recur_pre, axis=0, keepdims=True),
        jnp.sum(d_enter_pre, axis=0, keepdims=True),
        jnp.sum(d_conv * padded[8 : 8 + steps], axis=0, keepdims=True),
    ]
    d_branch = d_conv * params[2:3]
    for offset in range(1, KW):
        masked = d_conv * masks[offset - 1]
        sums.append(
            jnp.sum(masked * padded[8 - offset : 8 - offset + steps], axis=0, keepdims=True)
        )
        later[offset - 1, 0:steps] = masked * params[2 + offset : 3 + offset]
        d_branch = d_branch + later[offset - 1, offset : offset + steps]
    sums.append(jnp.sum(d_conv, axis=0, keepdims=True))
    sums.append(jnp.sum(d_log * recur, axis=0, keepdims=True))
    for row, value_sum in enumerate(sums):
        grad_small[row : row + 1] += value_sum
    d_both[0, :, :width] = low(d_branch)

    @pl.when(first & (pl.program_id(0) == pl.num_programs(0) - 1))
    def _():
        side = lax.broadcasted_iota(jnp.int32, (PAD, 2 * width), 1) % width
        blocks = jnp.where(side < PAD, grad_gate[0:PAD], grad_gate[PAD : 2 * PAD])
        rest = grad_small[...] - wide(low(grad_small[...]))
        packed[...] = low(blocks)
        packed[SMALL:PAD] = low(
            jnp.concatenate([jnp.concatenate([grad_small[...], rest], axis=1), blocks[-8:]], axis=0)
        )


def mixer_calls(rows, shards, steps, channels, model):
    blocks = rows * shards

    def position(row, shard, place):
        offset = (row * shards + shard) ^ place
        return (offset // 2) + (offset % 2) * (GROUP // 2)

    def whole(*dims):
        return pl.BlockSpec(dims, lambda row, shard, place: (0,) * len(dims))

    params = pltpu.CompilerParams(
        dimension_semantics=("arbitrary", "arbitrary"), vmem_limit_bytes=48 * 1024 * 1024
    )
    lanes = channels // 128
    forward = pl.pallas_call(
        forward_kernel,
        grid_spec=pltpu.PrefetchScalarGridSpec(
            num_scalar_prefetch=1,
            grid=(rows, shards),
            in_specs=[
                pl.BlockSpec((1, steps, model), lambda r, s, p: (position(r, s, p[0]), 0, 0)),
                pl.BlockSpec((1, steps, 128), lambda r, s, p: (r * shards + s, 0, 0)),
                whole(model, 2 * channels),
                whole(channels, 2 * channels),
                whole(1, 2 * channels),
                whole(8, channels),
            ],
            out_specs=[
                pl.BlockSpec(
                    (1, steps, 2 * channels), lambda r, s, p: (position(r, s, p[0]), 0, 0)
                ),
                pl.BlockSpec((1, steps, channels), lambda r, s, p: (r * shards + s, 0, 0)),
                pl.BlockSpec((1, steps, channels), lambda r, s, p: (position(r, s, p[0]), 0, 0)),
            ],
            scratch_shapes=[
                pltpu.VMEM((steps + 8, channels), F32),
                pltpu.VMEM((lanes, steps, 128), F32),
                pltpu.VMEM((lanes, steps, 128), F32),
                pltpu.VMEM((8, channels), F32),
                pltpu.VMEM((steps + 8, 128), F32),
            ],
        ),
        out_shape=[
            jax.ShapeDtypeStruct((blocks, steps, 2 * channels), F32),
            jax.ShapeDtypeStruct((blocks, steps, channels), F32),
            jax.ShapeDtypeStruct((blocks, steps, channels), BF16),
        ],
        compiler_params=params,
        cost_estimate=pl.CostEstimate(
            flops=blocks * steps * channels * (channels * 4 + model * 4),
            bytes_accessed=blocks * steps * channels * 14,
            transcendentals=blocks * steps * channels * 6,
        ),
        name="mixer_forward",
    )

    def turned(shard):
        return shards - 1 - shard

    def before(shard):
        return jnp.maximum(shards - 2 - shard, 0)

    backward = pl.pallas_call(
        backward_kernel,
        grid_spec=pltpu.PrefetchScalarGridSpec(
            num_scalar_prefetch=1,
            grid=(rows, shards),
            in_specs=[
                pl.BlockSpec(
                    (1, steps, 2 * channels), lambda r, s, p: (position(r, turned(s), p[0]), 0, 0)
                ),
                pl.BlockSpec(
                    (1, 8, channels),
                    lambda r, s, p: (position(r, before(s), p[0]), steps // 8 - 1, 0),
                ),
                pl.BlockSpec((1, steps, 128), lambda r, s, p: (r * shards + turned(s), 0, 0)),
                pl.BlockSpec(
                    (1, 8, 128), lambda r, s, p: (r * shards + before(s), steps // 8 - 1, 0)
                ),
                pl.BlockSpec((1, steps, channels), lambda r, s, p: (r * shards + turned(s), 0, 0)),
                pl.BlockSpec(
                    (1, 8, channels),
                    lambda r, s, p: (r * shards + before(s), steps // 8 - 1, 0),
                ),
                pl.BlockSpec(
                    (1, steps, model), lambda r, s, p: (position(r, turned(s), p[0]), 0, 0)
                ),
                pl.BlockSpec((model, channels), lambda r, s, p: (0, 2)),
                whole(channels, 2 * channels),
                whole(1, 2 * channels),
                whole(8, channels),
            ],
            out_specs=[
                pl.BlockSpec(
                    (1, steps, 2 * channels), lambda r, s, p: (position(r, turned(s), p[0]), 0, 0)
                ),
                whole(PAD, 2 * channels),
            ],
            scratch_shapes=[
                pltpu.VMEM((steps + 8, channels), F32),
                pltpu.VMEM((lanes, steps + 8, 128), F32),
                pltpu.VMEM((lanes, steps, 128), F32),
                pltpu.VMEM((steps, channels), F32),
                pltpu.VMEM((8, channels), F32),
                pltpu.VMEM((KW - 1, steps + 8, channels), F32),
                pltpu.VMEM((steps + 8, 128), F32),
                pltpu.VMEM((channels, 2 * channels), F32),
                pltpu.VMEM((8, channels), F32),
            ],
        ),
        out_shape=[
            jax.ShapeDtypeStruct((blocks, steps, 2 * channels), BF16),
            jax.ShapeDtypeStruct((PAD, 2 * channels), BF16),
        ],
        compiler_params=params,
        cost_estimate=pl.CostEstimate(
            flops=blocks * steps * channels * (channels * 12 + model * 2),
            bytes_accessed=blocks * steps * channels * 24,
            transcendentals=blocks * steps * channels * 8,
        ),
        name="mixer_backward",
    )
    return forward, backward


def local(
    stream_in,
    segment_ids,
    out_grad,
    branch_weight,
    gating_weight,
    output_weight,
    hidden_gate,
    hidden_linear,
    hidden_output,
    mixer_gain,
    hidden_gain,
    gate_blocks,
    gate_biases,
    conv_taps,
    conv_bias,
    decay_param,
):
    rows_here, steps, model_width = stream_in.shape
    shards = lax.axis_size("seq")
    rows = GROUP // shards
    assert rows_here == 1 and rows * shards == GROUP
    groups = device_count() // GROUP
    place = flat_index() % GROUP
    turn = flat_index() // GROUP
    own_rows, hidden_width = hidden_gate.shape
    hidden_part = hidden_width // GROUP
    tokens = GROUP * steps

    where = place.astype(jnp.int32).reshape(1)
    tiny = jnp.concatenate(
        [mixer_gain[None], hidden_gain[None], low(segment_ids)], axis=1
    )
    tiny_width = tiny.shape[1]
    mixer_parts = simple_call(
        split_mixer_kernel,
        "split_mixer",
        where,
        (
            branch_weight,
            gating_weight,
            output_weight,
            jnp.pad(tiny, ((0, 15), (0, 3 * WIDE - tiny_width))),
        ),
        [((own_rows + 16, 3 * WIDE), BF16)] * GROUP,
        [pltpu.VMEM((GROUP, own_rows, 3 * WIDE), F32)],
    )
    mixer_rows, tiny = simple_call(
        collect_mixer_kernel,
        "collect_mixer",
        where,
        all_swapped(mixer_parts),
        [
            ((GROUP, own_rows, 3 * WIDE), BF16),
            ((GROUP, 1, tiny_width), F32),
        ],
    )
    tiny = tiny.reshape(GROUP, tiny_width)
    mixer_weight = ring_gather(mixer_rows.reshape(-1, 3 * WIDE))
    both_weight, out_weight = mixer_weight[:, : 2 * WIDE], mixer_weight[:, 2 * WIDE :]
    gains = ring_stack(tiny[:, : 2 * own_rows], turn, groups)
    mixer_scale = gains[..., :own_rows].reshape(1, model_width)
    hidden_scale = gains[..., own_rows:].reshape(1, model_width)
    segments = jnp.broadcast_to(tiny[:, 2 * own_rows :, None], (GROUP, steps, 128))

    inputs = wide(stream_in).reshape(steps, model_width)
    inputs_scale = rms_scale(inputs)
    parts = group_parts(stream_in.reshape(steps, model_width))
    raw = jnp.concatenate(parts, axis=0)
    normed = norm_rows(raw, mixer_scale, steps)
    upstream = wide(out_grad).reshape(steps, model_width)
    hidden_parts = simple_call(
        split_hidden_kernel,
        "split_hidden",
        where,
        (hidden_gate, hidden_linear, hidden_output),
        [((own_rows, 3 * hidden_part), BF16)] * GROUP,
    )
    pair_rows, last_rows = simple_call(
        collect_kernel,
        "collect_hidden",
        where,
        lax.optimization_barrier(
            (
                all_swapped(lax.optimization_barrier((hidden_parts, parts[3:5]))[0]),
                (raw, mixer_scale),
            )
        )[0],
        [((GROUP, own_rows, 2 * hidden_part), BF16), ((GROUP, own_rows, hidden_part), BF16)],
    )
    pair_weight = ring_gather(pair_rows.reshape(-1, 2 * hidden_part))
    normed_blocks = after(normed, pair_rows).reshape(GROUP, steps, model_width)

    rate = -8.0 * jax.nn.softplus(-decay_param)
    params = jnp.concatenate(
        [gate_biases, conv_taps, conv_bias[None], rate[None]], axis=0
    )
    params = pick(jnp.swapaxes(to_windows(params), 0, 1), place)
    bias = params[:2].reshape(1, 2 * WIDE)
    params = params.at[7].set(jnp.where(params[7] == 0.0, -0.01, params[7]))
    blocks = lax.dynamic_slice_in_dim(gate_blocks, 2 * place, 2, 1)
    blocks = jnp.pad(blocks, ((0, 0), (0, 0), (0, PAD - BLK), (0, PAD - BLK)))
    empty = jnp.zeros((PAD, PAD), BF16)
    gate_weight = jnp.concatenate(
        [
            jnp.concatenate([blocks[0, 0], empty, blocks[1, 0], empty], axis=1),
            jnp.concatenate([empty, blocks[0, 1], empty, blocks[1, 1]], axis=1),
        ],
        axis=0,
    )
    mixer_forward, mixer_backward = mixer_calls(rows, shards, steps, WIDE, model_width)
    own = after(out_grad.reshape(steps, model_width), normed)
    swapped = first_swaps(own)
    pre, state, mixed = mixer_forward(
        where, normed_blocks, segments, mixer_weight, gate_weight, bias, params
    )
    mixed, swapped = lax.optimization_barrier((mixed.reshape(tokens, WIDE), swapped))
    upstream_parts = group_parts(own, swapped)
    last_weight = ring_gather(after(last_rows, mixed).reshape(-1, hidden_part))
    middle = inputs + group_total(pair_product(mixed, out_weight))

    middle_scale = rms_scale(middle)
    own = low(middle * middle_scale * hidden_scale)
    parts = group_parts(own, lax.optimization_barrier((first_swaps(own), pair_weight))[0])
    normed_mid = jnp.concatenate(parts, axis=0)
    upstream_all = jnp.concatenate(upstream_parts, axis=0)
    pair = product(normed_mid, pair_weight)
    gate_pre, linear_pre = pair[:, :hidden_part], pair[:, hidden_part:]
    value, slope = gelu_both(gate_pre)
    hidden, value, slope = lax.optimization_barrier(
        (low(value * linear_pre), value, linear_pre * slope)
    )
    grad_last_low = low(contract_rows(upstream_all, hidden))
    grad_last = ring_reduce(grad_last_low)
    half = tokens // 2
    hidden_far = low(contract_cols(after(hidden[half:], grad_last_low), last_weight))
    d_hidden = product(after(upstream_all, grad_last_low, hidden_far), last_weight)
    d_pair = jnp.concatenate(
        [low(d_hidden * slope), low(d_hidden * value)], axis=1
    )
    hidden_near = contract_cols(after(hidden[:half], d_pair), last_weight)
    hidden_out = pair_total(hidden_near, hidden_far)
    hidden_sent = send_totals(hidden_out)
    grad_pair_low = low(contract_rows(normed_mid, after(d_pair, hidden_out)))
    grad_pair = ring_reduce(grad_pair_low)
    hidden_rest = rest_totals(hidden_out, hidden_sent)
    d_pair, hidden_rest, hidden_sent = lax.optimization_barrier(
        (after(d_pair, grad_pair_low), hidden_rest, hidden_sent)
    )
    d_normed_mid, hidden_out = pair_product(
        d_pair, pair_weight, join_totals(hidden_out, hidden_sent, hidden_rest)
    )
    result = low(middle + hidden_out)
    d_middle = upstream + norm_back(
        middle, middle_scale, hidden_scale, group_total(d_normed_mid)
    )

    def to_owner(grads):
        return exchange(grads.reshape(GROUP, own_rows, -1))

    own = after(low(d_middle), grad_last)
    middle_low = group_gather(own)
    grad_out_low = low(contract_rows(middle_low, mixed))
    grad_out = ring_reduce(grad_out_low)
    middle_blocks = after(middle_low, grad_out_low, grad_pair).reshape(GROUP, steps, model_width)
    hidden_grads = to_owner(jnp.concatenate([grad_pair, grad_last], axis=1))
    d_both, packed = mixer_backward(
        where,
        pre,
        pre,
        segments,
        segments,
        state,
        state,
        middle_blocks,
        mixer_weight,
        gate_weight,
        bias,
        params,
    )
    d_both = d_both.reshape(tokens, 2 * WIDE)
    grad_both_low = low(contract_rows(normed, after(d_both, grad_out, hidden_grads)))
    grad_both = ring_reduce(grad_both_low)
    packed = ring_sum(packed, turn, groups)
    d_normed, packed = pair_product(after(d_both, grad_both_low), both_weight, packed)
    d_normed = group_total(d_normed)
    stream_grad = low(d_middle + norm_back(inputs, inputs_scale, mixer_scale, d_normed))

    grad_hgate, grad_hlinear, grad_houtput, grad_hgain = simple_call(
        hidden_owner_kernel,
        "hidden_owner",
        where,
        (hidden_gate, hidden_linear, wide(hidden_gain)[:, None])
        + (hidden_grads,),
        [((own_rows, hidden_width), F32)] * 3 + [((own_rows, 1), F32)],
    )
    both_grads, out_grads = to_owner(grad_both), to_owner(grad_out)

    packed = ring_stack(packed, turn, groups).reshape(PAD, 2 * WIDE)
    packed, out_grads = lax.optimization_barrier((packed, out_grads))
    across, along = lax.optimization_barrier((swap(packed, 4), swap(packed, 2)))
    near = [packed, along, across, swap(across, 2)]
    near, both_grads = lax.optimization_barrier((near, both_grads))
    grad_gblocks, small = simple_call(
        gates_owner_kernel,
        "gates_owner",
        where,
        near + [swap(part, 1) for part in near],
        [((2, NBLK, BLK, BLK), F32), ((8, R), F32)],
        [pltpu.VMEM((GROUP, 8, WIDE), F32)],
    )
    grad_decay = 8.0 * jax.nn.sigmoid(-decay_param) * small[7]

    grad_branch, grad_gating, grad_output, grad_mgain = simple_call(
        mixer_owner_kernel,
        "mixer_owner",
        where,
        (branch_weight, gating_weight, wide(mixer_gain)[:, None])
        + (both_grads, out_grads),
        [((own_rows, R), F32)] * 3 + [((own_rows, 1), F32)],
    )

    shape = (rows_here, steps, model_width)
    return (
        result.reshape(shape),
        stream_grad.reshape(shape),
        grad_branch,
        grad_gating,
        grad_output,
        grad_hgate,
        grad_hlinear,
        grad_houtput,
        grad_mgain.reshape(own_rows),
        grad_hgain.reshape(own_rows),
        grad_gblocks,
        small[:2],
        small[2:6],
        small[6],
        grad_decay,
    )


def solution(mesh):
    return jax.shard_map(
        local,
        mesh=mesh,
        in_specs=(
            P("batch", "seq", None),
            P("batch", "seq"),
            P("batch", "seq", None),
            P(("batch", "seq"), None),
            P(("batch", "seq"), None),
            P(("batch", "seq"), None),
            P(("batch", "seq"), None),
            P(("batch", "seq"), None),
            P(("batch", "seq"), None),
            P(("batch", "seq")),
            P(("batch", "seq")),
            P(),
            P(),
            P(),
            P(),
            P(),
        ),
        out_specs=(
            P("batch", "seq", None),
            P("batch", "seq", None),
            P(("batch", "seq"), None),
            P(("batch", "seq"), None),
            P(("batch", "seq"), None),
            P(("batch", "seq"), None),
            P(("batch", "seq"), None),
            P(("batch", "seq"), None),
            P(("batch", "seq")),
            P(("batch", "seq")),
            P(),
            P(),
            P(),
            P(),
            P(),
        ),
        check_vma=False,
    )
```

```python
import functools

import jax
import jax.numpy as jnp
from jax import lax
from jax.experimental import pallas as pl
from jax.experimental.pallas import tpu as pltpu
from jax.sharding import PartitionSpec as P

NBLK = 16
BLK = 171
NBIG = 10
KW = 4
R = 2730

EPSILON = 1e-06

GROUP = 8
AXES = ("batch", "seq")
PAD = 192
SMALL = 176
WIDE = 2 * PAD
SIZES = [BLK] * NBIG + [BLK - 1] * (NBLK - NBIG)
BEGINS = [sum(SIZES[:i]) for i in range(NBLK)]
ORDER = (0, 2, 4, 6, 1, 3, 5, 7)

BF16 = jnp.bfloat16
F32 = jnp.float32


def device_count():
    return lax.axis_size("batch") * lax.axis_size("seq")


def flat_index():
    return lax.axis_index("batch") * lax.axis_size("seq") + lax.axis_index("seq")


def swap(values, bit):
    return lax.ppermute(values, AXES, [(i, i ^ bit) for i in range(device_count())])


def onward(values, turns):
    count = device_count()
    pairs = [(i, (i + turns * GROUP) % count) for i in range(count)]
    return lax.ppermute(values, AXES, pairs)


def low(values):
    return values.astype(BF16)


def wide(values):
    return values.astype(F32)


def pick(values, index):
    return lax.dynamic_index_in_dim(values, index, 0, False)


def put(values, part, index):
    return lax.dynamic_update_index_in_dim(values, part, index, 0)


def after(values, *others):
    return lax.optimization_barrier((values,) + others)[0]


def ring_groups():
    count = device_count()
    return [list(range(i, count, GROUP)) for i in range(GROUP)]


def ring_gather(block):
    return lax.all_gather(block, AXES, axis=0, tiled=True, axis_index_groups=ring_groups())


def ring_reduce(values):
    return lax.psum_scatter(
        values, AXES, scatter_dimension=0, tiled=True, axis_index_groups=ring_groups()
    )


def ring_stack(block, turn, groups):
    out = jnp.broadcast_to(block, (groups,) + block.shape)
    for step in range(1, groups):
        out = put(out, onward(block, step), (turn + groups - step) % groups)
    return out


def ring_sum(values, turn, groups):
    chunks = values.reshape((groups, -1) + values.shape[1:])
    total = wide(pick(chunks, turn))
    for step in range(1, groups):
        total = total + wide(onward(pick(chunks, (turn + step) % groups), step))
    return low(total)


def exchange(pieces):
    count = device_count()
    sets = [list(range(i, i + GROUP)) for i in range(0, count, GROUP)]
    return lax.all_to_all(pieces, AXES, 0, 0, axis_index_groups=sets)


def all_swapped(parts):
    return [parts[0]] + [swap(parts[bit], bit) for bit in range(1, GROUP)]


def first_swaps(own):
    return swap(own, 4), swap(own, 2)


def group_parts(own, swapped=None):
    half = own.shape[0] // 2
    across, along = swapped or first_swaps(own)
    first, second = swap(across[:half], 2), swap(along[half:], 4)
    mine = [own, along, across, first, second]
    return mine + [swap(part, 1) for part in mine]


def group_gather(own):
    return jnp.concatenate(group_parts(own), axis=0)


def pair_total(near, far):
    near = near.reshape(4, -1, near.shape[-1])
    return near + wide(swap(low(far), 1)).reshape(near.shape)


def send_totals(total):
    half = total.shape[1] // 2
    return (
        swap(low(total[3, :half]), 4),
        swap(low(total[3, half:]), 2),
        swap(low(total[2, :half]), 4),
        swap(low(total[1, half:]), 2),
    )


def rest_totals(total, arrived):
    first, second, across, along = arrived
    half = total.shape[1] // 2
    return low(total[2, half:] + wide(second)), low(total[1, :half] + wide(first))


def join_totals(total, arrived, rest=None):
    first, second, across, along = arrived
    across_rest, along_rest = rest or rest_totals(total, arrived)
    across_rest, along_rest = swap(across_rest, 4), swap(along_rest, 2)
    return (
        total[0]
        + wide(jnp.concatenate([across, across_rest], axis=0))
        + wide(jnp.concatenate([along_rest, along], axis=0))
    )


def group_total(total):
    return join_totals(total, send_totals(total))


def to_windows(values):
    leading = [(0, 0)] * (values.ndim - 1)
    parts = [
        jnp.pad(values[..., begin : begin + size], leading + [(0, PAD - size)])
        for begin, size in zip(BEGINS, SIZES)
    ]
    return jnp.concatenate(parts, axis=-1).reshape(values.shape[:-1] + (GROUP, WIDE))


def norm_kernel(values, gain, out):
    rows = wide(values[...])
    out[...] = low(rows * rms_scale(rows) * gain[...])


def norm_rows(values, gain, steps):
    rows, width = values.shape
    return pl.pallas_call(
        norm_kernel,
        grid=(rows // steps,),
        in_specs=[
            pl.BlockSpec((steps, width), lambda i: (i, 0)),
            pl.BlockSpec((1, width), lambda i: (0, 0)),
        ],
        out_specs=pl.BlockSpec((steps, width), lambda i: (i, 0)),
        out_shape=jax.ShapeDtypeStruct((rows, width), BF16),
        compiler_params=pltpu.CompilerParams(vmem_limit_bytes=48 * 1024 * 1024),
        cost_estimate=pl.CostEstimate(flops=1, bytes_accessed=1, transcendentals=0),
        name="norm_rows",
    )(values, gain)


SCALAR = pl.BlockSpec(memory_space=pltpu.SMEM)
BUFFER = pl.BlockSpec(memory_space=pltpu.VMEM)


def simple_call(kernel, name, place, arrays, outs, scratch=()):
    moved = sum(a.size * a.dtype.itemsize for a in arrays)
    return pl.pallas_call(
        kernel,
        in_specs=[SCALAR] + [BUFFER] * len(arrays),
        out_specs=[BUFFER] * len(outs),
        out_shape=[jax.ShapeDtypeStruct(shape, dtype) for shape, dtype in outs],
        scratch_shapes=list(scratch),
        compiler_params=pltpu.CompilerParams(vmem_limit_bytes=48 * 1024 * 1024),
        cost_estimate=pl.CostEstimate(flops=moved, bytes_accessed=2 * moved, transcendentals=0),
        name=name,
    )(place, *arrays)


def split_mixer_kernel(place, branch, gating, output, tiny, *rest):
    outs, held = rest[:GROUP], rest[GROUP]
    rows = branch.shape[0]
    held[...] = jnp.zeros_like(held)
    for slot, ref in enumerate((branch, gating, output)):
        values = wide(ref[...])
        for i in range(NBLK):
            begin = slot * WIDE + (i % 2) * PAD
            held[i // 2, :, begin : begin + SIZES[i]] = values[
                :, BEGINS[i] : BEGINS[i] + SIZES[i]
            ]
    for bit in range(GROUP):
        outs[bit][:rows] = low(held[place[0] ^ bit])
        outs[bit][rows:] = tiny[...]


def split_hidden_kernel(place, gate, linear, output, *outs):
    part = gate.shape[1] // GROUP
    for bit in range(GROUP):
        columns = pl.ds(pl.multiple_of((place[0] ^ bit) * part, 128), part)
        for slot, ref in enumerate((gate, linear, output)):
            outs[bit][:, slot * part : (slot + 1) * part] = ref[:, columns]


def collect_kernel(place, *refs):
    parts, (first, second) = refs[:GROUP], refs[GROUP:]
    cut = first.shape[2]
    for bit in range(GROUP):
        first[place[0] ^ bit] = parts[bit][:, :cut]
        second[place[0] ^ bit] = parts[bit][:, cut:]


def collect_mixer_kernel(place, *refs):
    parts, (columns, tiny) = refs[:GROUP], refs[GROUP:]
    rows = columns.shape[1]
    for bit in range(GROUP):
        columns[place[0] ^ bit] = parts[bit][:rows]
        tiny[place[0] ^ bit] = wide(parts[bit][rows:])[:1, : tiny.shape[2]]


def hidden_owner_kernel(place, gate, linear, gain, grads, *outs):
    part = gate.shape[1] // GROUP
    total = jnp.zeros((gate.shape[0], 1), F32)
    for device in range(GROUP):
        columns = slice(device * part, device * part + part)
        d_gate = wide(grads[device, :, :part])
        d_linear = wide(grads[device, :, part : 2 * part])
        outs[0][:, columns] = d_gate
        outs[1][:, columns] = d_linear
        outs[2][:, columns] = wide(grads[device, :, 2 * part :])
        terms = d_gate * wide(gate[:, columns]) + d_linear * wide(linear[:, columns])
        total = total + jnp.sum(terms, axis=1, keepdims=True)
    outs[3][...] = total / gain[...]


def mixer_owner_kernel(place, branch, gating, gain, both, last, *outs):
    for i in range(NBLK):
        columns = slice(BEGINS[i], BEGINS[i] + SIZES[i])
        begin = (i % 2) * PAD
        values = wide(both[i // 2])
        outs[0][:, columns] = values[:, begin : begin + SIZES[i]]
        outs[1][:, columns] = values[:, WIDE + begin : WIDE + begin + SIZES[i]]
        outs[2][:, columns] = wide(last[i // 2])[:, begin : begin + SIZES[i]]
    terms = outs[0][...] * wide(branch[...]) + outs[1][...] * wide(gating[...])
    outs[3][...] = jnp.sum(terms, axis=1, keepdims=True) / gain[...]


def gates_owner_kernel(place, *refs):
    parts, (blocks, small), held = refs[:GROUP], refs[GROUP : GROUP + 2], refs[-1]
    for part, bit in zip(parts, ORDER):
        device = place[0] ^ bit
        for gate in range(2):
            for block in range(2):
                begin = gate * WIDE + block * PAD
                blocks[gate, 2 * device + block] = wide(part[:BLK, begin : begin + BLK])
        ending = wide(part[SMALL:PAD])[:8]
        held[device] = ending[:, :WIDE] + ending[:, WIDE:]
    for i in range(NBLK):
        begin = (i % 2) * PAD
        small[:, BEGINS[i] : BEGINS[i] + SIZES[i]] = held[i // 2, :, begin : begin + SIZES[i]]


def rms_scale(values):
    return lax.rsqrt(jnp.mean(values * values, axis=-1, keepdims=True) + EPSILON)


def norm_back(values, scale, gain, grads):
    scaled = grads * gain
    return scale * (
        scaled - values * scale * scale * jnp.mean(scaled * values, axis=-1, keepdims=True)
    )


def product(left, right):
    return jnp.dot(left, right, preferred_element_type=F32)


def contract_rows(left, right):
    return lax.dot_general(left, right, (((0,), (0,)), ((), ())), preferred_element_type=F32)


def contract_cols(left, right):
    return lax.dot_general(left, right, (((1,), (1,)), ((), ())), preferred_element_type=F32)


def pair_product(left, right, first=None):
    half = left.shape[0] // 2
    far = low(contract_cols(left[half:], right))
    if first is None:
        return pair_total(contract_cols(left[:half], right), far)
    near, first = lax.optimization_barrier((left[:half], first))
    return pair_total(contract_cols(near, right), far), first


def sigmoid(values):
    return 1.0 / (1.0 + jnp.exp(-values))


GELU_A = 0.7978845608028654
GELU_B = 0.044715


def gelu_both(values):
    square = values * values
    bent = jnp.tanh(GELU_A * values * (1.0 + GELU_B * square))
    value = 0.5 * values * (1.0 + bent)
    slope = 0.5 * (1.0 + bent) + 0.5 * values * (1.0 - bent * bent) * GELU_A * (
        1.0 + 3.0 * GELU_B * square
    )
    return value, slope


def minus_expm1(values):
    series = 1.0 / 40320.0
    for divisor in (5040.0, 720.0, 120.0, 24.0, 6.0, 2.0, 1.0):
        series = series * values + 1.0 / divisor
    return -values * series


def repeated(values, width):
    return jnp.concatenate([values] * (width // 128), axis=1)


def gate_values(conv, fresh, weight, bias, rate):
    pre = product(low(conv), weight) + bias
    width = conv.shape[1]
    recur, enter = sigmoid(pre[:, :width]), sigmoid(pre[:, width:])
    log_decay = rate * recur
    decay = jnp.exp(log_decay)
    raw_scale = jnp.sqrt(minus_expm1(2.0 * log_decay))
    carry = jnp.where(fresh, 0.0, decay)
    scale = jnp.where(fresh, 1.0, raw_scale)
    return recur, enter, decay, raw_scale, carry, scale


def same_masks(numbers, steps, width):
    own = numbers[8 : 8 + steps]
    masks = [
        repeated(jnp.where(numbers[8 - k : 8 - k + steps] == own, 1.0, 0.0), width)
        for k in range(1, KW)
    ]
    return masks, masks[0] < 0.5


def convolve(padded, masks, params, steps):
    conv = params[6:7] + params[2:3] * padded[8 : 8 + steps]
    for offset in range(1, KW):
        conv = conv + params[2 + offset : 3 + offset] * (
            padded[8 - offset : 8 - offset + steps] * masks[offset - 1]
        )
    return conv


def forward_kernel(
    place,
    normed,
    segment,
    both_weight,
    weight,
    bias,
    params,
    pre,
    state_out,
    mixed_out,
    padded,
    mult,
    partial,
    chain,
    numbers,
):
    steps, width = padded.shape[0] - 8, padded.shape[1]
    chunk = steps // 8

    @pl.when(pl.program_id(1) == 0)
    def _():
        padded[0:8] = jnp.zeros((8, width), F32)
        numbers[0:8] = jnp.full((8, 128), -1.0, F32)
        chain[...] = jnp.zeros_like(chain)

    @pl.when(pl.program_id(1) > 0)
    def _():
        padded[0:8] = padded[steps : steps + 8]
        numbers[0:8] = numbers[steps : steps + 8]

    pre[0] = product(normed[0], both_weight[...])
    padded[8 : 8 + steps] = pre[0, :, :width]
    numbers[8 : 8 + steps] = segment[0]
    masks, fresh = same_masks(numbers, steps, width)
    conv = convolve(padded, masks, params, steps)
    recur, enter, decay, raw_scale, carry, scale = gate_values(
        conv, fresh, weight[...], bias[...], params[7:8]
    )
    for lane in range(width // 128):
        lanes = slice(lane * 128, lane * 128 + 128)
        mult[lane] = carry[:, lanes]
        partial[lane] = (scale * enter * conv)[:, lanes]
    for lane in range(width // 128):
        state = jnp.zeros((8, 128), F32)
        reach = jnp.ones((8, 128), F32)
        for step in range(chunk):
            rows = pl.ds(step, 8, stride=chunk)
            factor = mult[lane, rows, :]
            state = factor * state + partial[lane, rows, :]
            reach = factor * reach
            partial[lane, rows, :] = state
            mult[lane, rows, :] = reach
        lanes = slice(lane * 128, lane * 128 + 128)
        entering = chain[0:1, lanes]
        for part in range(8):
            rows = slice(part * chunk, part * chunk + chunk)
            state_out[0, rows, lanes] = partial[lane, rows, :] + mult[lane, rows, :] * entering
            entering = state[part : part + 1] + reach[part : part + 1] * entering
        chain[0:1, lanes] = entering
    value, _ = gelu_both(pre[0, :, width:])
    mixed_out[0] = low(state_out[0] * value)


def backward_kernel(
    place,
    pre,
    rim,
    segment,
    segment_rim,
    state,
    state_rim,
    middle,
    out_weight,
    weight,
    bias,
    params,
    d_both,
    packed,
    padded,
    mult,
    partial,
    adjoint_all,
    chain,
    later,
    numbers,
    grad_gate,
    grad_small,
):
    steps, width = padded.shape[0] - 8, padded.shape[1]
    chunk = steps // 8
    last = pl.program_id(1) == 0
    first = pl.program_id(1) == pl.num_programs(1) - 1

    @pl.when(last & (pl.program_id(0) == 0))
    def _():
        grad_gate[...] = jnp.zeros_like(grad_gate)
        grad_small[...] = jnp.zeros_like(grad_small)

    @pl.when(last)
    def _():
        chain[...] = jnp.zeros_like(chain)
        later[:, steps : steps + 8] = jnp.zeros((KW - 1, 8, width), F32)

    @pl.when(jnp.logical_not(last))
    def _():
        later[:, steps : steps + 8] = later[:, 0:8]

    padded[0:8] = rim[0]
    padded[8 : 8 + steps] = pre[0, :, :width]
    numbers[0:8] = jnp.where(first, -1.0, segment_rim[0])
    numbers[8 : 8 + steps] = segment[0]
    masks, fresh = same_masks(numbers, steps, width)
    conv = convolve(padded, masks, params, steps)
    recur, enter, decay, raw_scale, carry, scale = gate_values(
        conv, fresh, weight[...], bias[...], params[7:8]
    )
    value, slope = gelu_both(pre[0, :, width:])
    d_out = product(middle[0], out_weight[...])
    d_both[0, :, width:] = low(d_out * state[0] * slope)
    d_state = d_out * value
    for lane in range(width // 128):
        lanes = slice(lane * 128, lane * 128 + 128)
        mult[lane, 0:steps, :] = carry[:, lanes]
        mult[lane, steps : steps + 8, :] = jnp.ones((8, 128), F32)
        partial[lane] = d_state[:, lanes]
    for lane in range(width // 128):
        lanes = slice(lane * 128, lane * 128 + 128)
        first_mult = mult[lane, 0:1, :]
        total = jnp.zeros((8, 128), F32)
        reach = jnp.ones((8, 128), F32)
        for step in reversed(range(chunk)):
            rows = pl.ds(step, 8, stride=chunk)
            factor = mult[lane, pl.ds(step + 1, 8, stride=chunk), :]
            total = factor * total + partial[lane, rows, :]
            reach = factor * reach
            partial[lane, rows, :] = total
            mult[lane, pl.ds(step + 1, 8, stride=chunk), :] = reach
        entering = chain[0:1, lanes]
        for part in reversed(range(8)):
            begin = part * chunk
            adjoint_all[begin : begin + chunk, lanes] = (
                partial[lane, begin : begin + chunk, :]
                + mult[lane, begin + 1 : begin + 1 + chunk, :] * entering
            )
            entering = total[part : part + 1] + reach[part : part + 1] * entering
        chain[0:1, lanes] = first_mult * entering
    adjoint = adjoint_all[...]
    padded_state = jnp.concatenate([state_rim[0, 7:8], state[0, : steps - 1]], axis=0)
    d_scale = adjoint * enter * conv
    d_enter = adjoint * scale * conv
    d_log = jnp.where(
        fresh, 0.0, decay * (adjoint * padded_state - d_scale * decay / raw_scale)
    )
    d_recur_pre = d_log * params[7:8] * recur * (1.0 - recur)
    d_enter_pre = d_enter * enter * (1.0 - enter)
    d_pre = jnp.concatenate([d_recur_pre, d_enter_pre], axis=1)
    d_pre_low = low(d_pre)
    d_conv = adjoint * scale * enter + contract_cols(d_pre_low, weight[...])
    grad_gate[...] += contract_rows(low(conv), d_pre_low)
    sums = [
        jnp.sum(d_recur_pre, axis=0, keepdims=True),
        jnp.sum(d_enter_pre, axis=0, keepdims=True),
        jnp.sum(d_conv * padded[8 : 8 + steps], axis=0, keepdims=True),
    ]
    d_branch = d_conv * params[2:3]
    for offset in range(1, KW):
        masked = d_conv * masks[offset - 1]
        sums.append(
            jnp.sum(masked * padded[8 - offset : 8 - offset + steps], axis=0, keepdims=True)
        )
        later[offset - 1, 0:steps] = masked * params[2 + offset : 3 + offset]
        d_branch = d_branch + later[offset - 1, offset : offset + steps]
    sums.append(jnp.sum(d_conv, axis=0, keepdims=True))
    sums.append(jnp.sum(d_log * recur, axis=0, keepdims=True))
    for row, value_sum in enumerate(sums):
        grad_small[row : row + 1] += value_sum
    d_both[0, :, :width] = low(d_branch)

    @pl.when(first & (pl.program_id(0) == pl.num_programs(0) - 1))
    def _():
        side = lax.broadcasted_iota(jnp.int32, (PAD, 2 * width), 1) % width
        blocks = jnp.where(side < PAD, grad_gate[0:PAD], grad_gate[PAD : 2 * PAD])
        rest = grad_small[...] - wide(low(grad_small[...]))
        packed[...] = low(blocks)
        packed[SMALL:PAD] = low(
            jnp.concatenate([jnp.concatenate([grad_small[...], rest], axis=1), blocks[-8:]], axis=0)
        )


def mixer_calls(rows, shards, steps, channels, model):
    blocks = rows * shards

    def position(row, shard, place):
        offset = (row * shards + shard) ^ place
        return (offset // 2) + (offset % 2) * (GROUP // 2)

    def whole(*dims):
        return pl.BlockSpec(dims, lambda row, shard, place: (0,) * len(dims))

    params = pltpu.CompilerParams(
        dimension_semantics=("arbitrary", "arbitrary"), vmem_limit_bytes=48 * 1024 * 1024
    )
    lanes = channels // 128
    forward = pl.pallas_call(
        forward_kernel,
        grid_spec=pltpu.PrefetchScalarGridSpec(
            num_scalar_prefetch=1,
            grid=(rows, shards),
            in_specs=[
                pl.BlockSpec((1, steps, model), lambda r, s, p: (position(r, s, p[0]), 0, 0)),
                pl.BlockSpec((1, steps, 128), lambda r, s, p: (r * shards + s, 0, 0)),
                whole(model, 2 * channels),
                whole(channels, 2 * channels),
                whole(1, 2 * channels),
                whole(8, channels),
            ],
            out_specs=[
                pl.BlockSpec(
                    (1, steps, 2 * channels), lambda r, s, p: (position(r, s, p[0]), 0, 0)
                ),
                pl.BlockSpec((1, steps, channels), lambda r, s, p: (r * shards + s, 0, 0)),
                pl.BlockSpec((1, steps, channels), lambda r, s, p: (position(r, s, p[0]), 0, 0)),
            ],
            scratch_shapes=[
                pltpu.VMEM((steps + 8, channels), F32),
                pltpu.VMEM((lanes, steps, 128), F32),
                pltpu.VMEM((lanes, steps, 128), F32),
                pltpu.VMEM((8, channels), F32),
                pltpu.VMEM((steps + 8, 128), F32),
            ],
        ),
        out_shape=[
            jax.ShapeDtypeStruct((blocks, steps, 2 * channels), F32),
            jax.ShapeDtypeStruct((blocks, steps, channels), F32),
            jax.ShapeDtypeStruct((blocks, steps, channels), BF16),
        ],
        compiler_params=params,
        cost_estimate=pl.CostEstimate(
            flops=blocks * steps * channels * (channels * 4 + model * 4),
            bytes_accessed=blocks * steps * channels * 14,
            transcendentals=blocks * steps * channels * 6,
        ),
        name="mixer_forward",
    )

    def turned(shard):
        return shards - 1 - shard

    def before(shard):
        return jnp.maximum(shards - 2 - shard, 0)

    backward = pl.pallas_call(
        backward_kernel,
        grid_spec=pltpu.PrefetchScalarGridSpec(
            num_scalar_prefetch=1,
            grid=(rows, shards),
            in_specs=[
                pl.BlockSpec(
                    (1, steps, 2 * channels), lambda r, s, p: (position(r, turned(s), p[0]), 0, 0)
                ),
                pl.BlockSpec(
                    (1, 8, channels),
                    lambda r, s, p: (position(r, before(s), p[0]), steps // 8 - 1, 0),
                ),
                pl.BlockSpec((1, steps, 128), lambda r, s, p: (r * shards + turned(s), 0, 0)),
                pl.BlockSpec(
                    (1, 8, 128), lambda r, s, p: (r * shards + before(s), steps // 8 - 1, 0)
                ),
                pl.BlockSpec((1, steps, channels), lambda r, s, p: (r * shards + turned(s), 0, 0)),
                pl.BlockSpec(
                    (1, 8, channels),
                    lambda r, s, p: (r * shards + before(s), steps // 8 - 1, 0),
                ),
                pl.BlockSpec(
                    (1, steps, model), lambda r, s, p: (position(r, turned(s), p[0]), 0, 0)
                ),
                pl.BlockSpec((model, channels), lambda r, s, p: (0, 2)),
                whole(channels, 2 * channels),
                whole(1, 2 * channels),
                whole(8, channels),
            ],
            out_specs=[
                pl.BlockSpec(
                    (1, steps, 2 * channels), lambda r, s, p: (position(r, turned(s), p[0]), 0, 0)
                ),
                whole(PAD, 2 * channels),
            ],
            scratch_shapes=[
                pltpu.VMEM((steps + 8, channels), F32),
                pltpu.VMEM((lanes, steps + 8, 128), F32),
                pltpu.VMEM((lanes, steps, 128), F32),
                pltpu.VMEM((steps, channels), F32),
                pltpu.VMEM((8, channels), F32),
                pltpu.VMEM((KW - 1, steps + 8, channels), F32),
                pltpu.VMEM((steps + 8, 128), F32),
                pltpu.VMEM((channels, 2 * channels), F32),
                pltpu.VMEM((8, channels), F32),
            ],
        ),
        out_shape=[
            jax.ShapeDtypeStruct((blocks, steps, 2 * channels), BF16),
            jax.ShapeDtypeStruct((PAD, 2 * channels), BF16),
        ],
        compiler_params=params,
        cost_estimate=pl.CostEstimate(
            flops=blocks * steps * channels * (channels * 12 + model * 2),
            bytes_accessed=blocks * steps * channels * 24,
            transcendentals=blocks * steps * channels * 8,
        ),
        name="mixer_backward",
    )
    return forward, backward


def local(
    stream_in,
    segment_ids,
    out_grad,
    branch_weight,
    gating_weight,
    output_weight,
    hidden_gate,
    hidden_linear,
    hidden_output,
    mixer_gain,
    hidden_gain,
    gate_blocks,
    gate_biases,
    conv_taps,
    conv_bias,
    decay_param,
):
    rows_here, steps, model_width = stream_in.shape
    shards = lax.axis_size("seq")
    rows = GROUP // shards
    assert rows_here == 1 and rows * shards == GROUP
    groups = device_count() // GROUP
    place = flat_index() % GROUP
    turn = flat_index() // GROUP
    own_rows, hidden_width = hidden_gate.shape
    hidden_part = hidden_width // GROUP
    tokens = GROUP * steps

    where = place.astype(jnp.int32).reshape(1)
    tiny = jnp.concatenate(
        [mixer_gain[None], hidden_gain[None], low(segment_ids)], axis=1
    )
    tiny_width = tiny.shape[1]
    mixer_parts = simple_call(
        split_mixer_kernel,
        "split_mixer",
        where,
        (
            branch_weight,
            gating_weight,
            output_weight,
            jnp.pad(tiny, ((0, 15), (0, 3 * WIDE - tiny_width))),
        ),
        [((own_rows + 16, 3 * WIDE), BF16)] * GROUP,
        [pltpu.VMEM((GROUP, own_rows, 3 * WIDE), F32)],
    )
    mixer_rows, tiny = simple_call(
        collect_mixer_kernel,
        "collect_mixer",
        where,
        all_swapped(mixer_parts),
        [
            ((GROUP, own_rows, 3 * WIDE), BF16),
            ((GROUP, 1, tiny_width), F32),
        ],
    )
    tiny = tiny.reshape(GROUP, tiny_width)
    mixer_weight = ring_gather(mixer_rows.reshape(-1, 3 * WIDE))
    both_weight, out_weight = mixer_weight[:, : 2 * WIDE], mixer_weight[:, 2 * WIDE :]
    gains = ring_stack(tiny[:, : 2 * own_rows], turn, groups)
    mixer_scale = gains[..., :own_rows].reshape(1, model_width)
    hidden_scale = gains[..., own_rows:].reshape(1, model_width)
    segments = jnp.broadcast_to(tiny[:, 2 * own_rows :, None], (GROUP, steps, 128))

    inputs = wide(stream_in).reshape(steps, model_width)
    inputs_scale = rms_scale(inputs)
    parts = group_parts(stream_in.reshape(steps, model_width))
    raw = jnp.concatenate(parts, axis=0)
    normed = norm_rows(raw, mixer_scale, steps)
    upstream = wide(out_grad).reshape(steps, model_width)
    hidden_parts = simple_call(
        split_hidden_kernel,
        "split_hidden",
        where,
        (hidden_gate, hidden_linear, hidden_output),
        [((own_rows, 3 * hidden_part), BF16)] * GROUP,
    )
    pair_rows, last_rows = simple_call(
        collect_kernel,
        "collect_hidden",
        where,
        lax.optimization_barrier(
            (
                all_swapped(lax.optimization_barrier((hidden_parts, parts[3:5]))[0]),
                (raw, mixer_scale),
            )
        )[0],
        [((GROUP, own_rows, 2 * hidden_part), BF16), ((GROUP, own_rows, hidden_part), BF16)],
    )
    pair_weight = ring_gather(pair_rows.reshape(-1, 2 * hidden_part))
    normed_blocks = after(normed, pair_rows).reshape(GROUP, steps, model_width)

    rate = -8.0 * jax.nn.softplus(-decay_param)
    params = jnp.concatenate(
        [gate_biases, conv_taps, conv_bias[None], rate[None]], axis=0
    )
    params = pick(jnp.swapaxes(to_windows(params), 0, 1), place)
    bias = params[:2].reshape(1, 2 * WIDE)
    params = params.at[7].set(jnp.where(params[7] == 0.0, -0.01, params[7]))
    blocks = lax.dynamic_slice_in_dim(gate_blocks, 2 * place, 2, 1)
    blocks = jnp.pad(blocks, ((0, 0), (0, 0), (0, PAD - BLK), (0, PAD - BLK)))
    empty = jnp.zeros((PAD, PAD), BF16)
    gate_weight = jnp.concatenate(
        [
            jnp.concatenate([blocks[0, 0], empty, blocks[1, 0], empty], axis=1),
            jnp.concatenate([empty, blocks[0, 1], empty, blocks[1, 1]], axis=1),
        ],
        axis=0,
    )
    mixer_forward, mixer_backward = mixer_calls(rows, shards, steps, WIDE, model_width)
    own = after(out_grad.reshape(steps, model_width), normed)
    swapped = first_swaps(own)
    pre, state, mixed = mixer_forward(
        where, normed_blocks, segments, mixer_weight, gate_weight, bias, params
    )
    mixed, swapped = lax.optimization_barrier((mixed.reshape(tokens, WIDE), swapped))
    upstream_parts = group_parts(own, swapped)
    last_weight = ring_gather(after(last_rows, mixed).reshape(-1, hidden_part))
    middle = inputs + group_total(pair_product(mixed, out_weight))

    middle_scale = rms_scale(middle)
    own = low(middle * middle_scale * hidden_scale)
    parts = group_parts(own, lax.optimization_barrier((first_swaps(own), pair_weight))[0])
    normed_mid = jnp.concatenate(parts, axis=0)
    upstream_all = jnp.concatenate(upstream_parts, axis=0)
    pair = product(normed_mid, pair_weight)
    gate_pre, linear_pre = pair[:, :hidden_part], pair[:, hidden_part:]
    value, slope = gelu_both(gate_pre)
    hidden, value, slope = lax.optimization_barrier(
        (low(value * linear_pre), value, linear_pre * slope)
    )
    grad_last_low = low(contract_rows(upstream_all, hidden))
    grad_last = ring_reduce(grad_last_low)
    half = tokens // 2
    hidden_far = low(contract_cols(after(hidden[half:], grad_last_low), last_weight))
    d_hidden = product(after(upstream_all, grad_last_low, hidden_far), last_weight)
    d_pair = jnp.concatenate(
        [low(d_hidden * slope), low(d_hidden * value)], axis=1
    )
    hidden_near = contract_cols(after(hidden[:half], d_pair), last_weight)
    hidden_out = pair_total(hidden_near, hidden_far)
    hidden_sent = send_totals(hidden_out)
    grad_pair_low = low(contract_rows(normed_mid, after(d_pair, hidden_out)))
    grad_pair = ring_reduce(grad_pair_low)
    hidden_rest = rest_totals(hidden_out, hidden_sent)
    d_pair, hidden_rest, hidden_sent = lax.optimization_barrier(
        (after(d_pair, grad_pair_low), hidden_rest, hidden_sent)
    )
    d_normed_mid, hidden_out = pair_product(
        d_pair, pair_weight, join_totals(hidden_out, hidden_sent, hidden_rest)
    )
    result = low(middle + hidden_out)
    d_middle = upstream + norm_back(
        middle, middle_scale, hidden_scale, group_total(d_normed_mid)
    )

    def to_owner(grads):
        return exchange(grads.reshape(GROUP, own_rows, -1))

    own = after(low(d_middle), grad_last)
    middle_low = group_gather(own)
    grad_out_low = low(contract_rows(middle_low, mixed))
    grad_out = ring_reduce(grad_out_low)
    middle_blocks = after(middle_low, grad_out_low, grad_pair).reshape(GROUP, steps, model_width)
    hidden_grads = to_owner(jnp.concatenate([grad_pair, grad_last], axis=1))
    d_both, packed = mixer_backward(
        where,
        pre,
        pre,
        segments,
        segments,
        state,
        state,
        middle_blocks,
        mixer_weight,
        gate_weight,
        bias,
        params,
    )
    d_both = d_both.reshape(tokens, 2 * WIDE)
    grad_both_low = low(contract_rows(normed, after(d_both, grad_out, hidden_grads)))
    grad_both = ring_reduce(grad_both_low)
    packed = ring_sum(packed, turn, groups)
    d_normed, packed = pair_product(after(d_both, grad_both_low), both_weight, packed)
    d_normed = group_total(d_normed)
    stream_grad = low(d_middle + norm_back(inputs, inputs_scale, mixer_scale, d_normed))

    grad_hgate, grad_hlinear, grad_houtput, grad_hgain = simple_call(
        hidden_owner_kernel,
        "hidden_owner",
        where,
        (hidden_gate, hidden_linear, wide(hidden_gain)[:, None])
        + (hidden_grads,),
        [((own_rows, hidden_width), F32)] * 3 + [((own_rows, 1), F32)],
    )
    both_grads, out_grads = to_owner(grad_both), to_owner(grad_out)

    packed = ring_stack(packed, turn, groups).reshape(PAD, 2 * WIDE)
    packed, out_grads = lax.optimization_barrier((packed, out_grads))
    across, along = lax.optimization_barrier((swap(packed, 4), swap(packed, 2)))
    beyond = [swap(across[: PAD // 2], 2), swap(along[PAD // 2 :], 4)]
    near = [packed, along, across, jnp.concatenate(beyond, axis=0)]
    near, both_grads = lax.optimization_barrier((near, both_grads))
    grad_gblocks, small = simple_call(
        gates_owner_kernel,
        "gates_owner",
        where,
        near + [swap(part, 1) for part in near],
        [((2, NBLK, BLK, BLK), F32), ((8, R), F32)],
        [pltpu.VMEM((GROUP, 8, WIDE), F32)],
    )
    grad_decay = 8.0 * jax.nn.sigmoid(-decay_param) * small[7]

    grad_branch, grad_gating, grad_output, grad_mgain = simple_call(
        mixer_owner_kernel,
        "mixer_owner",
        where,
        (branch_weight, gating_weight, wide(mixer_gain)[:, None])
        + (both_grads, out_grads),
        [((own_rows, R), F32)] * 3 + [((own_rows, 1), F32)],
    )

    shape = (rows_here, steps, model_width)
    return (
        result.reshape(shape),
        stream_grad.reshape(shape),
        grad_branch,
        grad_gating,
        grad_output,
        grad_hgate,
        grad_hlinear,
        grad_houtput,
        grad_mgain.reshape(own_rows),
        grad_hgain.reshape(own_rows),
        grad_gblocks,
        small[:2],
        small[2:6],
        small[6],
        grad_decay,
    )


def solution(mesh):
    return jax.shard_map(
        local,
        mesh=mesh,
        in_specs=(
            P("batch", "seq", None),
            P("batch", "seq"),
            P("batch", "seq", None),
            P(("batch", "seq"), None),
            P(("batch", "seq"), None),
            P(("batch", "seq"), None),
            P(("batch", "seq"), None),
            P(("batch", "seq"), None),
            P(("batch", "seq"), None),
            P(("batch", "seq")),
            P(("batch", "seq")),
            P(),
            P(),
            P(),
            P(),
            P(),
        ),
        out_specs=(
            P("batch", "seq", None),
            P("batch", "seq", None),
            P(("batch", "seq"), None),
            P(("batch", "seq"), None),
            P(("batch", "seq"), None),
            P(("batch", "seq"), None),
            P(("batch", "seq"), None),
            P(("batch", "seq"), None),
            P(("batch", "seq")),
            P(("batch", "seq")),
            P(),
            P(),
            P(),
            P(),
            P(),
        ),
        check_vma=False,
    )
```
